128 devices in a mesh: shard: 128 (over z, x, y, core).
Axes of the slice: x: 4, y: 4, z: 4, core: 2. Of those that a mesh axis runs over, the one named last changes fastest.
Arguments:
- entity_table: float32 [262144, 400], P('shard'), may hold values from -2.5 to 2.5
- entity_accum: float32 [262144], P('shard'), may hold values from 0.001 to 0.1
- hub_table: float32 [1024, 400], replicated, may hold values from -2.5 to 2.5
- hub_accum: float32 [1024], replicated, may hold values from 0.001 to 0.1
- relation_table: float32 [512, 400], replicated, may hold values from -2.5 to 2.5
- relation_accum: float32 [512], replicated, may hold values from 0.001 to 0.1
- head_ids: int32 [65536], P('shard'), may hold values from 0 to 3071
- relation_ids: int32 [65536], P('shard'), may hold values from 0 to 511
- tail_owner: int32 [65536, 1], P('shard'), may hold values from 0 to 127; in each aligned block of 512 rows (0 to 511, 512 to 1023, ...) at most 8 rows name the same one
- tail_rows: int32 [65536], P('shard'), may hold values from 0 to 2047
- negative_rows: int32 [2048], P('shard'), may hold values from 0 to 2047
Outputs:
- entity_new: float32 [262144, 400], P('shard')
- entity_accum_new: float32 [262144], P('shard')
- hub_new: float32 [1024, 400], replicated
- hub_accum_new: float32 [1024], replicated
- relation_new: float32 [512, 400], replicated
- relation_accum_new: float32 [512], replicated
- triple_loss: float32 [65536], P('shard')
The draws below stay inside these ranges and needn't reach their ends.
Inputs may be any that keep to these rules, and one draw needn't show every extreme that they name: Below 1024 a head is hub head_ids; otherwise it is row head_ids - 1024 of the entities held by the triple's own device. `tail_owner`: among the 512 triples of one device, at most 8 have their tail on one owner, and in every draw some owner is named exactly 8 times. `negative_rows`: entry j is a row of the entities held by device j // 16; rows may repeat.
All inputs are finite; a program needn't handle non-finite values.
Results may differ from the reference program's by a relative error of at most 0.0001.
Values sent between devices are 32-bit elements; how exact they have to be, the bound alone decides.
No kernel may reach another device: no remote copies, remote signals or barrier semaphores. Data moves between devices by JAX's collectives and lax.ppermute only.
A program may use at most 128 MiB of HBM per device.

```python
import math
import jax
import jax.numpy as jnp
import numpy as np
from jax import lax

WIDTH = 400
ENT_DEV = 2048
TRIP_DEV = 512
NEG_SHARD = 16
HUBS = 1024
REL = 512
ENTITIES = 262144
TRIPLES = 65536
NEGS = 2048
OWNERS = 128
CAP = 8
N_SHARD = 128


def plant(entries, stream_key, least, high):
    extent = entries.shape
    place = [jax.random.randint(jax.random.fold_in(stream_key, axis), (), 0, extent[axis]) for axis in range(len(extent))]
    entries = entries.at[tuple(place)].set(least)
    longest = extent.index(max(extent))
    place[longest] = (place[longest] + 1) % extent[longest]
    return entries.at[tuple(place)].set(high)


def levels(own_key, dims, cuts, low, largest):
    loudness, own = 1.0, jax.random.fold_in(own_key, 6)
    for axis_at, blocks in cuts:
        heights = jnp.exp(jax.random.uniform(jax.random.fold_in(own, axis_at), (blocks,), jnp.float32, low / len(cuts), largest / len(cuts)))
        loudness = loudness * jnp.repeat(heights, dims[axis_at] // blocks).reshape([-1 if axis == axis_at else 1 for axis in range(len(dims))])
    return loudness


def rank_bounds(count, lean):
    weights = [(1 << 20) // math.isqrt(grade ** lean) + 1 for grade in range(1, count + 1)]
    scale = 1 + sum(weights) // (1 << 30)
    return np.cumsum(np.array([max(1, weight // scale) for weight in weights]))


def ranked(rng, extent, amount, skew):
    table = rank_bounds(amount, skew)
    ticket = jax.random.randint(jax.random.fold_in(rng, 1), extent, 0, int(table[amount - 1]))
    grade = jnp.searchsorted(jnp.asarray(table, jnp.int32), ticket, side="right")
    return jax.random.permutation(jax.random.fold_in(rng, 2), amount)[grade].astype(jnp.int32)


def deal_out(stream_key, own, number, rows, number_of, top, most, slope):
    ranking = jax.random.permutation(stream_key, number_of)
    crowded, ordinary = load_shares(number_of, rows * top, most, slope, True), load_shares(number_of, rows * top, most, slope, False)
    places = jnp.arange(number_of)

    def named(tallies, rotation):
        used = int((tallies > 0).sum())
        fixed = max(1, used // 4)
        moved = fixed + (places - fixed + rotation * (used - fixed)) % max(1, number_of - fixed)
        return jnp.zeros((number_of,), jnp.int32).at[ranking[jnp.where(places < fixed, places, moved)]].set(jnp.asarray(tallies, jnp.int32))

    tallies = jnp.where(number % 4 == 0, named(crowded, number // 4), named(ordinary, number - number // 4 - 1))
    mixed = jax.random.permutation(jax.random.fold_in(own, 3), number_of)
    giver, receiver = mixed[0:number_of // 2 * 2:2], mixed[1:number_of // 2 * 2:2]
    margin = jnp.minimum(tallies[giver] - 1, most - tallies[receiver]) // 2
    margin = jnp.where((giver == ranking[0]) | (receiver == ranking[0]) | (tallies[receiver] == 0), 0, jnp.maximum(margin, 0))
    moved = jax.random.randint(jax.random.fold_in(own, 4), (number_of // 2,), 0, 1 << 20) % (margin + 1)
    tallies = tallies.at[giver].add(-moved).at[receiver].add(moved)
    items = jnp.searchsorted(jnp.cumsum(tallies), jnp.arange(rows * top), side="right").astype(jnp.int32)
    grid = items.reshape(top, rows).T
    grid = grid[jax.random.permutation(jax.random.fold_in(own, 1), rows)]
    rotation = jax.random.randint(jax.random.fold_in(own, 2), (rows, 1), 0, top)
    return jnp.take_along_axis(grid, (jnp.arange(top)[None, :] + rotation) % top, axis=1)


def load_shares(amount, total, reach, slope, full):
    weights = [(1 << 20) // math.isqrt(rank ** slope) + 1 for rank in range(1, amount + 1)]
    largest = reach if full else min(reach, max(-(-total // amount), total * weights[0] // sum(weights)))
    least = 1 if total - largest >= amount - 1 else 0
    counts, rest = [largest] + [least] * (amount - 1), total - largest - least * (amount - 1)
    while rest > 0:
        candidates = [i for i in range(1, amount) if counts[i] < largest] or [i for i in range(1, amount) if counts[i] < reach]
        pool, left = sum([weights[i] for i in candidates]), rest
        for i in candidates:
            more = min(reach - counts[i], max(1, left * weights[i] // pool), rest)
            counts[i] = counts[i] + more
            rest = rest - more
    return np.array(counts)


def scatter_about(rng, extent, deviation, most, split=(), kind=jnp.bfloat16):
    array = jax.random.normal(rng, extent, jnp.float32) * deviation
    if len(split) > 0:
        array = levels(rng, extent, split, -0.22, 0.18) * array
    return jnp.clip(array, min=-most, max=most).astype(kind)


def setup_inputs(seed: int = 0) -> dict:
    splits = jax.random.split(jax.random.key(seed), 12)
    entity_table = scatter_about(splits[0], (ENTITIES, WIDTH), 0.33, 2.5, ((0, 128),), jnp.float32)
    entity_accum = jnp.clip(jnp.exp(math.log(0.1) - 4.6051702 * jax.random.uniform(splits[1], (ENTITIES,), jnp.float32) ** levels(splits[1], (ENTITIES,), ((0, 128),), -0.2, 0.2)), 0.001, 0.1)
    hub_table = scatter_about(splits[2], (HUBS, WIDTH), 0.33, 2.5, (), jnp.float32)
    hub_accum = jnp.clip(jnp.exp(jax.random.uniform(splits[3], (HUBS,), jnp.float32, math.log(0.001), math.log(0.1))), 0.001, 0.1)
    relation_table = scatter_about(splits[4], (REL, WIDTH), 0.33, 2.5, (), jnp.float32)
    relation_accum = jnp.clip(jnp.exp(jax.random.uniform(splits[5], (REL,), jnp.float32, math.log(0.001), math.log(0.1))), 0.001, 0.1)
    head_ids = plant(jax.random.randint(splits[6], (TRIPLES,), 0, HUBS + ENT_DEV), jax.random.fold_in(splits[6], 1), 0, (HUBS + ENT_DEV) - 1).astype(jnp.int32)
    relation_ids = plant(ranked(splits[7], (TRIPLES,), REL, 2), jax.random.fold_in(splits[7], 3), 0, REL - 1).astype(jnp.int32)
    tail_owner_keys = jax.random.split(jax.random.fold_in(splits[8], 1), TRIPLES // TRIP_DEV)
    tail_owner_turns = jax.random.permutation(jax.random.fold_in(splits[8], 3), TRIPLES // TRIP_DEV)
    tail_owner = jax.vmap(lambda own, number: deal_out(jax.random.fold_in(splits[8], 2), own, number, TRIP_DEV, OWNERS, 1, CAP, 2))(tail_owner_keys, tail_owner_turns).reshape((TRIPLES, 1))
    tail_rows = plant(jax.random.randint(splits[9], (TRIPLES,), 0, ENT_DEV), jax.random.fold_in(splits[9], 1), 0, ENT_DEV - 1).astype(jnp.int32)
    negative_rows = plant(jax.random.randint(splits[10], (NEGS,), 0, ENT_DEV), jax.random.fold_in(splits[10], 1), 0, ENT_DEV - 1).astype(jnp.int32)
    return dict(entity_table=entity_table, entity_accum=entity_accum, hub_table=hub_table, hub_accum=hub_accum, relation_table=relation_table, relation_accum=relation_accum, head_ids=head_ids, relation_ids=relation_ids, tail_owner=tail_owner, tail_rows=tail_rows, negative_rows=negative_rows)


LEARN_RATE = 0.1

def compose(head_rows, rel_rows):
    half_width = head_rows.shape[-1] // 2
    head_re, head_im = (head_rows[..., :half_width], head_rows[..., half_width:])
    rel_re, rel_im = (rel_rows[..., :half_width], rel_rows[..., half_width:])
    return jnp.concatenate([head_re * rel_re - head_im * rel_im, head_re * rel_im + head_im * rel_re], axis=-1)

def spread(grad_query, head_rows, rel_rows):
    half_width = head_rows.shape[-1] // 2
    head_re, head_im = (head_rows[..., :half_width], head_rows[..., half_width:])
    rel_re, rel_im = (rel_rows[..., :half_width], rel_rows[..., half_width:])
    grad_re, grad_im = (grad_query[..., :half_width], grad_query[..., half_width:])
    grad_head = jnp.concatenate([grad_re * rel_re + grad_im * rel_im, grad_im * rel_re - grad_re * rel_im], axis=-1)
    grad_rel = jnp.concatenate([grad_re * head_re + grad_im * head_im, grad_im * head_re - grad_re * head_im], axis=-1)
    return (grad_head, grad_rel)

def adagrad(table_rows, accum_rows, grad_rows):
    new_accum = accum_rows + lax.optimization_barrier(jnp.mean(grad_rows * grad_rows, axis=-1))
    return (table_rows - LEARN_RATE * grad_rows / jnp.sqrt(new_accum)[:, None], new_accum)

def reference(entity_table, entity_accum, hub_table, hub_accum, relation_table, relation_accum, head_ids, relation_ids, tail_owner, tail_rows, negative_rows):
    highest = lax.Precision.HIGHEST
    device_of = jnp.arange(TRIPLES, dtype=jnp.int32) // TRIP_DEV
    is_hub = head_ids < HUBS
    hub_head = jnp.clip(head_ids, 0, HUBS - 1).astype(jnp.int32)
    ent_head = (device_of * ENT_DEV + jnp.clip(head_ids - HUBS, 0, ENT_DEV - 1)).astype(jnp.int32)
    head_vecs = jnp.where(is_hub[:, None], hub_table[hub_head], entity_table[ent_head])
    rel_vecs = relation_table[relation_ids]
    queries = compose(head_vecs, rel_vecs)
    tail_global = (tail_owner[:, 0] * ENT_DEV + tail_rows).astype(jnp.int32)
    tail_vecs = entity_table[tail_global]
    neg_global = (jnp.arange(NEGS, dtype=jnp.int32) // NEG_SHARD * ENT_DEV + negative_rows).astype(jnp.int32)
    neg_vecs = entity_table[neg_global]
    positive = lax.optimization_barrier(jnp.sum(queries * tail_vecs, axis=-1))
    grad_pos = -jax.nn.sigmoid(-positive)

    def block_step(running, query_block):
        scores = jnp.dot(query_block, neg_vecs.T, precision=highest, preferred_element_type=jnp.float32)
        neg_loss = lax.optimization_barrier(jnp.mean(jax.nn.softplus(scores), axis=1))
        grad_neg = jax.nn.sigmoid(scores) / NEGS
        query_term = jnp.dot(grad_neg, neg_vecs, precision=highest, preferred_element_type=jnp.float32)
        running = running + jnp.dot(grad_neg.T, query_block, precision=highest, preferred_element_type=jnp.float32)
        return (running, (neg_loss, query_term))
    grad_negvec, (neg_loss, query_term) = lax.scan(block_step, jnp.zeros((NEGS, WIDTH), jnp.float32), queries.reshape(N_SHARD, TRIP_DEV, WIDTH))
    triple_loss = jax.nn.softplus(-positive) + neg_loss.reshape(TRIPLES)
    grad_query = grad_pos[:, None] * tail_vecs + query_term.reshape(TRIPLES, WIDTH)
    grad_head, grad_rel = spread(grad_query, head_vecs, rel_vecs)
    entity_grad = jnp.zeros((ENTITIES, WIDTH), jnp.float32)
    entity_grad = entity_grad.at[ent_head].add(jnp.where(is_hub[:, None], 0.0, grad_head))
    entity_grad = entity_grad.at[tail_global].add(grad_pos[:, None] * queries)
    entity_grad = entity_grad.at[neg_global].add(grad_negvec)
    hub_grad = jnp.zeros((HUBS, WIDTH), jnp.float32).at[hub_head].add(jnp.where(is_hub[:, None], grad_head, 0.0))
    relation_grad = jnp.zeros((REL, WIDTH), jnp.float32).at[relation_ids].add(grad_rel)
    entity_new, entity_accum_new = adagrad(entity_table, entity_accum, entity_grad)
    hub_new, hub_accum_new = adagrad(hub_table, hub_accum, hub_grad)
    relation_new, relation_accum_new = adagrad(relation_table, relation_accum, relation_grad)
    return (entity_new, entity_accum_new, hub_new, hub_accum_new, relation_new, relation_accum_new, triple_loss)
```

```python
import jax
import jax.numpy as jnp
from jax import lax
from jax.sharding import Mesh, PartitionSpec as P

LEARN_RATE = 0.1
CHIPS = ("z", "x", "y")
SHARD = ("z", "x", "y", "core")
SWAP = [(0, 1), (1, 0)]


def compose(head_rows, rel_rows):
    half = head_rows.shape[-1] // 2
    head_re, head_im = (head_rows[..., :half], head_rows[..., half:])
    rel_re, rel_im = (rel_rows[..., :half], rel_rows[..., half:])
    return jnp.concatenate(
        [head_re * rel_re - head_im * rel_im, head_re * rel_im + head_im * rel_re], axis=-1
    )


def spread(grad_query, head_rows, rel_rows):
    half = head_rows.shape[-1] // 2
    head_re, head_im = (head_rows[..., :half], head_rows[..., half:])
    rel_re, rel_im = (rel_rows[..., :half], rel_rows[..., half:])
    grad_re, grad_im = (grad_query[..., :half], grad_query[..., half:])
    grad_head = jnp.concatenate(
        [grad_re * rel_re + grad_im * rel_im, grad_im * rel_re - grad_re * rel_im], axis=-1
    )
    grad_rel = jnp.concatenate(
        [grad_re * head_re + grad_im * head_im, grad_im * head_re - grad_re * head_im], axis=-1
    )
    return (grad_head, grad_rel)


def adagrad(table_rows, accum_rows, grad_rows):
    new_accum = accum_rows + jnp.mean(grad_rows * grad_rows, axis=-1)
    return (table_rows - LEARN_RATE * grad_rows / jnp.sqrt(new_accum)[:, None], new_accum)


def reduce_over_devices(halves, core):
    mine = lax.dynamic_index_in_dim(halves, core, 0, keepdims=False)
    other = lax.dynamic_index_in_dim(halves, 1 - core, 0, keepdims=False)
    mine = mine + lax.ppermute(other, "core", SWAP)
    chips = lax.axis_size(CHIPS)
    parts = lax.all_to_all(mine, CHIPS, split_axis=0, concat_axis=0, tiled=True)
    return jnp.sum(parts.reshape(chips, -1, parts.shape[-1]), axis=0)


def gather_from_devices(rows, core):
    chips = lax.axis_size(CHIPS)
    copies = jnp.broadcast_to(rows[None], (chips, *rows.shape)).reshape(-1, rows.shape[-1])
    mine = lax.all_to_all(copies, CHIPS, split_axis=0, concat_axis=0, tiled=True)
    other = lax.ppermute(mine, "core", SWAP)
    return jnp.where(core == 0, jnp.stack([mine, other]), jnp.stack([other, mine]))


def body(
    entity_table,
    entity_accum,
    hub_table,
    hub_accum,
    relation_table,
    relation_accum,
    head_ids,
    relation_ids,
    tail_owner,
    tail_rows,
    negative_rows,
):
    highest = lax.Precision.HIGHEST
    core = lax.axis_index("core")
    chip = lax.axis_index(CHIPS)
    chips = lax.axis_size(CHIPS)
    shards = lax.axis_size(SHARD)
    ent_dev, width = entity_table.shape
    hub_count = hub_table.shape[0]
    rel_count = relation_table.shape[0]
    trip_dev = head_ids.shape[0]
    capacity = 2 * trip_dev // shards
    slots = shards * capacity

    neg_vecs = lax.all_gather(entity_table[negative_rows], SHARD, axis=0, tiled=True)
    neg_total = neg_vecs.shape[0]
    neg_vecs = (
        neg_vecs.reshape(chips, 2, -1, width).transpose(1, 0, 2, 3).reshape(neg_total, width)
    )

    is_hub = head_ids < hub_count
    hub_head = jnp.clip(head_ids, 0, hub_count - 1)
    ent_head = jnp.clip(head_ids - hub_count, 0, ent_dev - 1)
    head_vecs = jnp.where(is_hub[:, None], hub_table[hub_head], entity_table[ent_head])
    rel_vecs = relation_table[relation_ids]
    queries = compose(head_vecs, rel_vecs)

    owner_ids = tail_owner[:, 0]
    order = jnp.arange(trip_dev, dtype=jnp.int32)
    earlier = (owner_ids[:, None] == owner_ids[None, :]) & (order[None, :] < order[:, None])
    place = owner_ids * capacity + jnp.sum(earlier.astype(jnp.int32), axis=1)
    hit = place[None, :] == jnp.arange(slots, dtype=jnp.int32)[:, None]
    source = jnp.sum(jnp.where(hit, order[None, :], 0), axis=1)
    row_sent = jnp.sum(jnp.where(hit, tail_rows[None, :] + 1, 0), axis=1) - 1

    sent = jnp.concatenate([queries[source], row_sent.astype(jnp.float32)[:, None]], axis=1)
    asked = lax.all_to_all(sent, SHARD, split_axis=0, concat_axis=0, tiled=True)
    asked_rows = asked[:, width].astype(jnp.int32)
    asked_queries = asked[:, :width]
    asked_tails = entity_table[jnp.maximum(asked_rows, 0)]
    asked_pos = jnp.sum(asked_queries * asked_tails, axis=-1)
    asked_gp = -jax.nn.sigmoid(-asked_pos)
    answer = jnp.concatenate([asked_gp[:, None] * asked_tails, asked_pos[:, None]], axis=1)
    returned = lax.all_to_all(answer, SHARD, split_axis=0, concat_axis=0, tiled=True)[place]
    tail_term = returned[:, :width]
    positive = returned[:, width]
    owned_grads = jnp.where((asked_rows >= 0)[:, None], asked_gp[:, None] * asked_queries, 0.0)

    scores = jnp.dot(queries, neg_vecs.T, precision=highest, preferred_element_type=jnp.float32)
    neg_loss = jnp.mean(jax.nn.softplus(scores), axis=1)
    grad_neg = jax.nn.sigmoid(scores) / neg_total
    triple_loss = jax.nn.softplus(-positive) + neg_loss
    grad_query = tail_term + jnp.dot(
        grad_neg, neg_vecs, precision=highest, preferred_element_type=jnp.float32
    )
    grad_head, grad_rel = spread(grad_query, head_vecs, rel_vecs)
    hub_grad = (
        jnp.zeros((hub_count, width), jnp.float32)
        .at[hub_head]
        .add(jnp.where(is_hub[:, None], grad_head, 0.0))
    )
    relation_grad = jnp.zeros(relation_table.shape, jnp.float32).at[relation_ids].add(grad_rel)

    hub_own, rel_own = hub_count // shards, rel_count // shards
    both = jnp.concatenate(
        [
            hub_grad.reshape(2, chips, hub_own, width),
            relation_grad.reshape(2, chips, rel_own, width),
        ],
        axis=2,
    ).reshape(2, -1, width)
    both_sum = reduce_over_devices(both, core)
    own = core * chips + chip
    own_table = jnp.concatenate(
        [
            lax.dynamic_slice_in_dim(hub_table, own * hub_own, hub_own, 0),
            lax.dynamic_slice_in_dim(relation_table, own * rel_own, rel_own, 0),
        ]
    )
    own_accum = jnp.concatenate(
        [
            lax.dynamic_slice_in_dim(hub_accum, own * hub_own, hub_own, 0),
            lax.dynamic_slice_in_dim(relation_accum, own * rel_own, rel_own, 0),
        ]
    )
    own_new, own_accum_new = adagrad(own_table, own_accum, both_sum)
    spread_rows = gather_from_devices(
        jnp.concatenate([own_new, own_accum_new[:, None]], axis=1), core
    ).reshape(shards, hub_own + rel_own, width + 1)
    hub_rows = spread_rows[:, :hub_own].reshape(hub_count, width + 1)
    rel_rows = spread_rows[:, hub_own:].reshape(rel_count, width + 1)

    negvec_part = jnp.dot(
        grad_neg.T, queries, precision=highest, preferred_element_type=jnp.float32
    )
    grad_negvec = reduce_over_devices(negvec_part.reshape(2, -1, width), core)

    entity_grad = jnp.zeros((ent_dev, width), jnp.float32)
    entity_grad = entity_grad.at[ent_head].add(jnp.where(is_hub[:, None], 0.0, grad_head))
    entity_grad = entity_grad.at[jnp.maximum(asked_rows, 0)].add(owned_grads)
    entity_grad = entity_grad.at[negative_rows].add(grad_negvec)
    entity_new, entity_accum_new = adagrad(entity_table, entity_accum, entity_grad)
    return (
        entity_new,
        entity_accum_new,
        hub_rows[:, :width],
        hub_rows[:, width],
        rel_rows[:, :width],
        rel_rows[:, width],
        triple_loss,
    )


def solution(mesh):
    sizes = (4, 4, 4, 2)
    fine = Mesh(mesh.devices.reshape(sizes), SHARD)
    rows, vector = P(SHARD, None), P(SHARD)
    placed = (rows, vector, P(), P(), P(), P(), vector, vector, rows, vector, vector)
    return jax.shard_map(
        body,
        mesh=fine,
        in_specs=placed,
        out_specs=(rows, vector, P(), P(), P(), P(), vector),
        check_vma=False,
    )
```

```python
import jax
import jax.numpy as jnp
from jax import lax
from jax.experimental import pallas as pl
from jax.experimental.pallas import tpu as pltpu
from jax.sharding import Mesh, PartitionSpec as P

LEARN_RATE = 0.1
CHIPS = ("z", "x", "y")
SHARD = ("z", "x", "y", "core")
SIZES = (4, 4, 4, 2)
SWAP = [(0, 1), (1, 0)]
F32, BF16, I32 = jnp.float32, jnp.bfloat16, jnp.int32

WIDTH, HALF, SIDE, WIDE, AUX = 400, 200, 256, 512, 200
ENT, HUB, REL, TRIP, CHIP_COUNT, CAP, NEG = 2048, 1024, 512, 512, 64, 8, 16
SLOTS = 2 * CHIP_COUNT * CAP
HUB_OWN, REL_OWN, OWN = 8, 4, 16
VMEM = pl.BlockSpec(memory_space=pltpu.VMEM)
SMEM = pl.BlockSpec(memory_space=pltpu.SMEM)
LIMIT = 56 << 20


def params(**more):
    return pltpu.CompilerParams(vmem_limit_bytes=LIMIT, **more)


def cost(flops, nbytes):
    return pl.CostEstimate(flops=int(flops), bytes_accessed=int(nbytes), transcendentals=0)


def split(x):
    high = x.astype(BF16)
    return high, (x - high.astype(F32)).astype(BF16)


def dot(a, b, contract=((1,), (0,))):
    return lax.dot_general(a, b, (contract, ((), ())), preferred_element_type=F32)


def hot(condition):
    return jnp.where(condition, 1.0, 0.0).astype(BF16)


def iota(shape, axis):
    return lax.broadcasted_iota(I32, shape, axis)


def aux_column(rows):
    part = rows[:, 128:SIDE]
    return jnp.sum(jnp.where(iota(part.shape, 1) == AUX - 128, part, 0.0), axis=1, keepdims=True)


def without_aux(rows):
    return jnp.where(iota(rows.shape, 1) == AUX, 0.0, rows)


def widen(re, im, aux=None):
    n = re.shape[1]
    gap = jnp.zeros((SIDE - HALF, n), F32)
    if aux is not None:
        first = jnp.where(iota((8, n), 0) == 0, aux, 0.0)
        middle = jnp.concatenate([first, jnp.zeros((SIDE - HALF - 8, n), F32)], axis=0)
    else:
        middle = gap
    return jnp.concatenate([re, middle, im, gap], axis=0)


def pick_negatives(rows_ref, ent_ref, out_ref, held_ref):
    held_ref[...] = jnp.zeros_like(held_ref)
    lane = iota((WIDTH, 128), 1)
    for j in range(NEG):
        row = rows_ref[j]
        block = ent_ref[:, pl.ds(pl.multiple_of((row // 128) * 128, 128), 128)]
        block = pltpu.roll(block, (j - row % 128 + 128) % 128, 1)
        here = lane == j
        held_ref[0:HALF, :] = jnp.where(here[:HALF], block[:HALF], held_ref[0:HALF, :])
        held_ref[SIDE : SIDE + HALF, :] = jnp.where(
            here[:HALF], block[HALF:], held_ref[SIDE : SIDE + HALF, :]
        )
    out_ref[...] = held_ref[...].T[:NEG]


def prepare(head_ref, rel_ref, owner_ref, tail_ref, ent_ref, hub_ref, relt_ref,
            query_ref, headv_ref, relv_ref, sent_ref, place_ref):
    head = head_ref[...]

    def gather(table, ids):
        marks = hot(iota((table.shape[1], TRIP), 0) == ids)
        high, low = split(table)
        return dot(high, marks) + dot(low, marks)

    heads = gather(hub_ref[...], head) + gather(ent_ref[...], head - HUB)
    rels = gather(relt_ref[...], rel_ref[...])
    h_re, h_im, r_re, r_im = heads[:HALF], heads[HALF:], rels[:HALF], rels[HALF:]
    q_re = h_re * r_re - h_im * r_im
    q_im = h_re * r_im + h_im * r_re
    headv_ref[...] = widen(h_re, h_im).T
    relv_ref[...] = widen(r_re, r_im).T
    query_ref[...] = widen(q_re, q_im).T

    owner = owner_ref[...]
    owned = hot(iota((2 * CHIP_COUNT, TRIP), 0) == owner)
    before = hot(iota((TRIP, TRIP), 0) < iota((TRIP, TRIP), 1))
    rank = jnp.sum(dot(owned, before) * owned.astype(F32), axis=0, keepdims=True)
    place = owner * CAP + rank.astype(I32)
    place_ref[...] = jnp.broadcast_to(place.astype(F32), (128, TRIP)).T.astype(I32)

    marks = hot(iota((SLOTS, TRIP), 0) == place)
    high, low = split(widen(q_re, q_im, tail_ref[...].astype(F32) + 1.0).T)
    sent_ref[...] = dot(marks, high) + dot(marks, low)


def turn_tables(own_ref, ent_ref, hub_ref, relt_ref, hubacc_ref, relacc_ref,
                high_ref, low_ref, mine_ref, held_ref):
    for block in range(ENT // 512):
        part = ent_ref[:, block * 512 : (block + 1) * 512]
        high, low = split(widen(part[:HALF], part[HALF:]).T)
        high_ref[block * 512 : (block + 1) * 512, :] = high
        low_ref[block * 512 : (block + 1) * 512, :] = low
    own = own_ref[0]
    lane = iota((1, 128), 1)

    def rows_of(ref, first, at):
        block = ref[:, pl.ds(pl.multiple_of((first // 128) * 128, 128), 128)]
        return pltpu.roll(block, (at - first % 128 + 128) % 128, 1)

    hub = rows_of(hub_ref, own * HUB_OWN, 0)
    rel = rows_of(relt_ref, own * REL_OWN, HUB_OWN)
    hub_acc = rows_of(hubacc_ref, own * HUB_OWN, 0)
    rel_acc = rows_of(relacc_ref, own * REL_OWN, HUB_OWN)
    is_hub, is_rel = lane < HUB_OWN, (lane >= HUB_OWN) & (lane < HUB_OWN + REL_OWN)
    both = jnp.where(is_hub, hub, jnp.where(is_rel, rel, 0.0))
    acc = jnp.where(is_hub, hub_acc, jnp.where(is_rel, rel_acc, 1.0))
    held_ref[...] = widen(both[:HALF], both[HALF:], acc)
    mine_ref[...] = held_ref[...].T[:OWN]


def answer_queries(asked_ref, high_ref, low_ref, out_ref):
    asked = asked_ref[...]
    row = aux_column(asked).astype(I32) - 1
    marks = hot(iota((asked.shape[0], ENT), 1) == row)
    tails = dot(marks, high_ref[...]) + dot(marks, low_ref[...])
    positive = jnp.sum(asked * tails, axis=1, keepdims=True)
    slope = -jax.nn.sigmoid(-positive)
    out_ref[...] = jnp.where(iota(tails.shape, 1) == AUX, positive, slope * tails)


def score(core_ref, query_ref, neg_ref, mine_ref, other_ref, grad_ref, loss_ref,
          qh_ref, ql_ref, sum_ref):
    side, step = pl.program_id(0), pl.program_id(1)

    @pl.when((side == 0) & (step == 0))
    def _():
        high, low = split(query_ref[...])
        qh_ref[...] = high
        ql_ref[...] = low
        grad_ref[...] = jnp.zeros_like(grad_ref)
        sum_ref[...] = jnp.zeros_like(sum_ref)

    neg = neg_ref[...].reshape(-1, WIDE)
    nh, nl = split(neg)
    qh, ql = qh_ref[...], ql_ref[...]
    nt = ((1,), (1,))
    s = dot(qh, nh, nt) + (dot(qh, nl, nt) + dot(ql, nh, nt))
    small = jnp.exp(-jnp.abs(s))
    loss = jnp.maximum(s, 0.0) + jnp.log1p(small)
    total = sum_ref[...]
    for part in range(loss.shape[1] // 128):
        total = total + loss[:, part * 128 : (part + 1) * 128]
    sum_ref[...] = total
    weight = jnp.where(s >= 0.0, 1.0, small) / (1.0 + small) * (1.0 / (ENT_NEGS))
    gh, gl = split(weight)
    grad_ref[...] += dot(gh, nh) + (dot(gh, nl) + dot(gl, nh))
    tn = ((0,), (0,))
    back = (dot(gh, qh, tn) + (dot(gh, ql, tn) + dot(gl, qh, tn))).reshape(mine_ref.shape)

    @pl.when(side == 0)
    def _():
        mine_ref[...] = back

    @pl.when(side == 1)
    def _():
        other_ref[...] = back

    loss_ref[...] = total


ENT_NEGS = 2 * CHIP_COUNT * NEG


def close_triples(core_ref, back_ref, place_ref, headv_ref, relv_ref, gradq_ref, loss_ref,
                  head_ref, rel_ref, gradh_ref, mine_ref, other_ref, out_ref):
    place = place_ref[...]
    lane = iota((TRIP, 128), 1)
    marks = jnp.concatenate(
        [hot(place == lane + part * 128) for part in range(SLOTS // 128)], axis=1
    )
    high, low = split(back_ref[...])
    tail = dot(marks, high) + dot(marks, low)
    positive = aux_column(tail)
    neg_loss = jnp.sum(loss_ref[...], axis=1, keepdims=True) * (1.0 / ENT_NEGS)
    drop = -positive
    loss = jnp.maximum(drop, 0.0) + jnp.log1p(jnp.exp(-jnp.abs(drop))) + neg_loss
    out_ref[...] = jnp.broadcast_to(loss, (TRIP, 128)).T[:1]
    grad = without_aux(tail) + gradq_ref[...]
    g_re, g_im = grad[:, :SIDE], grad[:, SIDE:]
    heads, rels = headv_ref[...], relv_ref[...]
    h_re, h_im, r_re, r_im = heads[:, :SIDE], heads[:, SIDE:], rels[:, :SIDE], rels[:, SIDE:]
    gh = jnp.concatenate([g_re * r_re + g_im * r_im, g_im * r_re - g_re * r_im], axis=1)
    gr = jnp.concatenate([g_re * h_re + g_im * h_im, g_im * h_re - g_re * h_im], axis=1)
    gradh_ref[...] = gh

    core = core_ref[0]
    at = iota((2 * CHIP_COUNT * 8, TRIP), 0)
    head, rel = head_ref[...], rel_ref[...]
    hub_id = (at + core * (HUB // 2)) % HUB
    rel_id = (at // 8 * REL_OWN + at % 8 + core * (REL // 2)) % REL
    hub_marks = hot(hub_id == head)
    rel_marks = hot((rel_id == rel) & (at % 8 < REL_OWN))
    for first, marks, value in ((0, hub_marks, gh), (8, rel_marks, gr)):
        high, low = split(value)
        sums = (dot(marks, high) + dot(marks, low)).reshape(2, CHIP_COUNT, 8, WIDE)
        mine_ref[:, first : first + 8, :] = sums[0]
        other_ref[:, first : first + 8, :] = sums[1]


def add_pairs(a_ref, b_ref, c_ref, d_ref, out_ref):
    out_ref[:, :NEG, :] = a_ref[...] + b_ref[...]
    out_ref[:, NEG:, :] = c_ref[...] + d_ref[...]


def scatter_entities(head_ref, gradh_ref, asked_ref, answer_ref, out_ref,
                     th_ref, tl_ref, hh_ref, hl_ref, row_ref):
    @pl.when(pl.program_id(0) == 0)
    def _():
        asked = asked_ref[...]
        row_ref[...] = jnp.broadcast_to(aux_column(asked).astype(I32) - 1, (SLOTS, 128))
        slope = -jax.nn.sigmoid(-aux_column(answer_ref[...]))
        high, low = split((without_aux(asked) * slope).T)
        th_ref[...] = high
        tl_ref[...] = low
        high, low = split(gradh_ref[...].T)
        hh_ref[...] = high
        hl_ref[...] = low

    count = out_ref.shape[1]
    first = pl.program_id(0) * count
    rows = row_ref[...]
    lane = iota((SLOTS, 128), 1) + first
    marks = jnp.concatenate([hot(rows == lane + k * 128) for k in range(count // 128)], axis=1)
    grad = dot(th_ref[...], marks) + dot(tl_ref[...], marks)
    marks = hot(iota((count, TRIP), 0) + first == head_ref[...] - HUB)
    nt = ((1,), (1,))
    grad = grad + (dot(hh_ref[...], marks, nt) + dot(hl_ref[...], marks, nt))
    out_ref[:HALF, :] = grad[:HALF]
    out_ref[HALF:, :] = grad[SIDE : SIDE + HALF]


def update_own(sums_ref, mine_ref, neg_ref, out_ref):
    total = jnp.sum(sums_ref[...], axis=0)
    neg_ref[...] = total[:NEG]
    grad = total[NEG:]
    mine = mine_ref[...]
    accum = aux_column(mine) + jnp.sum(grad * grad, axis=1, keepdims=True) / WIDTH
    new = mine - LEARN_RATE * grad / jnp.sqrt(accum)
    new = jnp.where(iota(new.shape, 1) == AUX, accum, new)
    out_ref[...] = jnp.broadcast_to(new[None], out_ref.shape)


def place_new(core_ref, mine_ref, other_ref, hub_ref, hubacc_ref, rel_ref, relacc_ref, held_ref):
    core = core_ref[0]
    for part_ref, side in ((mine_ref, core), (other_ref, 1 - core)):
        hubs = part_ref[:, :HUB_OWN, :].reshape(HUB // 2, WIDE).T
        at = pl.ds(pl.multiple_of(side * (HUB // 2), 128), HUB // 2)
        hub_ref[:HALF, at] = hubs[:HALF]
        hub_ref[HALF:, at] = hubs[SIDE : SIDE + HALF]
        hubacc_ref[:, at] = hubs[AUX : AUX + 1]
        for chip in range(CHIP_COUNT):
            held_ref[chip * REL_OWN : (chip + 1) * REL_OWN, :] = part_ref[
                chip, HUB_OWN : HUB_OWN + REL_OWN, :
            ]
        rels = held_ref[...].T
        at = pl.ds(pl.multiple_of(side * (REL // 2), 128), REL // 2)
        rel_ref[:HALF, at] = rels[:HALF]
        rel_ref[HALF:, at] = rels[SIDE : SIDE + HALF]
        relacc_ref[:, at] = rels[AUX : AUX + 1]


def update_entities(rows_ref, neg_ref, ent_ref, acc_ref, grad_ref, new_ref, newacc_ref):
    count = ent_ref.shape[1]
    first = pl.program_id(0) * count
    rows = rows_ref[...][:, :1]
    marks = hot(iota((NEG, count), 1) + first == rows)
    high, low = split(neg_ref[...])
    tn = ((0,), (0,))
    more = dot(high, marks, tn) + dot(low, marks, tn)
    g_re = grad_ref[:HALF, :] + more[:HALF]
    g_im = grad_ref[HALF:, :] + more[SIDE : SIDE + HALF]
    square = jnp.sum(g_re * g_re, axis=0, keepdims=True) + jnp.sum(
        g_im * g_im, axis=0, keepdims=True
    )
    accum = acc_ref[...] + square / WIDTH
    newacc_ref[...] = accum
    root = jnp.sqrt(accum)
    new_ref[:HALF, :] = ent_ref[:HALF, :] - LEARN_RATE * g_re / root
    new_ref[HALF:, :] = ent_ref[HALF:, :] - LEARN_RATE * g_im / root


def shape(*dims, dtype=F32):
    return jax.ShapeDtypeStruct(dims, dtype)


def body(
    entity_table,
    entity_accum,
    hub_table,
    hub_accum,
    relation_table,
    relation_accum,
    head_ids,
    relation_ids,
    tail_owner,
    tail_rows,
    negative_rows,
):
    core = lax.axis_index("core").astype(I32)
    chip = lax.axis_index(CHIPS).astype(I32)
    core_arg = core.reshape(1)
    own_arg = (core * CHIP_COUNT + chip).reshape(1)
    ent_t, hub_t, rel_t = entity_table.T, hub_table.T, relation_table.T
    head_row, rel_row = head_ids.reshape(1, TRIP), relation_ids.reshape(1, TRIP)
    owner_row, tail_row = tail_owner.reshape(1, TRIP), tail_rows.reshape(1, TRIP)

    picked = pl.pallas_call(
        pick_negatives,
        out_shape=shape(NEG, WIDE),
        in_specs=[SMEM, VMEM],
        out_specs=VMEM,
        scratch_shapes=[pltpu.VMEM((WIDE, 128), F32)],
        compiler_params=params(),
        name="pick_negatives",
    )(negative_rows, ent_t)
    negs = lax.all_gather(picked, SHARD, axis=0, tiled=True)

    query, heads, rels, sent, place = pl.pallas_call(
        prepare,
        out_shape=[
            shape(TRIP, WIDE), shape(TRIP, WIDE), shape(TRIP, WIDE), shape(SLOTS, WIDE),
            shape(TRIP, 128, dtype=I32),
        ],
        in_specs=[VMEM] * 7,
        out_specs=[VMEM] * 5,
        compiler_params=params(),
        name="prepare",
    )(head_row, rel_row, owner_row, tail_row, ent_t, hub_t, rel_t)

    def exchange(rows):
        parts = rows.reshape(2 * CHIP_COUNT, CAP, WIDE)
        got = lax.all_to_all(parts, SHARD, split_axis=0, concat_axis=0, tiled=True)
        return got.reshape(SLOTS, WIDE)

    asked = exchange(sent)
    ent_high, ent_low, mine_rows = pl.pallas_call(
        turn_tables,
        out_shape=[
            shape(ENT, WIDE, dtype=BF16), shape(ENT, WIDE, dtype=BF16), shape(OWN, WIDE)
        ],
        in_specs=[SMEM] + [VMEM] * 5,
        out_specs=[VMEM] * 3,
        scratch_shapes=[pltpu.VMEM((WIDE, 128), F32)],
        compiler_params=params(),
        cost_estimate=cost(1e6, 12e6),
        name="turn_tables",
    )(own_arg, ent_t, hub_t, rel_t, hub_accum.reshape(1, HUB), relation_accum.reshape(1, REL))

    rows = 256
    answer = pl.pallas_call(
        answer_queries,
        out_shape=shape(SLOTS, WIDE),
        grid=(SLOTS // rows,),
        in_specs=[pl.BlockSpec((rows, WIDE), lambda i: (i, 0)), VMEM, VMEM],
        out_specs=pl.BlockSpec((rows, WIDE), lambda i: (i, 0)),
        compiler_params=params(),
        name="answer_queries",
    )(asked, ent_high, ent_low)
    back = exchange(answer)

    group = 16
    steps = CHIP_COUNT // group
    neg_mine, neg_other, grad_q, loss_sum = pl.pallas_call(
        score,
        out_shape=[
            shape(CHIP_COUNT, NEG, WIDE), shape(CHIP_COUNT, NEG, WIDE), shape(TRIP, WIDE),
            shape(TRIP, 128),
        ],
        grid_spec=pltpu.PrefetchScalarGridSpec(
            num_scalar_prefetch=1,
            grid=(2, steps),
            in_specs=[
                pl.BlockSpec((TRIP, WIDE), lambda i, c, core: (0, 0)),
                pl.BlockSpec(
                    (group, 1, NEG, WIDE), lambda i, c, core: (c, (i + core[0]) % 2, 0, 0)
                ),
            ],
            out_specs=[
                pl.BlockSpec(
                    (group, NEG, WIDE), lambda i, c, core: (jnp.where(i == 0, c, steps - 1), 0, 0)
                ),
                pl.BlockSpec(
                    (group, NEG, WIDE), lambda i, c, core: (jnp.where(i == 0, 0, c), 0, 0)
                ),
                pl.BlockSpec((TRIP, WIDE), lambda i, c, core: (0, 0)),
                pl.BlockSpec((TRIP, 128), lambda i, c, core: (0, 0)),
            ],
            scratch_shapes=[
                pltpu.VMEM((TRIP, WIDE), BF16), pltpu.VMEM((TRIP, WIDE), BF16),
                pltpu.VMEM((TRIP, 128), F32),
            ],
        ),
        compiler_params=params(),
        cost_estimate=cost(20e9, 12e6),
        name="score",
    )(core_arg, query, negs.reshape(CHIP_COUNT, 2, NEG, WIDE))
    neg_swapped = lax.ppermute(neg_other, "core", SWAP)

    grad_head, both_mine, both_other, loss = pl.pallas_call(
        close_triples,
        out_shape=[
            shape(TRIP, WIDE), shape(CHIP_COUNT, OWN, WIDE), shape(CHIP_COUNT, OWN, WIDE),
            shape(1, TRIP),
        ],
        in_specs=[SMEM] + [VMEM] * 8,
        out_specs=[VMEM] * 4,
        compiler_params=params(),
        name="close_triples",
    )(core_arg, back, place, heads, rels, grad_q, loss_sum, head_row, rel_row)
    both_swapped = lax.ppermute(both_other, "core", SWAP)

    block = pl.BlockSpec((8, NEG, WIDE), lambda i: (i, 0, 0))
    paired = pl.pallas_call(
        add_pairs,
        out_shape=shape(CHIP_COUNT, NEG + OWN, WIDE),
        grid=(CHIP_COUNT // 8,),
        in_specs=[block] * 4,
        out_specs=pl.BlockSpec((8, NEG + OWN, WIDE), lambda i: (i, 0, 0)),
        compiler_params=params(),
        name="add_pairs",
    )(neg_mine, neg_swapped, both_mine, both_swapped)
    sums = lax.all_to_all(paired, CHIPS, split_axis=0, concat_axis=0, tiled=True)

    columns = 256
    whole = pl.BlockSpec((SLOTS, WIDE), lambda i: (0, 0))
    entity_grad = pl.pallas_call(
        scatter_entities,
        out_shape=shape(WIDTH, ENT),
        grid=(ENT // columns,),
        in_specs=[
            pl.BlockSpec((1, TRIP), lambda i: (0, 0)),
            pl.BlockSpec((TRIP, WIDE), lambda i: (0, 0)),
            whole,
            whole,
        ],
        out_specs=pl.BlockSpec((WIDTH, columns), lambda i: (0, i)),
        scratch_shapes=[
            pltpu.VMEM((WIDE, SLOTS), BF16), pltpu.VMEM((WIDE, SLOTS), BF16),
            pltpu.VMEM((WIDE, TRIP), BF16), pltpu.VMEM((WIDE, TRIP), BF16),
            pltpu.VMEM((SLOTS, 128), I32),
        ],
        compiler_params=params(),
        cost_estimate=cost(10e9, 12e6),
        name="scatter_entities",
    )(head_row, grad_head, asked, answer)

    neg_grad, own_new = pl.pallas_call(
        update_own,
        out_shape=[shape(NEG, WIDE), shape(CHIP_COUNT, OWN, WIDE)],
        in_specs=[VMEM] * 2,
        out_specs=[VMEM] * 2,
        compiler_params=params(),
        name="update_own",
    )(sums, mine_rows)
    new_mine = lax.all_to_all(own_new, CHIPS, split_axis=0, concat_axis=0, tiled=True)
    new_other = lax.ppermute(new_mine, "core", SWAP)

    columns = 512
    entity_new, entity_accum_new = pl.pallas_call(
        update_entities,
        out_shape=[shape(WIDTH, ENT), shape(1, ENT)],
        grid=(ENT // columns,),
        in_specs=[
            pl.BlockSpec((NEG, 128), lambda i: (0, 0)),
            pl.BlockSpec((NEG, WIDE), lambda i: (0, 0)),
            pl.BlockSpec((WIDTH, columns), lambda i: (0, i)),
            pl.BlockSpec((1, columns), lambda i: (0, i)),
            pl.BlockSpec((WIDTH, columns), lambda i: (0, i)),
        ],
        out_specs=[
            pl.BlockSpec((WIDTH, columns), lambda i: (0, i)),
            pl.BlockSpec((1, columns), lambda i: (0, i)),
        ],
        compiler_params=params(),
        cost_estimate=cost(1e9, 14e6),
        name="update_entities",
    )(
        jnp.broadcast_to(negative_rows[:, None], (NEG, 128)),
        neg_grad,
        ent_t,
        entity_accum.reshape(1, ENT),
        entity_grad,
    )

    hub_new, hub_accum_new, rel_new, rel_accum_new = pl.pallas_call(
        place_new,
        out_shape=[shape(WIDTH, HUB), shape(1, HUB), shape(WIDTH, REL), shape(1, REL)],
        in_specs=[SMEM, VMEM, VMEM],
        out_specs=[VMEM] * 4,
        scratch_shapes=[pltpu.VMEM((REL // 2, WIDE), F32)],
        compiler_params=params(),
        name="place_new",
    )(core_arg, new_mine, new_other)
    return (
        entity_new.T,
        entity_accum_new.reshape(ENT),
        hub_new.T,
        hub_accum_new.reshape(HUB),
        rel_new.T,
        rel_accum_new.reshape(REL),
        loss.reshape(TRIP),
    )


def solution(mesh):
    fine = Mesh(mesh.devices.reshape(SIZES), SHARD)
    rows, vector = P(SHARD, None), P(SHARD)
    placed = (rows, vector, P(), P(), P(), P(), vector, vector, rows, vector, vector)
    return jax.shard_map(
        body,
        mesh=fine,
        in_specs=placed,
        out_specs=(rows, vector, P(), P(), P(), P(), vector),
        check_vma=False,
    )
```

```python
import jax
import jax.numpy as jnp
from jax import lax
from jax.experimental import pallas as pl
from jax.experimental.pallas import tpu as pltpu
from jax.sharding import Mesh, PartitionSpec as P

LEARN_RATE = 0.1
CHIPS = ("z", "x", "y")
SHARD = ("z", "x", "y", "core")
SIZES = (4, 4, 4, 2)
SWAP = [(0, 1), (1, 0)]
F32, BF16, I32 = jnp.float32, jnp.bfloat16, jnp.int32

WIDTH, HALF, SIDE, WIDE, AUX = 400, 200, 256, 512, 200
ENT, HUB, REL, TRIP, CHIP_COUNT, CAP, NEG = 2048, 1024, 512, 512, 64, 8, 16
SLOTS = 2 * CHIP_COUNT * CAP
HUB_OWN, REL_OWN, OWN = 8, 4, 40
VMEM = pl.BlockSpec(memory_space=pltpu.VMEM)
SMEM = pl.BlockSpec(memory_space=pltpu.SMEM)


def params(mib):
    return pltpu.CompilerParams(vmem_limit_bytes=mib << 20)


def cost(flops, nbytes):
    return pl.CostEstimate(flops=int(flops), bytes_accessed=int(nbytes), transcendentals=0)


def split(x):
    high = x.astype(BF16)
    return high, (x - high.astype(F32)).astype(BF16)


def dot(a, b, contract=((1,), (0,))):
    return lax.dot_general(a, b, (contract, ((), ())), preferred_element_type=F32)


def hot(condition):
    return jnp.where(condition, 1.0, 0.0).astype(BF16)


def iota(shape, axis):
    return lax.broadcasted_iota(I32, shape, axis)


def aux_column(rows):
    part = rows[:, 128:SIDE]
    return jnp.sum(jnp.where(iota(part.shape, 1) == AUX - 128, part, 0.0), axis=1, keepdims=True)


def without_aux(rows):
    return jnp.where(iota(rows.shape, 1) == AUX, 0.0, rows)


def widen(re, im, aux=None):
    n = re.shape[1]
    gap = jnp.zeros((SIDE - HALF, n), F32)
    if aux is not None:
        first = jnp.where(iota((8, n), 0) == 0, aux, 0.0)
        middle = jnp.concatenate([first, jnp.zeros((SIDE - HALF - 8, n), F32)], axis=0)
    else:
        middle = gap
    return jnp.concatenate([re, middle, im, gap], axis=0)


def pick_negatives(rows_ref, ent_ref, out_ref, held_ref):
    held_ref[...] = jnp.zeros_like(held_ref)
    lane = iota((WIDTH, 128), 1)
    for j in range(NEG):
        row = rows_ref[j]
        block = ent_ref[:, pl.ds(pl.multiple_of((row // 128) * 128, 128), 128)]
        block = pltpu.roll(block, (j - row % 128 + 128) % 128, 1)
        here = lane == j
        held_ref[0:HALF, :] = jnp.where(here[:HALF], block[:HALF], held_ref[0:HALF, :])
        held_ref[SIDE : SIDE + HALF, :] = jnp.where(
            here[:HALF], block[HALF:], held_ref[SIDE : SIDE + HALF, :]
        )
    out_ref[...] = held_ref[...].T[:NEG]


def prepare(head_ref, rel_ref, owner_ref, tail_ref, ent_ref, hub_ref, relt_ref,
            query_ref, headv_ref, relv_ref, sent_ref, place_ref):
    head = head_ref[...]

    def gather(table, ids):
        marks = hot(iota((table.shape[1], TRIP), 0) == ids)
        high, low = split(table)
        return dot(high, marks) + dot(low, marks)

    heads = gather(hub_ref[...], head) + gather(ent_ref[...], head - HUB)
    rels = gather(relt_ref[...], rel_ref[...])
    h_re, h_im, r_re, r_im = heads[:HALF], heads[HALF:], rels[:HALF], rels[HALF:]
    q_re = h_re * r_re - h_im * r_im
    q_im = h_re * r_im + h_im * r_re
    headv_ref[...] = widen(h_re, h_im).T
    relv_ref[...] = widen(r_re, r_im).T
    query_ref[...] = widen(q_re, q_im).T

    owner = owner_ref[...]
    owned = hot(iota((2 * CHIP_COUNT, TRIP), 0) == owner)
    before = hot(iota((TRIP, TRIP), 0) < iota((TRIP, TRIP), 1))
    rank = jnp.sum(dot(owned, before) * owned.astype(F32), axis=0, keepdims=True)
    place = owner * CAP + rank.astype(I32)
    place_ref[...] = jnp.broadcast_to(place.astype(F32), (128, TRIP)).T.astype(I32)

    marks = hot(iota((SLOTS, TRIP), 0) == place)
    high, low = split(widen(q_re, q_im, tail_ref[...].astype(F32) + 1.0).T)
    sent_ref[...] = dot(marks, high) + dot(marks, low)


def turn_tables(own_ref, ent_ref, hub_ref, relt_ref, hubacc_ref, relacc_ref,
                high_ref, low_ref, mine_ref, held_ref):
    for block in range(ENT // 512):
        part = ent_ref[:, block * 512 : (block + 1) * 512]
        high, low = split(widen(part[:HALF], part[HALF:]).T)
        high_ref[block * 512 : (block + 1) * 512, :] = high
        low_ref[block * 512 : (block + 1) * 512, :] = low
    own = own_ref[0]
    lane = iota((1, 128), 1)

    def rows_of(ref, first, at):
        block = ref[:, pl.ds(pl.multiple_of((first // 128) * 128, 128), 128)]
        return pltpu.roll(block, (at - first % 128 + 128) % 128, 1)

    hub = rows_of(hub_ref, own * HUB_OWN, 0)
    rel = rows_of(relt_ref, own * REL_OWN, HUB_OWN)
    hub_acc = rows_of(hubacc_ref, own * HUB_OWN, 0)
    rel_acc = rows_of(relacc_ref, own * REL_OWN, HUB_OWN)
    is_hub, is_rel = lane < HUB_OWN, (lane >= HUB_OWN) & (lane < HUB_OWN + REL_OWN)
    both = jnp.where(is_hub, hub, jnp.where(is_rel, rel, 0.0))
    acc = jnp.where(is_hub, hub_acc, jnp.where(is_rel, rel_acc, 1.0))
    held_ref[...] = widen(both[:HALF], both[HALF:], acc)
    held_ref[SIDE + HALF : SIDE + HALF + 8, :] = jnp.broadcast_to(acc, (8, 128))
    rows = held_ref[...].T
    rel = rows[HUB_OWN : HUB_OWN + 8]
    rel = jnp.where(iota(rel.shape, 0) < REL_OWN, rel, pltpu.roll(rel, REL_OWN, 0))
    for k, tile in enumerate(pack(rows[:HUB_OWN], rel)):
        mine_ref[k * 8 : (k + 1) * 8, :] = tile


def pack(hub, rel):
    lane, low = iota((hub.shape[0], 128), 1), iota((hub.shape[0], 128), 0) % 8 < REL_OWN
    hubs = [hub[:, k * 128 : (k + 1) * 128] for k in range(4)]
    rels = [rel[:, k * 128 : (k + 1) * 128] for k in range(4)]
    turned = pltpu.roll(hubs[3], 72, 1)
    tail = pltpu.roll(jnp.where(low, rels[1], rels[3]), 16, 1)
    last = jnp.where(lane < 16, turned, jnp.where(lane < 89, tail, pltpu.roll(hubs[1], 17, 1)))
    return (
        hubs[0],
        hubs[2],
        jnp.where(low, rels[0], rels[2]),
        jnp.where(lane < 72, hubs[1], turned),
        jnp.where(lane < 90, last, 0.0),
    )


def answer_queries(asked_ref, high_ref, low_ref, out_ref):
    asked = asked_ref[...]
    row = aux_column(asked).astype(I32) - 1
    marks = hot(iota((asked.shape[0], ENT), 1) == row)
    tails = dot(marks, high_ref[...]) + dot(marks, low_ref[...])
    positive = jnp.sum(asked * tails, axis=1, keepdims=True)
    slope = -jax.nn.sigmoid(-positive)
    out_ref[...] = jnp.where(iota(tails.shape, 1) == AUX, positive, slope * tails)


def score(query_ref, neg_ref, grad_in, loss_in, back_ref, grad_ref, loss_ref):
    qh, ql = split(query_ref[...])
    grad, total = grad_in[...], loss_in[...]
    step = 256
    for first in range(0, neg_ref.shape[0], step):
        nh, nl = split(neg_ref[first : first + step, :])
        nt = ((1,), (1,))
        s = dot(qh, nh, nt) + (dot(qh, nl, nt) + dot(ql, nh, nt))
        small = jnp.exp(-jnp.abs(s))
        loss = jnp.maximum(s, 0.0) + jnp.log1p(small)
        for part in range(step // 128):
            total = total + loss[:, part * 128 : (part + 1) * 128]
        weight = jnp.where(s >= 0.0, 1.0, small) / (1.0 + small) * (1.0 / ENT_NEGS)
        gh, gl = split(weight)
        grad = grad + (dot(gh, nh) + (dot(gh, nl) + dot(gl, nh)))
        tn = ((0,), (0,))
        back_ref[first : first + step, :] = dot(gh, qh, tn) + (dot(gh, ql, tn) + dot(gl, qh, tn))
    grad_ref[...] = grad
    loss_ref[...] = total


ENT_NEGS = 2 * CHIP_COUNT * NEG


def close_triples(core_ref, back_ref, place_ref, headv_ref, relv_ref, gradq_ref, loss_ref,
                  head_ref, rel_ref, gradh_ref, mine_ref, other_ref, out_ref):
    place = place_ref[...]
    lane = iota((TRIP, 128), 1)
    marks = jnp.concatenate(
        [hot(place == lane + part * 128) for part in range(SLOTS // 128)], axis=1
    )
    high, low = split(back_ref[...])
    tail = dot(marks, high) + dot(marks, low)
    positive = aux_column(tail)
    neg_loss = jnp.sum(loss_ref[...], axis=1, keepdims=True) * (1.0 / ENT_NEGS)
    drop = -positive
    loss = jnp.maximum(drop, 0.0) + jnp.log1p(jnp.exp(-jnp.abs(drop))) + neg_loss
    out_ref[...] = jnp.broadcast_to(loss, (TRIP, 128)).T[:1]
    grad = without_aux(tail) + gradq_ref[...]
    g_re, g_im = grad[:, :SIDE], grad[:, SIDE:]
    heads, rels = headv_ref[...], relv_ref[...]
    h_re, h_im, r_re, r_im = heads[:, :SIDE], heads[:, SIDE:], rels[:, :SIDE], rels[:, SIDE:]
    gh = jnp.concatenate([g_re * r_re + g_im * r_im, g_im * r_re - g_re * r_im], axis=1)
    gr = jnp.concatenate([g_re * h_re + g_im * h_im, g_im * h_re - g_re * h_im], axis=1)
    gradh_ref[...] = gh

    core = core_ref[0]
    at = iota((2 * CHIP_COUNT * 8, TRIP), 0)
    head, rel = head_ref[...], rel_ref[...]
    hub_id = (at + core * (HUB // 2)) % HUB
    rel_id = (at // 8 * REL_OWN + at % REL_OWN + core * (REL // 2)) % REL
    sums = []
    for marks, value in ((hot(hub_id == head), gh), (hot(rel_id == rel), gr)):
        high, low = split(value)
        sums.append(dot(marks, high) + dot(marks, low))
    for k, tile in enumerate(pack(*sums)):
        tile = tile.reshape(2, CHIP_COUNT, 8, 128)
        mine_ref[:, k * 8 : (k + 1) * 8, :] = tile[0]
        other_ref[:, k * 8 : (k + 1) * 8, :] = tile[1]


def scatter_entities(head_ref, gradh_ref, asked_ref, answer_ref, out_ref,
                     th_ref, tl_ref, hh_ref, hl_ref, row_ref):
    @pl.when(pl.program_id(0) == 0)
    def _():
        asked = asked_ref[...]
        row_ref[...] = jnp.broadcast_to(aux_column(asked).astype(I32) - 1, (SLOTS, 128))
        slope = -jax.nn.sigmoid(-aux_column(answer_ref[...]))
        high, low = split((without_aux(asked) * slope).T)
        th_ref[...] = high
        tl_ref[...] = low
        high, low = split(gradh_ref[...].T)
        hh_ref[...] = high
        hl_ref[...] = low

    count = out_ref.shape[1]
    first = pl.program_id(0) * count
    rows = row_ref[...]
    lane = iota((SLOTS, 128), 1) + first
    marks = jnp.concatenate([hot(rows == lane + k * 128) for k in range(count // 128)], axis=1)
    grad = dot(th_ref[...], marks) + dot(tl_ref[...], marks)
    marks = hot(iota((count, TRIP), 0) + first == head_ref[...] - HUB)
    nt = ((1,), (1,))
    grad = grad + (dot(hh_ref[...], marks, nt) + dot(hl_ref[...], marks, nt))
    out_ref[:HALF, :] = grad[:HALF]
    out_ref[HALF:, :] = grad[SIDE : SIDE + HALF]


def update_own(sums_ref, mine_ref, out_ref):
    lane = iota((8, 128), 1)
    grads = [jnp.sum(sums_ref[:, k * 8 : (k + 1) * 8, :], axis=0) for k in range(5)]
    mine = [mine_ref[k * 8 : (k + 1) * 8, :] for k in range(5)]

    def across(x):
        return jnp.sum(x, axis=1, keepdims=True)

    in_hub, in_rel = lane < 16, (lane >= 16) & (lane < 88)
    squares = [g * g for g in grads]
    hub = across(squares[0] + squares[1] + squares[3] + jnp.where(in_hub, squares[4], 0.0))
    rel = jnp.broadcast_to(across(squares[2] + jnp.where(in_rel, squares[4], 0.0)), (8, 128))
    rel = rel + pltpu.roll(rel, REL_OWN, 0)
    hub_acc = across(jnp.where(lane == 89, mine[4], 0.0)) + hub / WIDTH
    rel_acc = across(jnp.where(lane == 88, mine[4], 0.0)) + rel / WIDTH
    hub_root, rel_root = jnp.sqrt(hub_acc), jnp.sqrt(rel_acc)
    mixed = jnp.where(in_hub, hub_root, rel_root)
    roots = (hub_root, hub_root, rel_root, hub_root, mixed)
    new = [m - LEARN_RATE * g / root for m, g, root in zip(mine, grads, roots)]
    new[4] = jnp.where(lane == 88, rel_acc, jnp.where(lane == 89, hub_acc, new[4]))
    for k in range(5):
        out_ref[:, k * 8 : (k + 1) * 8, :] = jnp.broadcast_to(new[k][None], (CHIP_COUNT, 8, 128))


def place_new(core_ref, mine_ref, other_ref, hub_ref, hubacc_ref, rel_ref, relacc_ref, held_ref):
    core = core_ref[0]
    for part_ref, side in ((mine_ref, core), (other_ref, 1 - core)):
        def turned(k):
            return part_ref[:, k * 8 : (k + 1) * 8, :].reshape(CHIP_COUNT * 8, 128).T

        at = pl.ds(pl.multiple_of(side * (HUB // 2), 128), HUB // 2)
        hub_ref[0:128, at] = turned(0)
        hub_ref[HALF : HALF + 128, at] = turned(1)
        mixed = turned(3)
        hub_ref[128:HALF, at] = mixed[:72]
        hub_ref[HALF + 128 : HALF + 184, at] = mixed[72:]
        last = turned(4)
        hub_ref[HALF + 184 : WIDTH, at] = last[:16]
        hubacc_ref[:, at] = last[89:90]
        for chip in range(CHIP_COUNT):
            here = slice(chip * REL_OWN, (chip + 1) * REL_OWN)
            held_ref[0, here, :] = part_ref[chip, 16:20, :]
            held_ref[1, here, :] = part_ref[chip, 32:36, :]
            held_ref[2, here, :] = part_ref[chip, 20:24, :]
            held_ref[3, here, :] = part_ref[chip, 36:40, :]
        at = pl.ds(pl.multiple_of(side * (REL // 2), 128), REL // 2)
        for half in range(2):
            rel_ref[half * HALF : half * HALF + 128, at] = held_ref[2 * half].T
            last = held_ref[2 * half + 1].T
            rel_ref[half * HALF + 128 : (half + 1) * HALF, at] = last[16:88]
            if half == 0:
                relacc_ref[:, at] = last[88:89]


def update_entities(rows_ref, neg_ref, ent_ref, acc_ref, grad_ref, new_ref, newacc_ref):
    count = ent_ref.shape[1]
    first = pl.program_id(0) * count
    rows = rows_ref[...][:, :1]
    marks = hot(iota((NEG, count), 1) + first == rows)
    high, low = split(neg_ref[...])
    tn = ((0,), (0,))
    more = dot(high, marks, tn) + dot(low, marks, tn)
    g_re = grad_ref[:HALF, :] + more[:HALF]
    g_im = grad_ref[HALF:, :] + more[SIDE : SIDE + HALF]
    square = jnp.sum(g_re * g_re, axis=0, keepdims=True) + jnp.sum(
        g_im * g_im, axis=0, keepdims=True
    )
    accum = acc_ref[...] + square / WIDTH
    newacc_ref[...] = accum
    root = jnp.sqrt(accum)
    new_ref[:HALF, :] = ent_ref[:HALF, :] - LEARN_RATE * g_re / root
    new_ref[HALF:, :] = ent_ref[HALF:, :] - LEARN_RATE * g_im / root


def around(block, axis):
    count = SIZES[SHARD.index(axis)]
    turns = [[(i, (i + k) % count) for i in range(count)] for k in range(1, count)]
    return [block] + [lax.ppermute(block, axis, turn) for turn in turns]


def add_around(blocks, axis):
    count = SIZES[SHARD.index(axis)]
    turns = [[((i + k) % count, i) for i in range(count)] for k in range(1, count)]
    one, two, three = [lax.ppermute(blocks[k + 1], axis, turn) for k, turn in enumerate(turns)]
    return (blocks[0] + one) + (two + three)


def shape(*dims, dtype=F32):
    return jax.ShapeDtypeStruct(dims, dtype)


def body(
    entity_table,
    entity_accum,
    hub_table,
    hub_accum,
    relation_table,
    relation_accum,
    head_ids,
    relation_ids,
    tail_owner,
    tail_rows,
    negative_rows,
):
    core = lax.axis_index("core").astype(I32)
    chip = lax.axis_index(CHIPS).astype(I32)
    core_arg = core.reshape(1)
    own_arg = (core * CHIP_COUNT + chip).reshape(1)
    ent_t, hub_t, rel_t = entity_table.T, hub_table.T, relation_table.T
    head_row, rel_row = head_ids.reshape(1, TRIP), relation_ids.reshape(1, TRIP)
    owner_row, tail_row = tail_owner.reshape(1, TRIP), tail_rows.reshape(1, TRIP)

    picked = pl.pallas_call(
        pick_negatives,
        out_shape=shape(NEG, WIDE),
        in_specs=[SMEM, VMEM],
        out_specs=VMEM,
        scratch_shapes=[pltpu.VMEM((WIDE, 128), F32)],
        compiler_params=params(12),
        name="pick_negatives",
    )(negative_rows, ent_t)
    picked, head_row = lax.optimization_barrier((picked, head_row))
    near = jnp.concatenate(around(picked, "z"), axis=0)

    query, heads, rels, sent, place = pl.pallas_call(
        prepare,
        out_shape=[
            shape(TRIP, WIDE), shape(TRIP, WIDE), shape(TRIP, WIDE), shape(SLOTS, WIDE),
            shape(TRIP, 128, dtype=I32),
        ],
        in_specs=[VMEM] * 7,
        out_specs=[VMEM] * 5,
        compiler_params=params(24),
        name="prepare",
    )(head_row, rel_row, owner_row, tail_row, ent_t, hub_t, rel_t)

    def exchange(rows):
        parts = rows.reshape(2 * CHIP_COUNT, CAP, WIDE)
        got = lax.all_to_all(parts, SHARD, split_axis=0, concat_axis=0, tiled=True)
        return got.reshape(SLOTS, WIDE)

    sent, near = lax.optimization_barrier((sent, near))
    near = jnp.concatenate(around(near, "x"), axis=0)
    near = lax.all_gather(near, "y", axis=0, tiled=True)
    far = lax.ppermute(near, "core", SWAP)
    asked = exchange(sent)
    ent_high, ent_low, mine_rows = pl.pallas_call(
        turn_tables,
        out_shape=[
            shape(ENT, WIDE, dtype=BF16), shape(ENT, WIDE, dtype=BF16), shape(OWN, 128)
        ],
        in_specs=[SMEM] + [VMEM] * 5,
        out_specs=[VMEM] * 3,
        scratch_shapes=[pltpu.VMEM((WIDE, 128), F32)],
        compiler_params=params(22),
        cost_estimate=cost(1e6, 12e6),
        name="turn_tables",
    )(own_arg, ent_t, hub_t, rel_t, hub_accum.reshape(1, HUB), relation_accum.reshape(1, REL))

    rows = 256
    answer = pl.pallas_call(
        answer_queries,
        out_shape=shape(SLOTS, WIDE),
        grid=(SLOTS // rows,),
        in_specs=[pl.BlockSpec((rows, WIDE), lambda i: (i, 0)), VMEM, VMEM],
        out_specs=pl.BlockSpec((rows, WIDE), lambda i: (i, 0)),
        compiler_params=params(16),
        name="answer_queries",
    )(asked, ent_high, ent_low)
    back = exchange(answer)

    def scored(block, grad, loss):
        return pl.pallas_call(
            score,
            out_shape=[shape(*block.shape), shape(TRIP, WIDE), shape(TRIP, 128)],
            in_specs=[VMEM] * 4,
            out_specs=[VMEM] * 3,
            compiler_params=params(24),
            cost_estimate=cost(10e9, 8e6),
            name="score",
        )(query, block, grad, loss)

    zeros = jnp.zeros((TRIP, WIDE), F32), jnp.zeros((TRIP, 128), F32)
    near_back, grad_q, loss_sum = scored(near, *zeros)
    far_back, grad_q, loss_sum = scored(far, grad_q, loss_sum)
    part = near_back + lax.ppermute(far_back, "core", SWAP)
    part = lax.psum_scatter(part, "y", scatter_dimension=0, tiled=True)
    for axis in ("x", "z"):
        part = add_around(jnp.split(part, 4, axis=0), axis)
    neg_grad = part

    grad_head, both_mine, both_other, loss = pl.pallas_call(
        close_triples,
        out_shape=[
            shape(TRIP, WIDE), shape(CHIP_COUNT, OWN, 128), shape(CHIP_COUNT, OWN, 128),
            shape(1, TRIP),
        ],
        in_specs=[SMEM] + [VMEM] * 8,
        out_specs=[VMEM] * 4,
        compiler_params=params(24),
        name="close_triples",
    )(core_arg, back, place, heads, rels, grad_q, loss_sum, head_row, rel_row)
    both_swapped = lax.ppermute(both_other, "core", SWAP)

    paired = both_mine + both_swapped
    paired, asked, answer = lax.optimization_barrier((paired, asked, answer))
    sums = lax.all_to_all(paired, CHIPS, split_axis=0, concat_axis=0, tiled=True)

    columns = 256
    whole = pl.BlockSpec((SLOTS, WIDE), lambda i: (0, 0))
    entity_grad = pl.pallas_call(
        scatter_entities,
        out_shape=shape(WIDTH, ENT),
        grid=(ENT // columns,),
        in_specs=[
            pl.BlockSpec((1, TRIP), lambda i: (0, 0)),
            pl.BlockSpec((TRIP, WIDE), lambda i: (0, 0)),
            whole,
            whole,
        ],
        out_specs=pl.BlockSpec((WIDTH, columns), lambda i: (0, i)),
        scratch_shapes=[
            pltpu.VMEM((WIDE, SLOTS), BF16), pltpu.VMEM((WIDE, SLOTS), BF16),
            pltpu.VMEM((WIDE, TRIP), BF16), pltpu.VMEM((WIDE, TRIP), BF16),
            pltpu.VMEM((SLOTS, 128), I32),
        ],
        compiler_params=params(26),
        cost_estimate=cost(10e9, 12e6),
        name="scatter_entities",
    )(head_row, grad_head, asked, answer)

    sums, entity_grad = lax.optimization_barrier((sums, entity_grad))
    own_new = pl.pallas_call(
        update_own,
        out_shape=shape(CHIP_COUNT, OWN, 128),
        in_specs=[VMEM] * 2,
        out_specs=VMEM,
        compiler_params=params(12),
        name="update_own",
    )(sums, mine_rows)
    new_mine = lax.all_to_all(own_new, CHIPS, split_axis=0, concat_axis=0, tiled=True)
    columns = 512
    entity_new, entity_accum_new = pl.pallas_call(
        update_entities,
        out_shape=[shape(WIDTH, ENT), shape(1, ENT)],
        grid=(ENT // columns,),
        in_specs=[
            pl.BlockSpec((NEG, 128), lambda i: (0, 0)),
            pl.BlockSpec((NEG, WIDE), lambda i: (0, 0)),
            pl.BlockSpec((WIDTH, columns), lambda i: (0, i)),
            pl.BlockSpec((1, columns), lambda i: (0, i)),
            pl.BlockSpec((WIDTH, columns), lambda i: (0, i)),
        ],
        out_specs=[
            pl.BlockSpec((WIDTH, columns), lambda i: (0, i)),
            pl.BlockSpec((1, columns), lambda i: (0, i)),
        ],
        compiler_params=params(12),
        cost_estimate=cost(1e9, 14e6),
        name="update_entities",
    )(
        jnp.broadcast_to(negative_rows[:, None], (NEG, 128)),
        neg_grad,
        ent_t,
        entity_accum.reshape(1, ENT),
        entity_grad,
    )

    new_other = lax.ppermute(new_mine, "core", SWAP)
    hub_new, hub_accum_new, rel_new, rel_accum_new = pl.pallas_call(
        place_new,
        out_shape=[shape(WIDTH, HUB), shape(1, HUB), shape(WIDTH, REL), shape(1, REL)],
        in_specs=[SMEM, VMEM, VMEM],
        out_specs=[VMEM] * 4,
        scratch_shapes=[pltpu.VMEM((4, REL // 2, 128), F32)],
        compiler_params=params(14),
        name="place_new",
    )(core_arg, new_mine, new_other)
    return (
        entity_new.T,
        entity_accum_new.reshape(ENT),
        hub_new.T,
        hub_accum_new.reshape(HUB),
        rel_new.T,
        rel_accum_new.reshape(REL),
        loss.reshape(TRIP),
    )


def solution(mesh):
    fine = Mesh(mesh.devices.reshape(SIZES), SHARD)
    rows, vector = P(SHARD, None), P(SHARD)
    placed = (rows, vector, P(), P(), P(), P(), vector, vector, rows, vector, vector)
    return jax.shard_map(
        body,
        mesh=fine,
        in_specs=placed,
        out_specs=(rows, vector, P(), P(), P(), P(), vector),
        check_vma=False,
    )
```

```python
import jax
import jax.numpy as jnp
from jax import lax
from jax.experimental import pallas as pl
from jax.experimental.pallas import tpu as pltpu
from jax.sharding import Mesh, PartitionSpec as P

LEARN_RATE = 0.1
CHIPS = ("z", "x", "y")
SHARD = ("z", "x", "y", "core")
SIZES = (4, 4, 4, 2)
SWAP = [(0, 1), (1, 0)]
F32, BF16, I32 = jnp.float32, jnp.bfloat16, jnp.int32

WIDTH, HALF, SIDE, WIDE, AUX = 400, 200, 256, 512, 200
ENT, HUB, REL, TRIP, CHIP_COUNT, CAP, NEG = 2048, 1024, 512, 512, 64, 8, 16
SLOTS = 2 * CHIP_COUNT * CAP
HUB_OWN, REL_OWN, OWN = 8, 4, 40
VMEM = pl.BlockSpec(memory_space=pltpu.VMEM)
SMEM = pl.BlockSpec(memory_space=pltpu.SMEM)


def params():
    return pltpu.CompilerParams(vmem_limit_bytes=56 << 20)


def cost(flops, nbytes):
    return pl.CostEstimate(flops=int(flops), bytes_accessed=int(nbytes), transcendentals=0)


def split(x):
    high = x.astype(BF16)
    return high, (x - high.astype(F32)).astype(BF16)


def dot(a, b, contract=((1,), (0,))):
    return lax.dot_general(a, b, (contract, ((), ())), preferred_element_type=F32)


def hot(condition):
    return jnp.where(condition, 1.0, 0.0).astype(BF16)


def iota(shape, axis):
    return lax.broadcasted_iota(I32, shape, axis)


def aux_column(rows):
    part = rows[:, 128:SIDE]
    return jnp.sum(jnp.where(iota(part.shape, 1) == AUX - 128, part, 0.0), axis=1, keepdims=True)


def without_aux(rows):
    return jnp.where(iota(rows.shape, 1) == AUX, 0.0, rows)


def widen(re, im, aux=None):
    n = re.shape[1]
    gap = jnp.zeros((SIDE - HALF, n), F32)
    if aux is not None:
        first = jnp.where(iota((8, n), 0) == 0, aux, 0.0)
        middle = jnp.concatenate([first, jnp.zeros((SIDE - HALF - 8, n), F32)], axis=0)
    else:
        middle = gap
    return jnp.concatenate([re, middle, im, gap], axis=0)


def pick_negatives(rows_ref, ent_ref, out_ref, held_ref):
    held_ref[...] = jnp.zeros_like(held_ref)
    lane = iota((WIDTH, 128), 1)
    for j in range(NEG):
        row = rows_ref[j]
        block = ent_ref[:, pl.ds(pl.multiple_of((row // 128) * 128, 128), 128)]
        block = pltpu.roll(block, (j - row % 128 + 128) % 128, 1)
        here = lane == j
        held_ref[0:HALF, :] = jnp.where(here[:HALF], block[:HALF], held_ref[0:HALF, :])
        held_ref[SIDE : SIDE + HALF, :] = jnp.where(
            here[:HALF], block[HALF:], held_ref[SIDE : SIDE + HALF, :]
        )
    out_ref[...] = held_ref[...].T[:NEG]


def prepare(head_ref, rel_ref, owner_ref, tail_ref, ent_ref, hub_ref, relt_ref,
            query_ref, headv_ref, relv_ref, sent_ref, place_ref):
    head = head_ref[...]

    def gather(table, ids):
        marks = hot(iota((table.shape[1], TRIP), 0) == ids)
        high, low = split(table)
        return dot(high, marks) + dot(low, marks)

    heads = gather(hub_ref[...], head) + gather(ent_ref[...], head - HUB)
    rels = gather(relt_ref[...], rel_ref[...])
    h_re, h_im, r_re, r_im = heads[:HALF], heads[HALF:], rels[:HALF], rels[HALF:]
    q_re = h_re * r_re - h_im * r_im
    q_im = h_re * r_im + h_im * r_re
    headv_ref[...] = widen(h_re, h_im).T
    relv_ref[...] = widen(r_re, r_im).T
    query_ref[...] = widen(q_re, q_im).T

    owner = owner_ref[...]
    owned = hot(iota((2 * CHIP_COUNT, TRIP), 0) == owner)
    before = hot(iota((TRIP, TRIP), 0) < iota((TRIP, TRIP), 1))
    rank = jnp.sum(dot(owned, before) * owned.astype(F32), axis=0, keepdims=True)
    place = owner * CAP + rank.astype(I32)
    place_ref[...] = jnp.broadcast_to(place.astype(F32), (128, TRIP)).T.astype(I32)

    marks = hot(iota((SLOTS, TRIP), 0) == place)
    high, low = split(widen(q_re, q_im, tail_ref[...].astype(F32) + 1.0).T)
    sent_ref[...] = dot(marks, high) + dot(marks, low)


def turn_tables(own_ref, ent_ref, hub_ref, relt_ref, hubacc_ref, relacc_ref,
                high_ref, low_ref, mine_ref, held_ref):
    for block in range(ENT // 512):
        part = ent_ref[:, block * 512 : (block + 1) * 512]
        high, low = split(widen(part[:HALF], part[HALF:]).T)
        high_ref[block * 512 : (block + 1) * 512, :] = high
        low_ref[block * 512 : (block + 1) * 512, :] = low
    own = own_ref[0]
    lane = iota((1, 128), 1)

    def rows_of(ref, first, at):
        block = ref[:, pl.ds(pl.multiple_of((first // 128) * 128, 128), 128)]
        return pltpu.roll(block, (at - first % 128 + 128) % 128, 1)

    hub = rows_of(hub_ref, own * HUB_OWN, 0)
    rel = rows_of(relt_ref, own * REL_OWN, HUB_OWN)
    hub_acc = rows_of(hubacc_ref, own * HUB_OWN, 0)
    rel_acc = rows_of(relacc_ref, own * REL_OWN, HUB_OWN)
    is_hub, is_rel = lane < HUB_OWN, (lane >= HUB_OWN) & (lane < HUB_OWN + REL_OWN)
    both = jnp.where(is_hub, hub, jnp.where(is_rel, rel, 0.0))
    acc = jnp.where(is_hub, hub_acc, jnp.where(is_rel, rel_acc, 1.0))
    held_ref[...] = widen(both[:HALF], both[HALF:], acc)
    held_ref[SIDE + HALF : SIDE + HALF + 8, :] = jnp.broadcast_to(acc, (8, 128))
    rows = held_ref[...].T
    rel = rows[HUB_OWN : HUB_OWN + 8]
    rel = jnp.where(iota(rel.shape, 0) < REL_OWN, rel, pltpu.roll(rel, REL_OWN, 0))
    for k, tile in enumerate(pack(rows[:HUB_OWN], rel)):
        mine_ref[k * 8 : (k + 1) * 8, :] = tile


def pack(hub, rel):
    lane, low = iota((hub.shape[0], 128), 1), iota((hub.shape[0], 128), 0) % 8 < REL_OWN
    hubs = [hub[:, k * 128 : (k + 1) * 128] for k in range(4)]
    rels = [rel[:, k * 128 : (k + 1) * 128] for k in range(4)]
    turned = pltpu.roll(hubs[3], 72, 1)
    tail = pltpu.roll(jnp.where(low, rels[1], rels[3]), 16, 1)
    last = jnp.where(lane < 16, turned, jnp.where(lane < 89, tail, pltpu.roll(hubs[1], 17, 1)))
    return (
        hubs[0],
        hubs[2],
        jnp.where(low, rels[0], rels[2]),
        jnp.where(lane < 72, hubs[1], turned),
        jnp.where(lane < 90, last, 0.0),
    )


def answer_queries(asked_ref, high_ref, low_ref, out_ref):
    asked = asked_ref[...]
    row = aux_column(asked).astype(I32) - 1
    marks = hot(iota((asked.shape[0], ENT), 1) == row)
    tails = dot(marks, high_ref[...]) + dot(marks, low_ref[...])
    positive = jnp.sum(asked * tails, axis=1, keepdims=True)
    slope = -jax.nn.sigmoid(-positive)
    out_ref[...] = jnp.where(iota(tails.shape, 1) == AUX, positive, slope * tails)


def score(query_ref, neg_ref, grad_in, loss_in, back_ref, grad_ref, loss_ref):
    qh, ql = split(query_ref[...])
    grad, total = grad_in[...], loss_in[...]
    step = 256
    for first in range(0, neg_ref.shape[0], step):
        nh, nl = split(neg_ref[first : first + step, :])
        nt = ((1,), (1,))
        s = dot(qh, nh, nt) + (dot(qh, nl, nt) + dot(ql, nh, nt))
        small = jnp.exp(-jnp.abs(s))
        loss = jnp.maximum(s, 0.0) + jnp.log1p(small)
        for part in range(step // 128):
            total = total + loss[:, part * 128 : (part + 1) * 128]
        weight = jnp.where(s >= 0.0, 1.0, small) / (1.0 + small) * (1.0 / ENT_NEGS)
        gh, gl = split(weight)
        grad = grad + (dot(gh, nh) + (dot(gh, nl) + dot(gl, nh)))
        tn = ((0,), (0,))
        back_ref[first : first + step, :] = dot(gh, qh, tn) + (dot(gh, ql, tn) + dot(gl, qh, tn))
    grad_ref[...] = grad
    loss_ref[...] = total


ENT_NEGS = 2 * CHIP_COUNT * NEG


def close_triples(core_ref, back_ref, place_ref, headv_ref, relv_ref, gradq_ref, loss_ref,
                  head_ref, rel_ref, gradh_ref, mine_ref, other_ref, out_ref):
    place = place_ref[...]
    lane = iota((TRIP, 128), 1)
    marks = jnp.concatenate(
        [hot(place == lane + part * 128) for part in range(SLOTS // 128)], axis=1
    )
    high, low = split(back_ref[...])
    tail = dot(marks, high) + dot(marks, low)
    positive = aux_column(tail)
    neg_loss = jnp.sum(loss_ref[...], axis=1, keepdims=True) * (1.0 / ENT_NEGS)
    drop = -positive
    loss = jnp.maximum(drop, 0.0) + jnp.log1p(jnp.exp(-jnp.abs(drop))) + neg_loss
    out_ref[...] = jnp.broadcast_to(loss, (TRIP, 128)).T[:1]
    grad = without_aux(tail) + gradq_ref[...]
    g_re, g_im = grad[:, :SIDE], grad[:, SIDE:]
    heads, rels = headv_ref[...], relv_ref[...]
    h_re, h_im, r_re, r_im = heads[:, :SIDE], heads[:, SIDE:], rels[:, :SIDE], rels[:, SIDE:]
    gh = jnp.concatenate([g_re * r_re + g_im * r_im, g_im * r_re - g_re * r_im], axis=1)
    gr = jnp.concatenate([g_re * h_re + g_im * h_im, g_im * h_re - g_re * h_im], axis=1)
    gradh_ref[...] = gh

    core = core_ref[0]
    at = iota((2 * CHIP_COUNT * 8, TRIP), 0)
    head, rel = head_ref[...], rel_ref[...]
    hub_id = (at + core * (HUB // 2)) % HUB
    rel_id = (at // 8 * REL_OWN + at % REL_OWN + core * (REL // 2)) % REL
    sums = []
    for marks, value in ((hot(hub_id == head), gh), (hot(rel_id == rel), gr)):
        high, low = split(value)
        sums.append(dot(marks, high) + dot(marks, low))
    for k, tile in enumerate(pack(*sums)):
        tile = tile.reshape(2, CHIP_COUNT, 8, 128)
        mine_ref[:, k * 8 : (k + 1) * 8, :] = tile[0]
        other_ref[:, k * 8 : (k + 1) * 8, :] = tile[1]


def scatter_entities(head_ref, gradh_ref, asked_ref, answer_ref, out_ref,
                     th_ref, tl_ref, hh_ref, hl_ref, row_ref):
    @pl.when(pl.program_id(0) == 0)
    def _():
        asked = asked_ref[...]
        row_ref[...] = jnp.broadcast_to(aux_column(asked).astype(I32) - 1, (SLOTS, 128))
        slope = -jax.nn.sigmoid(-aux_column(answer_ref[...]))
        high, low = split((without_aux(asked) * slope).T)
        th_ref[...] = high
        tl_ref[...] = low
        high, low = split(gradh_ref[...].T)
        hh_ref[...] = high
        hl_ref[...] = low

    count = out_ref.shape[1]
    first = pl.program_id(0) * count
    rows = row_ref[...]
    lane = iota((SLOTS, 128), 1) + first
    marks = jnp.concatenate([hot(rows == lane + k * 128) for k in range(count // 128)], axis=1)
    grad = dot(th_ref[...], marks) + dot(tl_ref[...], marks)
    marks = hot(iota((count, TRIP), 0) + first == head_ref[...] - HUB)
    nt = ((1,), (1,))
    grad = grad + (dot(hh_ref[...], marks, nt) + dot(hl_ref[...], marks, nt))
    out_ref[:HALF, :] = grad[:HALF]
    out_ref[HALF:, :] = grad[SIDE : SIDE + HALF]


def update_own(sums_ref, mine_ref, out_ref):
    lane = iota((8, 128), 1)
    grads = [jnp.sum(sums_ref[:, k * 8 : (k + 1) * 8, :], axis=0) for k in range(5)]
    mine = [mine_ref[k * 8 : (k + 1) * 8, :] for k in range(5)]

    def across(x):
        return jnp.sum(x, axis=1, keepdims=True)

    in_hub, in_rel = lane < 16, (lane >= 16) & (lane < 88)
    squares = [g * g for g in grads]
    hub = across(squares[0] + squares[1] + squares[3] + jnp.where(in_hub, squares[4], 0.0))
    rel = jnp.broadcast_to(across(squares[2] + jnp.where(in_rel, squares[4], 0.0)), (8, 128))
    rel = rel + pltpu.roll(rel, REL_OWN, 0)
    hub_acc = across(jnp.where(lane == 89, mine[4], 0.0)) + hub / WIDTH
    rel_acc = across(jnp.where(lane == 88, mine[4], 0.0)) + rel / WIDTH
    hub_root, rel_root = jnp.sqrt(hub_acc), jnp.sqrt(rel_acc)
    mixed = jnp.where(in_hub, hub_root, rel_root)
    roots = (hub_root, hub_root, rel_root, hub_root, mixed)
    new = [m - LEARN_RATE * g / root for m, g, root in zip(mine, grads, roots)]
    new[4] = jnp.where(lane == 88, rel_acc, jnp.where(lane == 89, hub_acc, new[4]))
    for k in range(5):
        out_ref[:, k * 8 : (k + 1) * 8, :] = jnp.broadcast_to(new[k][None], (CHIP_COUNT, 8, 128))


def place_new(core_ref, mine_ref, other_ref, hub_ref, hubacc_ref, rel_ref, relacc_ref, held_ref):
    core = core_ref[0]
    for part_ref, side in ((mine_ref, core), (other_ref, 1 - core)):
        def turned(k):
            return part_ref[:, k * 8 : (k + 1) * 8, :].reshape(CHIP_COUNT * 8, 128).T

        at = pl.ds(pl.multiple_of(side * (HUB // 2), 128), HUB // 2)
        hub_ref[0:128, at] = turned(0)
        hub_ref[HALF : HALF + 128, at] = turned(1)
        mixed = turned(3)
        hub_ref[128:HALF, at] = mixed[:72]
        hub_ref[HALF + 128 : HALF + 184, at] = mixed[72:]
        last = turned(4)
        hub_ref[HALF + 184 : WIDTH, at] = last[:16]
        hubacc_ref[:, at] = last[89:90]
        for chip in range(CHIP_COUNT):
            here = slice(chip * REL_OWN, (chip + 1) * REL_OWN)
            held_ref[0, here, :] = part_ref[chip, 16:20, :]
            held_ref[1, here, :] = part_ref[chip, 32:36, :]
            held_ref[2, here, :] = part_ref[chip, 20:24, :]
            held_ref[3, here, :] = part_ref[chip, 36:40, :]
        at = pl.ds(pl.multiple_of(side * (REL // 2), 128), REL // 2)
        for half in range(2):
            rel_ref[half * HALF : half * HALF + 128, at] = held_ref[2 * half].T
            last = held_ref[2 * half + 1].T
            rel_ref[half * HALF + 128 : (half + 1) * HALF, at] = last[16:88]
            if half == 0:
                relacc_ref[:, at] = last[88:89]


def update_entities(rows_ref, neg_ref, ent_ref, acc_ref, grad_ref, new_ref, newacc_ref):
    count = ent_ref.shape[1]
    first = pl.program_id(0) * count
    rows = rows_ref[...][:, :1]
    marks = hot(iota((NEG, count), 1) + first == rows)
    high, low = split(neg_ref[...])
    tn = ((0,), (0,))
    more = dot(high, marks, tn) + dot(low, marks, tn)
    g_re = grad_ref[:HALF, :] + more[:HALF]
    g_im = grad_ref[HALF:, :] + more[SIDE : SIDE + HALF]
    square = jnp.sum(g_re * g_re, axis=0, keepdims=True) + jnp.sum(
        g_im * g_im, axis=0, keepdims=True
    )
    accum = acc_ref[...] + square / WIDTH
    newacc_ref[...] = accum
    root = jnp.sqrt(accum)
    new_ref[:HALF, :] = ent_ref[:HALF, :] - LEARN_RATE * g_re / root
    new_ref[HALF:, :] = ent_ref[HALF:, :] - LEARN_RATE * g_im / root


def around(block, axis):
    count = SIZES[SHARD.index(axis)]
    turns = [[(i, (i + k) % count) for i in range(count)] for k in range(1, count)]
    return [block] + [lax.ppermute(block, axis, turn) for turn in turns]


def add_around(blocks, axis):
    count = SIZES[SHARD.index(axis)]
    turns = [[((i + k) % count, i) for i in range(count)] for k in range(1, count)]
    one, two, three = [lax.ppermute(blocks[k + 1], axis, turn) for k, turn in enumerate(turns)]
    return (blocks[0] + one) + (two + three)


def shape(*dims, dtype=F32):
    return jax.ShapeDtypeStruct(dims, dtype)


def body(
    entity_table,
    entity_accum,
    hub_table,
    hub_accum,
    relation_table,
    relation_accum,
    head_ids,
    relation_ids,
    tail_owner,
    tail_rows,
    negative_rows,
):
    core = lax.axis_index("core").astype(I32)
    chip = lax.axis_index(CHIPS).astype(I32)
    core_arg = core.reshape(1)
    own_arg = (core * CHIP_COUNT + chip).reshape(1)
    ent_t, hub_t, rel_t = entity_table.T, hub_table.T, relation_table.T
    head_row, rel_row = head_ids.reshape(1, TRIP), relation_ids.reshape(1, TRIP)
    owner_row, tail_row = tail_owner.reshape(1, TRIP), tail_rows.reshape(1, TRIP)

    picked = pl.pallas_call(
        pick_negatives,
        out_shape=shape(NEG, WIDE),
        in_specs=[SMEM, VMEM],
        out_specs=VMEM,
        scratch_shapes=[pltpu.VMEM((WIDE, 128), F32)],
        compiler_params=params(),
        name="pick_negatives",
    )(negative_rows, ent_t)
    picked, head_row = lax.optimization_barrier((picked, head_row))
    near = jnp.concatenate(around(picked, "z"), axis=0)

    query, heads, rels, sent, place = pl.pallas_call(
        prepare,
        out_shape=[
            shape(TRIP, WIDE), shape(TRIP, WIDE), shape(TRIP, WIDE), shape(SLOTS, WIDE),
            shape(TRIP, 128, dtype=I32),
        ],
        in_specs=[VMEM] * 7,
        out_specs=[VMEM] * 5,
        compiler_params=params(),
        name="prepare",
    )(head_row, rel_row, owner_row, tail_row, ent_t, hub_t, rel_t)

    def exchange(rows):
        parts = rows.reshape(2 * CHIP_COUNT, CAP, WIDE)
        got = lax.all_to_all(parts, SHARD, split_axis=0, concat_axis=0, tiled=True)
        return got.reshape(SLOTS, WIDE)

    sent, near, own_arg = lax.optimization_barrier((sent, near, own_arg))
    near = lax.all_gather(near, ("x", "y"), axis=0, tiled=True)
    asked = exchange(sent)
    ent_high, ent_low, mine_rows = pl.pallas_call(
        turn_tables,
        out_shape=[
            shape(ENT, WIDE, dtype=BF16), shape(ENT, WIDE, dtype=BF16), shape(OWN, 128)
        ],
        in_specs=[SMEM] + [VMEM] * 5,
        out_specs=[VMEM] * 3,
        scratch_shapes=[pltpu.VMEM((WIDE, 128), F32)],
        compiler_params=params(),
        cost_estimate=cost(1e6, 12e6),
        name="turn_tables",
    )(own_arg, ent_t, hub_t, rel_t, hub_accum.reshape(1, HUB), relation_accum.reshape(1, REL))

    rows = 256
    answer = pl.pallas_call(
        answer_queries,
        out_shape=shape(SLOTS, WIDE),
        grid=(SLOTS // rows,),
        in_specs=[pl.BlockSpec((rows, WIDE), lambda i: (i, 0)), VMEM, VMEM],
        out_specs=pl.BlockSpec((rows, WIDE), lambda i: (i, 0)),
        compiler_params=params(),
        name="answer_queries",
    )(asked, ent_high, ent_low)
    near, answer = lax.optimization_barrier((near, answer))
    far = lax.ppermute(near, "core", SWAP)
    back = exchange(answer)

    def scored(block, grad, loss):
        return pl.pallas_call(
            score,
            out_shape=[shape(*block.shape), shape(TRIP, WIDE), shape(TRIP, 128)],
            in_specs=[VMEM] * 4,
            out_specs=[VMEM] * 3,
            compiler_params=params(),
            cost_estimate=cost(10e9, 8e6),
            name="score",
        )(query, block, grad, loss)

    zeros = jnp.zeros((TRIP, WIDE), F32), jnp.zeros((TRIP, 128), F32)
    far_back, grad_q, loss_sum = scored(far, *zeros)
    far_back = lax.ppermute(far_back, "core", SWAP)
    near_back, grad_q, loss_sum = scored(near, grad_q, loss_sum)
    part, back = lax.optimization_barrier((near_back + far_back, back))
    part = lax.psum_scatter(part, "x", scatter_dimension=0, tiled=True)
    y = lax.axis_index("y").astype(I32)
    blocks = part.reshape(4, 4 * NEG, WIDE)
    blocks = [lax.dynamic_index_in_dim(blocks, (y + 4 - k) & 3, 0, keepdims=False) for k in range(4)]
    part = add_around(blocks, "y")
    neg_grad = add_around(jnp.split(part, 4, axis=0), "z")

    grad_head, both_mine, both_other, loss = pl.pallas_call(
        close_triples,
        out_shape=[
            shape(TRIP, WIDE), shape(CHIP_COUNT, OWN, 128), shape(CHIP_COUNT, OWN, 128),
            shape(1, TRIP),
        ],
        in_specs=[SMEM] + [VMEM] * 8,
        out_specs=[VMEM] * 4,
        compiler_params=params(),
        name="close_triples",
    )(core_arg, back, place, heads, rels, grad_q, loss_sum, head_row, rel_row)
    both_swapped = lax.ppermute(both_other, "core", SWAP)

    paired = both_mine + both_swapped
    paired, asked, answer = lax.optimization_barrier((paired, asked, answer))
    sums = lax.all_to_all(paired, CHIPS, split_axis=0, concat_axis=0, tiled=True)

    columns = 256
    whole = pl.BlockSpec((SLOTS, WIDE), lambda i: (0, 0))
    entity_grad = pl.pallas_call(
        scatter_entities,
        out_shape=shape(WIDTH, ENT),
        grid=(ENT // columns,),
        in_specs=[
            pl.BlockSpec((1, TRIP), lambda i: (0, 0)),
            pl.BlockSpec((TRIP, WIDE), lambda i: (0, 0)),
            whole,
            whole,
        ],
        out_specs=pl.BlockSpec((WIDTH, columns), lambda i: (0, i)),
        scratch_shapes=[
            pltpu.VMEM((WIDE, SLOTS), BF16), pltpu.VMEM((WIDE, SLOTS), BF16),
            pltpu.VMEM((WIDE, TRIP), BF16), pltpu.VMEM((WIDE, TRIP), BF16),
            pltpu.VMEM((SLOTS, 128), I32),
        ],
        compiler_params=params(),
        cost_estimate=cost(10e9, 12e6),
        name="scatter_entities",
    )(head_row, grad_head, asked, answer)

    sums, entity_grad = lax.optimization_barrier((sums, entity_grad))
    own_new = pl.pallas_call(
        update_own,
        out_shape=shape(CHIP_COUNT, OWN, 128),
        in_specs=[VMEM] * 2,
        out_specs=VMEM,
        compiler_params=params(),
        name="update_own",
    )(sums, mine_rows)
    new_mine = lax.all_to_all(own_new, CHIPS, split_axis=0, concat_axis=0, tiled=True)
    columns = 512
    entity_new, entity_accum_new = pl.pallas_call(
        update_entities,
        out_shape=[shape(WIDTH, ENT), shape(1, ENT)],
        grid=(ENT // columns,),
        in_specs=[
            pl.BlockSpec((NEG, 128), lambda i: (0, 0)),
            pl.BlockSpec((NEG, WIDE), lambda i: (0, 0)),
            pl.BlockSpec((WIDTH, columns), lambda i: (0, i)),
            pl.BlockSpec((1, columns), lambda i: (0, i)),
            pl.BlockSpec((WIDTH, columns), lambda i: (0, i)),
        ],
        out_specs=[
            pl.BlockSpec((WIDTH, columns), lambda i: (0, i)),
            pl.BlockSpec((1, columns), lambda i: (0, i)),
        ],
        compiler_params=params(),
        cost_estimate=cost(1e9, 14e6),
        name="update_entities",
    )(
        jnp.broadcast_to(negative_rows[:, None], (NEG, 128)),
        neg_grad,
        ent_t,
        entity_accum.reshape(1, ENT),
        entity_grad,
    )

    new_other = lax.ppermute(new_mine, "core", SWAP)
    new_mine, entity_new = lax.optimization_barrier((new_mine, entity_new))
    hub_new, hub_accum_new, rel_new, rel_accum_new = pl.pallas_call(
        place_new,
        out_shape=[shape(WIDTH, HUB), shape(1, HUB), shape(WIDTH, REL), shape(1, REL)],
        in_specs=[SMEM, VMEM, VMEM],
        out_specs=[VMEM] * 4,
        scratch_shapes=[pltpu.VMEM((4, REL // 2, 128), F32)],
        compiler_params=params(),
        name="place_new",
    )(core_arg, new_mine, new_other)
    return (
        entity_new.T,
        entity_accum_new.reshape(ENT),
        hub_new.T,
        hub_accum_new.reshape(HUB),
        rel_new.T,
        rel_accum_new.reshape(REL),
        loss.reshape(TRIP),
    )


def solution(mesh):
    fine = Mesh(mesh.devices.reshape(SIZES), SHARD)
    rows, vector = P(SHARD, None), P(SHARD)
    placed = (rows, vector, P(), P(), P(), P(), vector, vector, rows, vector, vector)
    return jax.shard_map(
        body,
        mesh=fine,
        in_specs=placed,
        out_specs=(rows, vector, P(), P(), P(), P(), vector),
        check_vma=False,
    )
```

```python
import jax
import jax.numpy as jnp
from jax import lax
from jax.experimental import pallas as pl
from jax.experimental.pallas import tpu as pltpu
from jax.sharding import Mesh, PartitionSpec as P

LEARN_RATE = 0.1
CHIPS = ("z", "x", "y")
SHARD = ("z", "x", "y", "core")
SIZES = (4, 4, 4, 2)
SWAP = [(0, 1), (1, 0)]
F32, BF16, I32 = jnp.float32, jnp.bfloat16, jnp.int32

WIDTH, HALF, SIDE, WIDE, AUX = 400, 200, 256, 512, 200
ENT, HUB, REL, TRIP, CHIP_COUNT, CAP, NEG = 2048, 1024, 512, 512, 64, 8, 16
SLOTS = 2 * CHIP_COUNT * CAP
HUB_OWN, REL_OWN, OWN = 8, 4, 40
VMEM = pl.BlockSpec(memory_space=pltpu.VMEM)
SMEM = pl.BlockSpec(memory_space=pltpu.SMEM)


def params():
    return pltpu.CompilerParams(vmem_limit_bytes=56 << 20)


def cost(flops, nbytes):
    return pl.CostEstimate(flops=int(flops), bytes_accessed=int(nbytes), transcendentals=0)


def split(x):
    high = x.astype(BF16)
    return high, (x - high.astype(F32)).astype(BF16)


def dot(a, b, contract=((1,), (0,))):
    return lax.dot_general(a, b, (contract, ((), ())), preferred_element_type=F32)


def hot(condition):
    return jnp.where(condition, 1.0, 0.0).astype(BF16)


def iota(shape, axis):
    return lax.broadcasted_iota(I32, shape, axis)


def aux_column(rows):
    part = rows[:, 128:SIDE]
    return jnp.sum(jnp.where(iota(part.shape, 1) == AUX - 128, part, 0.0), axis=1, keepdims=True)


def without_aux(rows):
    return jnp.where(iota(rows.shape, 1) == AUX, 0.0, rows)


def widen(re, im, aux=None):
    n = re.shape[1]
    gap = jnp.zeros((SIDE - HALF, n), F32)
    if aux is not None:
        first = jnp.where(iota((8, n), 0) == 0, aux, 0.0)
        middle = jnp.concatenate([first, jnp.zeros((SIDE - HALF - 8, n), F32)], axis=0)
    else:
        middle = gap
    return jnp.concatenate([re, middle, im, gap], axis=0)


def pick_negatives(rows_ref, ent_ref, out_ref, held_ref):
    held_ref[...] = jnp.zeros_like(held_ref)
    lane = iota((WIDTH, 128), 1)
    for j in range(NEG):
        row = rows_ref[j]
        block = ent_ref[:, pl.ds(pl.multiple_of((row // 128) * 128, 128), 128)]
        block = pltpu.roll(block, (j - row % 128 + 128) % 128, 1)
        here = lane == j
        held_ref[0:HALF, :] = jnp.where(here[:HALF], block[:HALF], held_ref[0:HALF, :])
        held_ref[SIDE : SIDE + HALF, :] = jnp.where(
            here[:HALF], block[HALF:], held_ref[SIDE : SIDE + HALF, :]
        )
    out_ref[...] = held_ref[...].T[:NEG]


def prepare(head_ref, rel_ref, owner_ref, tail_ref, ent_ref, hub_ref, relt_ref,
            query_ref, headv_ref, relv_ref, sent_ref, place_ref):
    head = head_ref[...]

    def gather(table, ids):
        marks = hot(iota((table.shape[1], TRIP), 0) == ids)
        high, low = split(table)
        return dot(high, marks) + dot(low, marks)

    heads = gather(hub_ref[...], head) + gather(ent_ref[...], head - HUB)
    rels = gather(relt_ref[...], rel_ref[...])
    h_re, h_im, r_re, r_im = heads[:HALF], heads[HALF:], rels[:HALF], rels[HALF:]
    q_re = h_re * r_re - h_im * r_im
    q_im = h_re * r_im + h_im * r_re
    headv_ref[...] = widen(h_re, h_im).T
    relv_ref[...] = widen(r_re, r_im).T
    query_ref[...] = widen(q_re, q_im).T

    owner = owner_ref[...]
    owned = hot(iota((2 * CHIP_COUNT, TRIP), 0) == owner)
    before = hot(iota((TRIP, TRIP), 0) < iota((TRIP, TRIP), 1))
    rank = jnp.sum(dot(owned, before) * owned.astype(F32), axis=0, keepdims=True)
    place = owner * CAP + rank.astype(I32)
    place_ref[...] = jnp.broadcast_to(place.astype(F32), (128, TRIP)).T.astype(I32)

    marks = hot(iota((SLOTS, TRIP), 0) == place)
    high, low = split(widen(q_re, q_im, tail_ref[...].astype(F32) + 1.0).T)
    sent_ref[...] = dot(marks, high) + dot(marks, low)


def turn_tables(own_ref, ent_ref, hub_ref, relt_ref, hubacc_ref, relacc_ref,
                high_ref, low_ref, mine_ref, held_ref):
    for block in range(ENT // 512):
        part = ent_ref[:, block * 512 : (block + 1) * 512]
        high, low = split(widen(part[:HALF], part[HALF:]).T)
        high_ref[block * 512 : (block + 1) * 512, :] = high
        low_ref[block * 512 : (block + 1) * 512, :] = low
    own = own_ref[0]
    lane = iota((1, 128), 1)

    def rows_of(ref, first, at):
        block = ref[:, pl.ds(pl.multiple_of((first // 128) * 128, 128), 128)]
        return pltpu.roll(block, (at - first % 128 + 128) % 128, 1)

    hub = rows_of(hub_ref, own * HUB_OWN, 0)
    rel = rows_of(relt_ref, own * REL_OWN, HUB_OWN)
    hub_acc = rows_of(hubacc_ref, own * HUB_OWN, 0)
    rel_acc = rows_of(relacc_ref, own * REL_OWN, HUB_OWN)
    is_hub, is_rel = lane < HUB_OWN, (lane >= HUB_OWN) & (lane < HUB_OWN + REL_OWN)
    both = jnp.where(is_hub, hub, jnp.where(is_rel, rel, 0.0))
    acc = jnp.where(is_hub, hub_acc, jnp.where(is_rel, rel_acc, 1.0))
    held_ref[...] = widen(both[:HALF], both[HALF:], acc)
    held_ref[SIDE + HALF : SIDE + HALF + 8, :] = jnp.broadcast_to(acc, (8, 128))
    rows = held_ref[...].T
    rel = rows[HUB_OWN : HUB_OWN + 8]
    rel = jnp.where(iota(rel.shape, 0) < REL_OWN, rel, pltpu.roll(rel, REL_OWN, 0))
    for k, tile in enumerate(pack(rows[:HUB_OWN], rel)):
        mine_ref[k * 8 : (k + 1) * 8, :] = tile


def pack(hub, rel):
    lane, low = iota((hub.shape[0], 128), 1), iota((hub.shape[0], 128), 0) % 8 < REL_OWN
    hubs = [hub[:, k * 128 : (k + 1) * 128] for k in range(4)]
    rels = [rel[:, k * 128 : (k + 1) * 128] for k in range(4)]
    turned = pltpu.roll(hubs[3], 72, 1)
    tail = pltpu.roll(jnp.where(low, rels[1], rels[3]), 16, 1)
    last = jnp.where(lane < 16, turned, jnp.where(lane < 89, tail, pltpu.roll(hubs[1], 17, 1)))
    return (
        hubs[0],
        hubs[2],
        jnp.where(low, rels[0], rels[2]),
        jnp.where(lane < 72, hubs[1], turned),
        jnp.where(lane < 90, last, 0.0),
    )


def answer_queries(asked_ref, high_ref, low_ref, out_ref):
    asked = asked_ref[...]
    row = aux_column(asked).astype(I32) - 1
    marks = hot(iota((asked.shape[0], ENT), 1) == row)
    tails = dot(marks, high_ref[...]) + dot(marks, low_ref[...])
    positive = jnp.sum(asked * tails, axis=1, keepdims=True)
    slope = -jax.nn.sigmoid(-positive)
    out_ref[...] = jnp.where(iota(tails.shape, 1) == AUX, positive, slope * tails)


def log_one_plus(x):
    series = x * (1.0 - x * (0.5 - x * (1.0 / 3.0)))
    return jnp.where(x < 1e-3, series, jnp.log(1.0 + x))


def score(core_ref, query_ref, neg_ref, near_ref, far_ref, grad_ref, loss_ref, qh_ref, ql_ref):
    side = pl.program_id(0)

    @pl.when((side == 0) & (pl.program_id(1) == 0))
    def _():
        high, low = split(query_ref[...])
        qh_ref[...] = high
        ql_ref[...] = low
        grad_ref[...] = jnp.zeros_like(grad_ref)
        loss_ref[...] = jnp.zeros_like(loss_ref)

    qh, ql = qh_ref[...], ql_ref[...]
    grad, total = grad_ref[...], loss_ref[...]
    negs = neg_ref[...].reshape(-1, WIDE)
    step = 256
    backs = []
    for first in range(0, negs.shape[0], step):
        nh, nl = split(negs[first : first + step, :])
        nt = ((1,), (1,))
        s = dot(qh, nh, nt) + (dot(qh, nl, nt) + dot(ql, nh, nt))
        small = jnp.exp(-jnp.abs(s))
        loss = jnp.maximum(s, 0.0) + log_one_plus(small)
        for part in range(step // 128):
            total = total + loss[:, part * 128 : (part + 1) * 128]
        whole = 1.0 + small
        turn = pl.reciprocal(whole, approx=True)
        turn = turn * (2.0 - whole * turn)
        weight = jnp.where(s >= 0.0, turn, small * turn)
        gh, gl = split(weight)
        grad = grad + (dot(gh, nh) + (dot(gh, nl) + dot(gl, nh)))
        tn = ((0,), (0,))
        back = dot(gh, qh, tn) + (dot(gh, ql, tn) + dot(gl, qh, tn))
        backs.append(back * (1.0 / ENT_NEGS))
    grad_ref[...] = grad
    loss_ref[...] = total
    back = jnp.concatenate(backs, axis=0).reshape(near_ref.shape)

    @pl.when(side == 0)
    def _():
        near_ref[...] = back

    @pl.when(side == 1)
    def _():
        far_ref[...] = back


ENT_NEGS = 2 * CHIP_COUNT * NEG


def close_triples(core_ref, back_ref, place_ref, headv_ref, relv_ref, gradq_ref, loss_ref,
                  head_ref, rel_ref, gradh_ref, mine_ref, other_ref, out_ref):
    place = place_ref[...]
    lane = iota((TRIP, 128), 1)
    marks = jnp.concatenate(
        [hot(place == lane + part * 128) for part in range(SLOTS // 128)], axis=1
    )
    high, low = split(back_ref[...])
    tail = dot(marks, high) + dot(marks, low)
    positive = aux_column(tail)
    neg_loss = jnp.sum(loss_ref[...], axis=1, keepdims=True) * (1.0 / ENT_NEGS)
    drop = -positive
    loss = jnp.maximum(drop, 0.0) + jnp.log1p(jnp.exp(-jnp.abs(drop))) + neg_loss
    out_ref[...] = jnp.broadcast_to(loss, (TRIP, 128)).T[:1]
    grad = without_aux(tail) + gradq_ref[...] * (1.0 / ENT_NEGS)
    g_re, g_im = grad[:, :SIDE], grad[:, SIDE:]
    heads, rels = headv_ref[...], relv_ref[...]
    h_re, h_im, r_re, r_im = heads[:, :SIDE], heads[:, SIDE:], rels[:, :SIDE], rels[:, SIDE:]
    gh = jnp.concatenate([g_re * r_re + g_im * r_im, g_im * r_re - g_re * r_im], axis=1)
    gr = jnp.concatenate([g_re * h_re + g_im * h_im, g_im * h_re - g_re * h_im], axis=1)
    gradh_ref[...] = gh

    core = core_ref[0]
    at = iota((2 * CHIP_COUNT * 8, TRIP), 0)
    head, rel = head_ref[...], rel_ref[...]
    hub_id = (at + core * (HUB // 2)) % HUB
    rel_id = (at // 8 * REL_OWN + at % REL_OWN + core * (REL // 2)) % REL
    sums = []
    for marks, value in ((hot(hub_id == head), gh), (hot(rel_id == rel), gr)):
        high, low = split(value)
        sums.append(dot(marks, high) + dot(marks, low))
    for k, tile in enumerate(pack(*sums)):
        tile = tile.reshape(2, CHIP_COUNT, 8, 128)
        mine_ref[:, k * 8 : (k + 1) * 8, :] = tile[0]
        other_ref[:, k * 8 : (k + 1) * 8, :] = tile[1]


def scatter_entities(head_ref, gradh_ref, asked_ref, answer_ref, out_ref,
                     th_ref, tl_ref, hh_ref, hl_ref, row_ref):
    @pl.when(pl.program_id(0) == 0)
    def _():
        asked = asked_ref[...]
        row_ref[...] = jnp.broadcast_to(aux_column(asked).astype(I32) - 1, (SLOTS, 128))
        slope = -jax.nn.sigmoid(-aux_column(answer_ref[...]))
        high, low = split((without_aux(asked) * slope).T)
        th_ref[...] = high
        tl_ref[...] = low
        high, low = split(gradh_ref[...].T)
        hh_ref[...] = high
        hl_ref[...] = low

    count = out_ref.shape[1]
    first = pl.program_id(0) * count
    rows = row_ref[...]
    lane = iota((SLOTS, 128), 1) + first
    marks = jnp.concatenate([hot(rows == lane + k * 128) for k in range(count // 128)], axis=1)
    grad = dot(th_ref[...], marks) + dot(tl_ref[...], marks)
    marks = hot(iota((count, TRIP), 0) + first == head_ref[...] - HUB)
    nt = ((1,), (1,))
    grad = grad + (dot(hh_ref[...], marks, nt) + dot(hl_ref[...], marks, nt))
    out_ref[:HALF, :] = grad[:HALF]
    out_ref[HALF:, :] = grad[SIDE : SIDE + HALF]


def update_own(sums_ref, mine_ref, out_ref):
    lane = iota((8, 128), 1)
    grads = [jnp.sum(sums_ref[:, k * 8 : (k + 1) * 8, :], axis=0) for k in range(5)]
    mine = [mine_ref[k * 8 : (k + 1) * 8, :] for k in range(5)]

    def across(x):
        return jnp.sum(x, axis=1, keepdims=True)

    in_hub, in_rel = lane < 16, (lane >= 16) & (lane < 88)
    squares = [g * g for g in grads]
    hub = across(squares[0] + squares[1] + squares[3] + jnp.where(in_hub, squares[4], 0.0))
    rel = jnp.broadcast_to(across(squares[2] + jnp.where(in_rel, squares[4], 0.0)), (8, 128))
    rel = rel + pltpu.roll(rel, REL_OWN, 0)
    hub_acc = across(jnp.where(lane == 89, mine[4], 0.0)) + hub / WIDTH
    rel_acc = across(jnp.where(lane == 88, mine[4], 0.0)) + rel / WIDTH
    hub_root, rel_root = jnp.sqrt(hub_acc), jnp.sqrt(rel_acc)
    mixed = jnp.where(in_hub, hub_root, rel_root)
    roots = (hub_root, hub_root, rel_root, hub_root, mixed)
    new = [m - LEARN_RATE * g / root for m, g, root in zip(mine, grads, roots)]
    new[4] = jnp.where(lane == 88, rel_acc, jnp.where(lane == 89, hub_acc, new[4]))
    for k in range(5):
        out_ref[:, k * 8 : (k + 1) * 8, :] = jnp.broadcast_to(new[k][None], (CHIP_COUNT, 8, 128))


def place_new(core_ref, mine_ref, other_ref, hub_ref, hubacc_ref, rel_ref, relacc_ref, held_ref):
    core = core_ref[0]
    for part_ref, side in ((mine_ref, core), (other_ref, 1 - core)):
        def turned(k):
            return part_ref[:, k * 8 : (k + 1) * 8, :].reshape(CHIP_COUNT * 8, 128).T

        at = pl.ds(pl.multiple_of(side * (HUB // 2), 128), HUB // 2)
        hub_ref[0:128, at] = turned(0)
        hub_ref[HALF : HALF + 128, at] = turned(1)
        mixed = turned(3)
        hub_ref[128:HALF, at] = mixed[:72]
        hub_ref[HALF + 128 : HALF + 184, at] = mixed[72:]
        last = turned(4)
        hub_ref[HALF + 184 : WIDTH, at] = last[:16]
        hubacc_ref[:, at] = last[89:90]
        for chip in range(CHIP_COUNT):
            here = slice(chip * REL_OWN, (chip + 1) * REL_OWN)
            held_ref[0, here, :] = part_ref[chip, 16:20, :]
            held_ref[1, here, :] = part_ref[chip, 32:36, :]
            held_ref[2, here, :] = part_ref[chip, 20:24, :]
            held_ref[3, here, :] = part_ref[chip, 36:40, :]
        at = pl.ds(pl.multiple_of(side * (REL // 2), 128), REL // 2)
        for half in range(2):
            rel_ref[half * HALF : half * HALF + 128, at] = held_ref[2 * half].T
            last = held_ref[2 * half + 1].T
            rel_ref[half * HALF + 128 : (half + 1) * HALF, at] = last[16:88]
            if half == 0:
                relacc_ref[:, at] = last[88:89]


def update_entities(rows_ref, neg_ref, ent_ref, acc_ref, grad_ref, new_ref, newacc_ref):
    count = ent_ref.shape[1]
    first = pl.program_id(0) * count
    rows = rows_ref[...][:, :1]
    marks = hot(iota((NEG, count), 1) + first == rows)
    high, low = split(neg_ref[...])
    tn = ((0,), (0,))
    more = dot(high, marks, tn) + dot(low, marks, tn)
    g_re = grad_ref[:HALF, :] + more[:HALF]
    g_im = grad_ref[HALF:, :] + more[SIDE : SIDE + HALF]
    square = jnp.sum(g_re * g_re, axis=0, keepdims=True) + jnp.sum(
        g_im * g_im, axis=0, keepdims=True
    )
    accum = acc_ref[...] + square / WIDTH
    newacc_ref[...] = accum
    root = jnp.sqrt(accum)
    new_ref[:HALF, :] = ent_ref[:HALF, :] - LEARN_RATE * g_re / root
    new_ref[HALF:, :] = ent_ref[HALF:, :] - LEARN_RATE * g_im / root


def around(block, axis):
    count = SIZES[SHARD.index(axis)]
    turns = [[(i, (i + k) % count) for i in range(count)] for k in range(1, count)]
    return [block] + [lax.ppermute(block, axis, turn) for turn in turns]


def add_around(blocks, axis):
    count = SIZES[SHARD.index(axis)]
    turns = [[((i + k) % count, i) for i in range(count)] for k in range(1, count)]
    one, two, three = [lax.ppermute(blocks[k + 1], axis, turn) for k, turn in enumerate(turns)]
    return (blocks[0] + one) + (two + three)


def shape(*dims, dtype=F32):
    return jax.ShapeDtypeStruct(dims, dtype)


def body(
    entity_table,
    entity_accum,
    hub_table,
    hub_accum,
    relation_table,
    relation_accum,
    head_ids,
    relation_ids,
    tail_owner,
    tail_rows,
    negative_rows,
):
    core = lax.axis_index("core").astype(I32)
    chip = lax.axis_index(CHIPS).astype(I32)
    core_arg = core.reshape(1)
    own_arg = (core * CHIP_COUNT + chip).reshape(1)
    ent_t, hub_t, rel_t = entity_table.T, hub_table.T, relation_table.T
    head_row, rel_row = head_ids.reshape(1, TRIP), relation_ids.reshape(1, TRIP)
    owner_row, tail_row = tail_owner.reshape(1, TRIP), tail_rows.reshape(1, TRIP)

    picked = pl.pallas_call(
        pick_negatives,
        out_shape=shape(NEG, WIDE),
        in_specs=[SMEM, VMEM],
        out_specs=VMEM,
        scratch_shapes=[pltpu.VMEM((WIDE, 128), F32)],
        compiler_params=params(),
        name="pick_negatives",
    )(negative_rows, ent_t)
    picked, head_row = lax.optimization_barrier((picked, head_row))
    near = jnp.concatenate(around(picked, "z"), axis=0)

    query, heads, rels, sent, place = pl.pallas_call(
        prepare,
        out_shape=[
            shape(TRIP, WIDE), shape(TRIP, WIDE), shape(TRIP, WIDE), shape(SLOTS, WIDE),
            shape(TRIP, 128, dtype=I32),
        ],
        in_specs=[VMEM] * 7,
        out_specs=[VMEM] * 5,
        compiler_params=params(),
        name="prepare",
    )(head_row, rel_row, owner_row, tail_row, ent_t, hub_t, rel_t)

    def exchange(rows):
        parts = rows.reshape(2 * CHIP_COUNT, CAP, WIDE)
        got = lax.all_to_all(parts, SHARD, split_axis=0, concat_axis=0, tiled=True)
        return got.reshape(SLOTS, WIDE)

    sent, near, own_arg = lax.optimization_barrier((sent, near, own_arg))
    near = lax.all_gather(near, ("x", "y", "core"), axis=0, tiled=True)
    asked = exchange(sent)
    ent_high, ent_low, mine_rows = pl.pallas_call(
        turn_tables,
        out_shape=[
            shape(ENT, WIDE, dtype=BF16), shape(ENT, WIDE, dtype=BF16), shape(OWN, 128)
        ],
        in_specs=[SMEM] + [VMEM] * 5,
        out_specs=[VMEM] * 3,
        scratch_shapes=[pltpu.VMEM((WIDE, 128), F32)],
        compiler_params=params(),
        cost_estimate=cost(1e6, 1e5),
        name="turn_tables",
    )(own_arg, ent_t, hub_t, rel_t, hub_accum.reshape(1, HUB), relation_accum.reshape(1, REL))

    rows = 256
    answer = pl.pallas_call(
        answer_queries,
        out_shape=shape(SLOTS, WIDE),
        grid=(SLOTS // rows,),
        in_specs=[pl.BlockSpec((rows, WIDE), lambda i: (i, 0)), VMEM, VMEM],
        out_specs=pl.BlockSpec((rows, WIDE), lambda i: (i, 0)),
        compiler_params=params(),
        name="answer_queries",
    )(asked, ent_high, ent_low)
    near, _ = lax.optimization_barrier((near, answer))
    back = exchange(answer)

    group, steps, places = 8, 2, 16
    near_back, far_back, grad_q, loss_sum = pl.pallas_call(
        score,
        out_shape=[
            shape(places, 4 * NEG, WIDE), shape(places, 4 * NEG, WIDE), shape(TRIP, WIDE),
            shape(TRIP, 128),
        ],
        grid_spec=pltpu.PrefetchScalarGridSpec(
            num_scalar_prefetch=1,
            grid=(2, steps),
            in_specs=[
                pl.BlockSpec((TRIP, WIDE), lambda i, c, core: (0, 0)),
                pl.BlockSpec(
                    (group, 1, 4 * NEG, WIDE), lambda i, c, core: (c, (i + core[0]) % 2, 0, 0)
                ),
            ],
            out_specs=[
                pl.BlockSpec(
                    (group, 4 * NEG, WIDE),
                    lambda i, c, core: (jnp.where(i == 0, c, steps - 1), 0, 0),
                ),
                pl.BlockSpec(
                    (group, 4 * NEG, WIDE), lambda i, c, core: (jnp.where(i == 0, 0, c), 0, 0)
                ),
                pl.BlockSpec((TRIP, WIDE), lambda i, c, core: (0, 0)),
                pl.BlockSpec((TRIP, 128), lambda i, c, core: (0, 0)),
            ],
            scratch_shapes=[pltpu.VMEM((TRIP, WIDE), BF16), pltpu.VMEM((TRIP, WIDE), BF16)],
        ),
        compiler_params=params(),
        cost_estimate=cost(20e9, 12e6),
        name="score",
    )(core_arg, query, near.reshape(places, 2, 4 * NEG, WIDE))
    near_back, far_back = near_back.reshape(-1, WIDE), far_back.reshape(-1, WIDE)

    far_back, back = lax.optimization_barrier((far_back, back))
    far_back = lax.ppermute(far_back, "core", SWAP)
    grad_head, both_mine, both_other, loss = pl.pallas_call(
        close_triples,
        out_shape=[
            shape(TRIP, WIDE), shape(CHIP_COUNT, OWN, 128), shape(CHIP_COUNT, OWN, 128),
            shape(1, TRIP),
        ],
        in_specs=[SMEM] + [VMEM] * 8,
        out_specs=[VMEM] * 4,
        compiler_params=params(),
        name="close_triples",
    )(core_arg, back, place, heads, rels, grad_q, loss_sum, head_row, rel_row)
    both_swapped = lax.ppermute(both_other, "core", SWAP)

    near_back, _ = lax.optimization_barrier((near_back, both_other))
    part = near_back + far_back
    part, both_mine = lax.optimization_barrier((part, both_mine))
    part = lax.psum_scatter(part, "x", scatter_dimension=0, tiled=True)
    y = lax.axis_index("y").astype(I32)
    blocks = part.reshape(4, 4 * NEG, WIDE)
    blocks = [lax.dynamic_index_in_dim(blocks, (y + 4 - k) & 3, 0, keepdims=False) for k in range(4)]
    part = add_around(blocks, "y")
    neg_grad = add_around(jnp.split(part, 4, axis=0), "z")

    paired = both_mine + both_swapped
    paired, asked, answer = lax.optimization_barrier((paired, asked, answer))
    sums = lax.all_to_all(paired, CHIPS, split_axis=0, concat_axis=0, tiled=True)

    columns = 256
    whole = pl.BlockSpec((SLOTS, WIDE), lambda i: (0, 0))
    entity_grad = pl.pallas_call(
        scatter_entities,
        out_shape=shape(WIDTH, ENT),
        grid=(ENT // columns,),
        in_specs=[
            pl.BlockSpec((1, TRIP), lambda i: (0, 0)),
            pl.BlockSpec((TRIP, WIDE), lambda i: (0, 0)),
            whole,
            whole,
        ],
        out_specs=pl.BlockSpec((WIDTH, columns), lambda i: (0, i)),
        scratch_shapes=[
            pltpu.VMEM((WIDE, SLOTS), BF16), pltpu.VMEM((WIDE, SLOTS), BF16),
            pltpu.VMEM((WIDE, TRIP), BF16), pltpu.VMEM((WIDE, TRIP), BF16),
            pltpu.VMEM((SLOTS, 128), I32),
        ],
        compiler_params=params(),
        cost_estimate=cost(1e6, 1e5),
        name="scatter_entities",
    )(head_row, grad_head, asked, answer)

    sums, entity_grad = lax.optimization_barrier((sums, entity_grad))
    own_new = pl.pallas_call(
        update_own,
        out_shape=shape(CHIP_COUNT, OWN, 128),
        in_specs=[VMEM] * 2,
        out_specs=VMEM,
        compiler_params=params(),
        name="update_own",
    )(sums, mine_rows)
    new_mine = lax.all_to_all(own_new, CHIPS, split_axis=0, concat_axis=0, tiled=True)
    columns = 512
    entity_new, entity_accum_new = pl.pallas_call(
        update_entities,
        out_shape=[shape(WIDTH, ENT), shape(1, ENT)],
        grid=(ENT // columns,),
        in_specs=[
            pl.BlockSpec((NEG, 128), lambda i: (0, 0)),
            pl.BlockSpec((NEG, WIDE), lambda i: (0, 0)),
            pl.BlockSpec((WIDTH, columns), lambda i: (0, i)),
            pl.BlockSpec((1, columns), lambda i: (0, i)),
            pl.BlockSpec((WIDTH, columns), lambda i: (0, i)),
        ],
        out_specs=[
            pl.BlockSpec((WIDTH, columns), lambda i: (0, i)),
            pl.BlockSpec((1, columns), lambda i: (0, i)),
        ],
        compiler_params=params(),
        cost_estimate=cost(1e6, 1e5),
        name="update_entities",
    )(
        jnp.broadcast_to(negative_rows[:, None], (NEG, 128)),
        neg_grad,
        ent_t,
        entity_accum.reshape(1, ENT),
        entity_grad,
    )

    new_mine, entity_new = lax.optimization_barrier((new_mine, entity_new))
    new_other = lax.ppermute(new_mine, "core", SWAP)
    hub_new, hub_accum_new, rel_new, rel_accum_new = pl.pallas_call(
        place_new,
        out_shape=[shape(WIDTH, HUB), shape(1, HUB), shape(WIDTH, REL), shape(1, REL)],
        in_specs=[SMEM, VMEM, VMEM],
        out_specs=[VMEM] * 4,
        scratch_shapes=[pltpu.VMEM((4, REL // 2, 128), F32)],
        compiler_params=params(),
        name="place_new",
    )(core_arg, new_mine, new_other)
    return (
        entity_new.T,
        entity_accum_new.reshape(ENT),
        hub_new.T,
        hub_accum_new.reshape(HUB),
        rel_new.T,
        rel_accum_new.reshape(REL),
        loss.reshape(TRIP),
    )


def solution(mesh):
    fine = Mesh(mesh.devices.reshape(SIZES), SHARD)
    rows, vector = P(SHARD, None), P(SHARD)
    placed = (rows, vector, P(), P(), P(), P(), vector, vector, rows, vector, vector)
    return jax.shard_map(
        body,
        mesh=fine,
        in_specs=placed,
        out_specs=(rows, vector, P(), P(), P(), P(), vector),
        check_vma=False,
    )
```

```python
import jax
import jax.numpy as jnp
from jax import lax
from jax.experimental import pallas as pl
from jax.experimental.pallas import tpu as pltpu
from jax.sharding import Mesh, PartitionSpec as P

LEARN_RATE = 0.1
CHIPS = ("z", "x", "y")
SHARD = ("z", "x", "y", "core")
SIZES = (4, 4, 4, 2)
SWAP = [(0, 1), (1, 0)]
F32, BF16, I32 = jnp.float32, jnp.bfloat16, jnp.int32

WIDTH, HALF, SIDE, WIDE, AUX = 400, 200, 256, 512, 200
ENT, HUB, REL, TRIP, CHIP_COUNT, CAP, NEG = 2048, 1024, 512, 512, 64, 8, 16
SLOTS = 2 * CHIP_COUNT * CAP
HUB_OWN, REL_OWN, OWN = 8, 4, 40
VMEM = pl.BlockSpec(memory_space=pltpu.VMEM)
SMEM = pl.BlockSpec(memory_space=pltpu.SMEM)


def params():
    return pltpu.CompilerParams(vmem_limit_bytes=56 << 20)


def cost(flops, nbytes):
    return pl.CostEstimate(flops=int(flops), bytes_accessed=int(nbytes), transcendentals=0)


def split(x):
    high = x.astype(BF16)
    return high, (x - high.astype(F32)).astype(BF16)


def dot(a, b, contract=((1,), (0,))):
    return lax.dot_general(a, b, (contract, ((), ())), preferred_element_type=F32)


def hot(condition):
    return jnp.where(condition, 1.0, 0.0).astype(BF16)


def iota(shape, axis):
    return lax.broadcasted_iota(I32, shape, axis)


def aux_column(rows):
    part = rows[:, 128:SIDE]
    return jnp.sum(jnp.where(iota(part.shape, 1) == AUX - 128, part, 0.0), axis=1, keepdims=True)


def without_aux(rows):
    return jnp.where(iota(rows.shape, 1) == AUX, 0.0, rows)


def widen(re, im, aux=None):
    n = re.shape[1]
    gap = jnp.zeros((SIDE - HALF, n), F32)
    if aux is not None:
        first = jnp.where(iota((8, n), 0) == 0, aux, 0.0)
        middle = jnp.concatenate([first, jnp.zeros((SIDE - HALF - 8, n), F32)], axis=0)
    else:
        middle = gap
    return jnp.concatenate([re, middle, im, gap], axis=0)


def pick_negatives(rows_ref, ent_ref, out_ref, held_ref):
    held_ref[...] = jnp.zeros_like(held_ref)
    lane = iota((WIDTH, 128), 1)
    for j in range(NEG):
        row = rows_ref[j]
        block = ent_ref[:, pl.ds(pl.multiple_of((row // 128) * 128, 128), 128)]
        block = pltpu.roll(block, (j - row % 128 + 128) % 128, 1)
        here = lane == j
        held_ref[0:HALF, :] = jnp.where(here[:HALF], block[:HALF], held_ref[0:HALF, :])
        held_ref[SIDE : SIDE + HALF, :] = jnp.where(
            here[:HALF], block[HALF:], held_ref[SIDE : SIDE + HALF, :]
        )
    out_ref[...] = held_ref[...].T[:NEG]


def prepare(head_ref, rel_ref, owner_ref, tail_ref, ent_ref, hub_ref, relt_ref,
            query_ref, headv_ref, relv_ref, sent_ref, place_ref):
    head = head_ref[...]

    def gather(table, ids):
        marks = hot(iota((table.shape[1], TRIP), 0) == ids)
        high, low = split(table)
        return dot(high, marks) + dot(low, marks)

    heads = gather(hub_ref[...], head) + gather(ent_ref[...], head - HUB)
    rels = gather(relt_ref[...], rel_ref[...])
    h_re, h_im, r_re, r_im = heads[:HALF], heads[HALF:], rels[:HALF], rels[HALF:]
    q_re = h_re * r_re - h_im * r_im
    q_im = h_re * r_im + h_im * r_re
    headv_ref[...] = widen(h_re, h_im).T
    relv_ref[...] = widen(r_re, r_im).T
    query_ref[...] = widen(q_re, q_im).T

    owner = owner_ref[...]
    owned = hot(iota((2 * CHIP_COUNT, TRIP), 0) == owner)
    before = hot(iota((TRIP, TRIP), 0) < iota((TRIP, TRIP), 1))
    rank = jnp.sum(dot(owned, before) * owned.astype(F32), axis=0, keepdims=True)
    place = owner * CAP + rank.astype(I32)
    place_ref[...] = jnp.broadcast_to(place.astype(F32), (128, TRIP)).T.astype(I32)

    marks = hot(iota((SLOTS, TRIP), 0) == place)
    high, low = split(widen(q_re, q_im, tail_ref[...].astype(F32) + 1.0).T)
    sent_ref[...] = dot(marks, high) + dot(marks, low)


def turn_tables(own_ref, ent_ref, hub_ref, relt_ref, hubacc_ref, relacc_ref,
                high_ref, low_ref, mine_ref, held_ref):
    for block in range(ENT // 512):
        part = ent_ref[:, block * 512 : (block + 1) * 512]
        high, low = split(widen(part[:HALF], part[HALF:]).T)
        high_ref[block * 512 : (block + 1) * 512, :] = high
        low_ref[block * 512 : (block + 1) * 512, :] = low
    own = own_ref[0]
    lane = iota((1, 128), 1)

    def rows_of(ref, first, at):
        block = ref[:, pl.ds(pl.multiple_of((first // 128) * 128, 128), 128)]
        return pltpu.roll(block, (at - first % 128 + 128) % 128, 1)

    hub = rows_of(hub_ref, own * HUB_OWN, 0)
    rel = rows_of(relt_ref, own * REL_OWN, HUB_OWN)
    hub_acc = rows_of(hubacc_ref, own * HUB_OWN, 0)
    rel_acc = rows_of(relacc_ref, own * REL_OWN, HUB_OWN)
    is_hub, is_rel = lane < HUB_OWN, (lane >= HUB_OWN) & (lane < HUB_OWN + REL_OWN)
    both = jnp.where(is_hub, hub, jnp.where(is_rel, rel, 0.0))
    acc = jnp.where(is_hub, hub_acc, jnp.where(is_rel, rel_acc, 1.0))
    held_ref[...] = widen(both[:HALF], both[HALF:], acc)
    held_ref[SIDE + HALF : SIDE + HALF + 8, :] = jnp.broadcast_to(acc, (8, 128))
    rows = held_ref[...].T
    rel = rows[HUB_OWN : HUB_OWN + 8]
    rel = jnp.where(iota(rel.shape, 0) < REL_OWN, rel, pltpu.roll(rel, REL_OWN, 0))
    for k, tile in enumerate(pack(rows[:HUB_OWN], rel)):
        mine_ref[k * 8 : (k + 1) * 8, :] = tile


def pack(hub, rel):
    lane, low = iota((hub.shape[0], 128), 1), iota((hub.shape[0], 128), 0) % 8 < REL_OWN
    hubs = [hub[:, k * 128 : (k + 1) * 128] for k in range(4)]
    rels = [rel[:, k * 128 : (k + 1) * 128] for k in range(4)]
    turned = pltpu.roll(hubs[3], 72, 1)
    tail = pltpu.roll(jnp.where(low, rels[1], rels[3]), 16, 1)
    last = jnp.where(lane < 16, turned, jnp.where(lane < 89, tail, pltpu.roll(hubs[1], 17, 1)))
    return (
        hubs[0],
        hubs[2],
        jnp.where(low, rels[0], rels[2]),
        jnp.where(lane < 72, hubs[1], turned),
        jnp.where(lane < 90, last, 0.0),
    )


def answer_queries(asked_ref, high_ref, low_ref, out_ref):
    asked = asked_ref[...]
    row = aux_column(asked).astype(I32) - 1
    marks = hot(iota((asked.shape[0], ENT), 1) == row)
    tails = dot(marks, high_ref[...]) + dot(marks, low_ref[...])
    positive = jnp.sum(asked * tails, axis=1, keepdims=True)
    slope = -jax.nn.sigmoid(-positive)
    out_ref[...] = jnp.where(iota(tails.shape, 1) == AUX, positive, slope * tails)


def log_one_plus(x):
    series = x * (1.0 - x * (0.5 - x * (1.0 / 3.0)))
    return jnp.where(x < 1e-3, series, jnp.log(1.0 + x))


def score(at_ref, query_ref, neg_ref, near_ref, far_ref, grad_ref, loss_ref, qh_ref, ql_ref):
    side = pl.program_id(0)

    @pl.when((side == 0) & (pl.program_id(1) == 0))
    def _():
        high, low = split(query_ref[...])
        qh_ref[...] = high
        ql_ref[...] = low
        grad_ref[...] = jnp.zeros_like(grad_ref)
        loss_ref[...] = jnp.zeros_like(loss_ref)

    qh, ql = qh_ref[...], ql_ref[...]
    grad, total = grad_ref[...], loss_ref[...]
    negs = neg_ref[...].reshape(-1, WIDE)
    step = 256
    backs = []
    q_cols, q_rows = jnp.concatenate([qh, qh, ql], axis=1), jnp.concatenate([qh, ql, qh], axis=0)
    for first in range(0, negs.shape[0], step):
        nh, nl = split(negs[first : first + step, :])
        s = dot(q_cols, jnp.concatenate([nh, nl, nh], axis=1), ((1,), (1,)))
        small = jnp.exp(-jnp.abs(s))
        loss = jnp.maximum(s, 0.0) + log_one_plus(small)
        for part in range(step // 128):
            total = total + loss[:, part * 128 : (part + 1) * 128]
        whole = 1.0 + small
        turn = pl.reciprocal(whole, approx=True)
        turn = turn * (2.0 - whole * turn)
        weight = jnp.where(s >= 0.0, turn, small * turn)
        gh, gl = split(weight)
        grad = grad + dot(
            jnp.concatenate([gh, gh, gl], axis=1), jnp.concatenate([nh, nl, nh], axis=0)
        )
        back = dot(jnp.concatenate([gh, gh, gl], axis=0), q_rows, ((0,), (0,)))
        backs.append(back * (1.0 / ENT_NEGS))
    grad_ref[...] = grad
    loss_ref[...] = total
    back = jnp.concatenate(backs, axis=0).reshape(-1, 4, NEG, WIDE)

    def put(ref):
        for k in range(4):
            ref[(at_ref[1] + 4 - k) & 3] = back[:, k]

    @pl.when(side == 0)
    def _():
        put(near_ref)

    @pl.when(side == 1)
    def _():
        put(far_ref)


ENT_NEGS = 2 * CHIP_COUNT * NEG


def close_triples(core_ref, back_ref, place_ref, headv_ref, relv_ref, gradq_ref, loss_ref,
                  head_ref, rel_ref, gradh_ref, mine_ref, other_ref, out_ref):
    place = place_ref[...]
    lane = iota((TRIP, 128), 1)
    marks = jnp.concatenate(
        [hot(place == lane + part * 128) for part in range(SLOTS // 128)], axis=1
    )
    high, low = split(back_ref[...])
    tail = dot(marks, high) + dot(marks, low)
    positive = aux_column(tail)
    neg_loss = jnp.sum(loss_ref[...], axis=1, keepdims=True) * (1.0 / ENT_NEGS)
    drop = -positive
    loss = jnp.maximum(drop, 0.0) + jnp.log1p(jnp.exp(-jnp.abs(drop))) + neg_loss
    out_ref[...] = jnp.broadcast_to(loss, (TRIP, 128)).T[:1]
    grad = without_aux(tail) + gradq_ref[...] * (1.0 / ENT_NEGS)
    g_re, g_im = grad[:, :SIDE], grad[:, SIDE:]
    heads, rels = headv_ref[...], relv_ref[...]
    h_re, h_im, r_re, r_im = heads[:, :SIDE], heads[:, SIDE:], rels[:, :SIDE], rels[:, SIDE:]
    gh = jnp.concatenate([g_re * r_re + g_im * r_im, g_im * r_re - g_re * r_im], axis=1)
    gr = jnp.concatenate([g_re * h_re + g_im * h_im, g_im * h_re - g_re * h_im], axis=1)
    gradh_ref[...] = gh

    core = core_ref[0]
    at = iota((2 * CHIP_COUNT * 8, TRIP), 0)
    head, rel = head_ref[...], rel_ref[...]
    hub_id = (at + core * (HUB // 2)) % HUB
    rel_id = (at // 8 * REL_OWN + at % REL_OWN + core * (REL // 2)) % REL
    sums = []
    for marks, value in ((hot(hub_id == head), gh), (hot(rel_id == rel), gr)):
        high, low = split(value)
        sums.append(dot(marks, high) + dot(marks, low))
    for k, tile in enumerate(pack(*sums)):
        tile = tile.reshape(2, CHIP_COUNT, 8, 128)
        mine_ref[:, k * 8 : (k + 1) * 8, :] = tile[0]
        other_ref[:, k * 8 : (k + 1) * 8, :] = tile[1]


def scatter_entities(head_ref, gradh_ref, asked_ref, answer_ref, out_ref,
                     th_ref, tl_ref, hh_ref, hl_ref, row_ref):
    @pl.when(pl.program_id(0) == 0)
    def _():
        asked = asked_ref[...]
        row_ref[...] = jnp.broadcast_to(aux_column(asked).astype(I32) - 1, (SLOTS, 128))
        slope = -jax.nn.sigmoid(-aux_column(answer_ref[...]))
        high, low = split((without_aux(asked) * slope).T)
        th_ref[...] = high
        tl_ref[...] = low
        high, low = split(gradh_ref[...].T)
        hh_ref[...] = high
        hl_ref[...] = low

    count = out_ref.shape[1]
    first = pl.program_id(0) * count
    rows = row_ref[...]
    lane = iota((SLOTS, 128), 1) + first
    marks = jnp.concatenate([hot(rows == lane + k * 128) for k in range(count // 128)], axis=1)
    grad = dot(th_ref[...], marks) + dot(tl_ref[...], marks)
    marks = hot(iota((count, TRIP), 0) + first == head_ref[...] - HUB)
    nt = ((1,), (1,))
    grad = grad + (dot(hh_ref[...], marks, nt) + dot(hl_ref[...], marks, nt))
    out_ref[:HALF, :] = grad[:HALF]
    out_ref[HALF:, :] = grad[SIDE : SIDE + HALF]


def update_own(sums_ref, mine_ref, out_ref):
    lane = iota((8, 128), 1)
    grads = [jnp.sum(sums_ref[:, k * 8 : (k + 1) * 8, :], axis=0) for k in range(5)]
    mine = [mine_ref[k * 8 : (k + 1) * 8, :] for k in range(5)]

    def across(x):
        return jnp.sum(x, axis=1, keepdims=True)

    in_hub, in_rel = lane < 16, (lane >= 16) & (lane < 88)
    squares = [g * g for g in grads]
    hub = across(squares[0] + squares[1] + squares[3] + jnp.where(in_hub, squares[4], 0.0))
    rel = jnp.broadcast_to(across(squares[2] + jnp.where(in_rel, squares[4], 0.0)), (8, 128))
    rel = rel + pltpu.roll(rel, REL_OWN, 0)
    hub_acc = across(jnp.where(lane == 89, mine[4], 0.0)) + hub / WIDTH
    rel_acc = across(jnp.where(lane == 88, mine[4], 0.0)) + rel / WIDTH
    hub_root, rel_root = jnp.sqrt(hub_acc), jnp.sqrt(rel_acc)
    mixed = jnp.where(in_hub, hub_root, rel_root)
    roots = (hub_root, hub_root, rel_root, hub_root, mixed)
    new = [m - LEARN_RATE * g / root for m, g, root in zip(mine, grads, roots)]
    new[4] = jnp.where(lane == 88, rel_acc, jnp.where(lane == 89, hub_acc, new[4]))
    for k in range(5):
        out_ref[:, k * 8 : (k + 1) * 8, :] = jnp.broadcast_to(new[k][None], (CHIP_COUNT, 8, 128))


def place_new(core_ref, mine_ref, other_ref, hub_ref, hubacc_ref, rel_ref, relacc_ref, held_ref):
    core = core_ref[0]
    for part_ref, side in ((mine_ref, core), (other_ref, 1 - core)):
        def turned(k):
            return part_ref[:, k * 8 : (k + 1) * 8, :].reshape(CHIP_COUNT * 8, 128).T

        at = pl.ds(pl.multiple_of(side * (HUB // 2), 128), HUB // 2)
        hub_ref[0:128, at] = turned(0)
        hub_ref[HALF : HALF + 128, at] = turned(1)
        mixed = turned(3)
        hub_ref[128:HALF, at] = mixed[:72]
        hub_ref[HALF + 128 : HALF + 184, at] = mixed[72:]
        last = turned(4)
        hub_ref[HALF + 184 : WIDTH, at] = last[:16]
        hubacc_ref[:, at] = last[89:90]
        for chip in range(CHIP_COUNT):
            here = slice(chip * REL_OWN, (chip + 1) * REL_OWN)
            held_ref[0, here, :] = part_ref[chip, 16:20, :]
            held_ref[1, here, :] = part_ref[chip, 32:36, :]
            held_ref[2, here, :] = part_ref[chip, 20:24, :]
            held_ref[3, here, :] = part_ref[chip, 36:40, :]
        at = pl.ds(pl.multiple_of(side * (REL // 2), 128), REL // 2)
        for half in range(2):
            rel_ref[half * HALF : half * HALF + 128, at] = held_ref[2 * half].T
            last = held_ref[2 * half + 1].T
            rel_ref[half * HALF + 128 : (half + 1) * HALF, at] = last[16:88]
            if half == 0:
                relacc_ref[:, at] = last[88:89]


def update_entities(rows_ref, neg_ref, ent_ref, acc_ref, grad_ref, new_ref, newacc_ref,
                    high_ref, low_ref):
    @pl.when(pl.program_id(0) == 0)
    def _():
        high, low = split(jnp.sum(neg_ref[...], axis=0))
        high_ref[...] = high
        low_ref[...] = low

    count = ent_ref.shape[1]
    first = pl.program_id(0) * count
    rows = rows_ref[...][:, :1]
    marks = hot(iota((NEG, count), 1) + first == rows)
    tn = ((0,), (0,))
    more = dot(high_ref[...], marks, tn) + dot(low_ref[...], marks, tn)
    g_re = grad_ref[:HALF, :] + more[:HALF]
    g_im = grad_ref[HALF:, :] + more[SIDE : SIDE + HALF]
    square = jnp.sum(g_re * g_re, axis=0, keepdims=True) + jnp.sum(
        g_im * g_im, axis=0, keepdims=True
    )
    accum = acc_ref[...] + square / WIDTH
    newacc_ref[...] = accum
    root = jnp.sqrt(accum)
    new_ref[:HALF, :] = ent_ref[:HALF, :] - LEARN_RATE * g_re / root
    new_ref[HALF:, :] = ent_ref[HALF:, :] - LEARN_RATE * g_im / root


def around(block, axis):
    count = SIZES[SHARD.index(axis)]
    turns = [[(i, (i + k) % count) for i in range(count)] for k in range(1, count)]
    return [block] + [lax.ppermute(block, axis, turn) for turn in turns]


def shape(*dims, dtype=F32):
    return jax.ShapeDtypeStruct(dims, dtype)


def body(
    entity_table,
    entity_accum,
    hub_table,
    hub_accum,
    relation_table,
    relation_accum,
    head_ids,
    relation_ids,
    tail_owner,
    tail_rows,
    negative_rows,
):
    core = lax.axis_index("core").astype(I32)
    chip = lax.axis_index(CHIPS).astype(I32)
    core_arg = core.reshape(1)
    own_arg = (core * CHIP_COUNT + chip).reshape(1)
    ent_t, hub_t, rel_t = entity_table.T, hub_table.T, relation_table.T
    head_row, rel_row = head_ids.reshape(1, TRIP), relation_ids.reshape(1, TRIP)
    owner_row, tail_row = tail_owner.reshape(1, TRIP), tail_rows.reshape(1, TRIP)

    picked = pl.pallas_call(
        pick_negatives,
        out_shape=shape(NEG, WIDE),
        in_specs=[SMEM, VMEM],
        out_specs=VMEM,
        scratch_shapes=[pltpu.VMEM((WIDE, 128), F32)],
        compiler_params=params(),
        name="pick_negatives",
    )(negative_rows, ent_t)
    picked, head_row = lax.optimization_barrier((picked, head_row))
    near = jnp.concatenate(around(picked, "z"), axis=0)

    query, heads, rels, sent, place = pl.pallas_call(
        prepare,
        out_shape=[
            shape(TRIP, WIDE), shape(TRIP, WIDE), shape(TRIP, WIDE), shape(SLOTS, WIDE),
            shape(TRIP, 128, dtype=I32),
        ],
        in_specs=[VMEM] * 7,
        out_specs=[VMEM] * 5,
        compiler_params=params(),
        name="prepare",
    )(head_row, rel_row, owner_row, tail_row, ent_t, hub_t, rel_t)

    def exchange(rows):
        parts = rows.reshape(2 * CHIP_COUNT, CAP, WIDE)
        got = lax.all_to_all(parts, SHARD, split_axis=0, concat_axis=0, tiled=True)
        return got.reshape(SLOTS, WIDE)

    sent, near, own_arg = lax.optimization_barrier((sent, near, own_arg))
    near = lax.all_gather(near, ("x", "y", "core"), axis=0, tiled=True)
    asked = exchange(sent)
    ent_high, ent_low, mine_rows = pl.pallas_call(
        turn_tables,
        out_shape=[
            shape(ENT, WIDE, dtype=BF16), shape(ENT, WIDE, dtype=BF16), shape(OWN, 128)
        ],
        in_specs=[SMEM] + [VMEM] * 5,
        out_specs=[VMEM] * 3,
        scratch_shapes=[pltpu.VMEM((WIDE, 128), F32)],
        compiler_params=params(),
        cost_estimate=cost(1e6, 1e5),
        name="turn_tables",
    )(own_arg, ent_t, hub_t, rel_t, hub_accum.reshape(1, HUB), relation_accum.reshape(1, REL))

    rows = 256
    answer = pl.pallas_call(
        answer_queries,
        out_shape=shape(SLOTS, WIDE),
        grid=(SLOTS // rows,),
        in_specs=[pl.BlockSpec((rows, WIDE), lambda i: (i, 0)), VMEM, VMEM],
        out_specs=pl.BlockSpec((rows, WIDE), lambda i: (i, 0)),
        compiler_params=params(),
        name="answer_queries",
    )(asked, ent_high, ent_low)
    near, _ = lax.optimization_barrier((near, answer))
    back = exchange(answer)

    group, steps, places = 8, 2, 16
    near_back, far_back, grad_q, loss_sum = pl.pallas_call(
        score,
        out_shape=[
            shape(4, places, NEG, WIDE), shape(4, places, NEG, WIDE), shape(TRIP, WIDE),
            shape(TRIP, 128),
        ],
        grid_spec=pltpu.PrefetchScalarGridSpec(
            num_scalar_prefetch=1,
            grid=(2, steps),
            in_specs=[
                pl.BlockSpec((TRIP, WIDE), lambda i, c, at: (0, 0)),
                pl.BlockSpec(
                    (group, 1, 4 * NEG, WIDE), lambda i, c, at: (c, (i + at[0]) % 2, 0, 0)
                ),
            ],
            out_specs=[
                pl.BlockSpec(
                    (4, group, NEG, WIDE),
                    lambda i, c, at: (0, jnp.where(i == 0, c, steps - 1), 0, 0),
                ),
                pl.BlockSpec(
                    (4, group, NEG, WIDE), lambda i, c, at: (0, jnp.where(i == 0, 0, c), 0, 0)
                ),
                pl.BlockSpec((TRIP, WIDE), lambda i, c, at: (0, 0)),
                pl.BlockSpec((TRIP, 128), lambda i, c, at: (0, 0)),
            ],
            scratch_shapes=[pltpu.VMEM((TRIP, WIDE), BF16), pltpu.VMEM((TRIP, WIDE), BF16)],
        ),
        compiler_params=params(),
        cost_estimate=cost(20e9, 12e6),
        name="score",
    )(
        jnp.stack([core, lax.axis_index("z").astype(I32)]),
        query,
        near.reshape(places, 2, 4 * NEG, WIDE),
    )
    far_back, back = lax.optimization_barrier((far_back, back))
    part = near_back + lax.ppermute(far_back, "core", SWAP)
    part, back = lax.optimization_barrier((part.reshape(CHIP_COUNT, NEG, WIDE), back))
    neg_sums = lax.all_to_all(part, CHIPS, split_axis=0, concat_axis=0, tiled=True)

    grad_head, both_mine, both_other, loss = pl.pallas_call(
        close_triples,
        out_shape=[
            shape(TRIP, WIDE), shape(CHIP_COUNT, OWN, 128), shape(CHIP_COUNT, OWN, 128),
            shape(1, TRIP),
        ],
        in_specs=[SMEM] + [VMEM] * 8,
        out_specs=[VMEM] * 4,
        compiler_params=params(),
        name="close_triples",
    )(core_arg, back, place, heads, rels, grad_q, loss_sum, head_row, rel_row)
    both_swapped = lax.ppermute(both_other, "core", SWAP)

    paired = both_mine + both_swapped
    paired, neg_sums, asked, answer = lax.optimization_barrier((paired, neg_sums, asked, answer))
    sums = lax.all_to_all(paired, CHIPS, split_axis=0, concat_axis=0, tiled=True)

    columns = 256
    whole = pl.BlockSpec((SLOTS, WIDE), lambda i: (0, 0))
    entity_grad = pl.pallas_call(
        scatter_entities,
        out_shape=shape(WIDTH, ENT),
        grid=(ENT // columns,),
        in_specs=[
            pl.BlockSpec((1, TRIP), lambda i: (0, 0)),
            pl.BlockSpec((TRIP, WIDE), lambda i: (0, 0)),
            whole,
            whole,
        ],
        out_specs=pl.BlockSpec((WIDTH, columns), lambda i: (0, i)),
        scratch_shapes=[
            pltpu.VMEM((WIDE, SLOTS), BF16), pltpu.VMEM((WIDE, SLOTS), BF16),
            pltpu.VMEM((WIDE, TRIP), BF16), pltpu.VMEM((WIDE, TRIP), BF16),
            pltpu.VMEM((SLOTS, 128), I32),
        ],
        compiler_params=params(),
        cost_estimate=cost(1e6, 1e5),
        name="scatter_entities",
    )(head_row, grad_head, asked, answer)

    sums, entity_grad = lax.optimization_barrier((sums, entity_grad))
    own_new = pl.pallas_call(
        update_own,
        out_shape=shape(CHIP_COUNT, OWN, 128),
        in_specs=[VMEM] * 2,
        out_specs=VMEM,
        compiler_params=params(),
        name="update_own",
    )(sums, mine_rows)
    new_mine = lax.all_to_all(own_new, CHIPS, split_axis=0, concat_axis=0, tiled=True)
    columns = 512
    entity_new, entity_accum_new = pl.pallas_call(
        update_entities,
        out_shape=[shape(WIDTH, ENT), shape(1, ENT)],
        grid=(ENT // columns,),
        in_specs=[
            pl.BlockSpec((NEG, 128), lambda i: (0, 0)),
            pl.BlockSpec((CHIP_COUNT, NEG, WIDE), lambda i: (0, 0, 0)),
            pl.BlockSpec((WIDTH, columns), lambda i: (0, i)),
            pl.BlockSpec((1, columns), lambda i: (0, i)),
            pl.BlockSpec((WIDTH, columns), lambda i: (0, i)),
        ],
        out_specs=[
            pl.BlockSpec((WIDTH, columns), lambda i: (0, i)),
            pl.BlockSpec((1, columns), lambda i: (0, i)),
        ],
        scratch_shapes=[pltpu.VMEM((NEG, WIDE), BF16), pltpu.VMEM((NEG, WIDE), BF16)],
        compiler_params=params(),
        cost_estimate=cost(1e6, 1e5),
        name="update_entities",
    )(
        jnp.broadcast_to(negative_rows[:, None], (NEG, 128)),
        neg_sums,
        ent_t,
        entity_accum.reshape(1, ENT),
        entity_grad,
    )

    new_mine, entity_new = lax.optimization_barrier((new_mine, entity_new))
    new_other = lax.ppermute(new_mine, "core", SWAP)
    hub_new, hub_accum_new, rel_new, rel_accum_new = pl.pallas_call(
        place_new,
        out_shape=[shape(WIDTH, HUB), shape(1, HUB), shape(WIDTH, REL), shape(1, REL)],
        in_specs=[SMEM, VMEM, VMEM],
        out_specs=[VMEM] * 4,
        scratch_shapes=[pltpu.VMEM((4, REL // 2, 128), F32)],
        compiler_params=params(),
        name="place_new",
    )(core_arg, new_mine, new_other)
    return (
        entity_new.T,
        entity_accum_new.reshape(ENT),
        hub_new.T,
        hub_accum_new.reshape(HUB),
        rel_new.T,
        rel_accum_new.reshape(REL),
        loss.reshape(TRIP),
    )


def solution(mesh):
    fine = Mesh(mesh.devices.reshape(SIZES), SHARD)
    rows, vector = P(SHARD, None), P(SHARD)
    placed = (rows, vector, P(), P(), P(), P(), vector, vector, rows, vector, vector)
    return jax.shard_map(
        body,
        mesh=fine,
        in_specs=placed,
        out_specs=(rows, vector, P(), P(), P(), P(), vector),
        check_vma=False,
    )
```

```python
import jax
import jax.numpy as jnp
from jax import lax
from jax.experimental import pallas as pl
from jax.experimental.pallas import tpu as pltpu
from jax.sharding import Mesh, PartitionSpec as P

LEARN_RATE = 0.1
CHIPS = ("z", "x", "y")
SHARD = ("z", "x", "y", "core")
SIZES = (4, 4, 4, 2)
SWAP = [(0, 1), (1, 0)]
F32, BF16, I32 = jnp.float32, jnp.bfloat16, jnp.int32

WIDTH, HALF, SIDE, WIDE, AUX = 400, 200, 256, 512, 200
ENT, HUB, REL, TRIP, CHIP_COUNT, CAP, NEG = 2048, 1024, 512, 512, 64, 8, 16
SLOTS = 2 * CHIP_COUNT * CAP
HUB_OWN, REL_OWN, OWN = 8, 4, 40
VMEM = pl.BlockSpec(memory_space=pltpu.VMEM)
SMEM = pl.BlockSpec(memory_space=pltpu.SMEM)


def params():
    return pltpu.CompilerParams(vmem_limit_bytes=56 << 20)


def cost(flops, nbytes):
    return pl.CostEstimate(flops=int(flops), bytes_accessed=int(nbytes), transcendentals=0)


def split(x):
    high = x.astype(BF16)
    return high, (x - high.astype(F32)).astype(BF16)


def dot(a, b, contract=((1,), (0,))):
    return lax.dot_general(a, b, (contract, ((), ())), preferred_element_type=F32)


def hot(condition):
    return jnp.where(condition, 1.0, 0.0).astype(BF16)


def iota(shape, axis):
    return lax.broadcasted_iota(I32, shape, axis)


def aux_column(rows):
    part = rows[:, 128:SIDE]
    return jnp.sum(jnp.where(iota(part.shape, 1) == AUX - 128, part, 0.0), axis=1, keepdims=True)


def without_aux(rows):
    return jnp.where(iota(rows.shape, 1) == AUX, 0.0, rows)


def widen(re, im, aux=None):
    n = re.shape[1]
    gap = jnp.zeros((SIDE - HALF, n), F32)
    if aux is not None:
        first = jnp.where(iota((8, n), 0) == 0, aux, 0.0)
        middle = jnp.concatenate([first, jnp.zeros((SIDE - HALF - 8, n), F32)], axis=0)
    else:
        middle = gap
    return jnp.concatenate([re, middle, im, gap], axis=0)


def pick_negatives(rows_ref, ent_ref, out_ref, held_ref):
    held_ref[...] = jnp.zeros_like(held_ref)
    lane = iota((WIDTH, 128), 1)
    for j in range(NEG):
        row = rows_ref[j]
        block = ent_ref[:, pl.ds(pl.multiple_of((row // 128) * 128, 128), 128)]
        block = pltpu.roll(block, (j - row % 128 + 128) % 128, 1)
        here = lane == j
        held_ref[0:HALF, :] = jnp.where(here[:HALF], block[:HALF], held_ref[0:HALF, :])
        held_ref[SIDE : SIDE + HALF, :] = jnp.where(
            here[:HALF], block[HALF:], held_ref[SIDE : SIDE + HALF, :]
        )
    out_ref[...] = held_ref[...].T[:NEG]


def prepare(head_ref, rel_ref, owner_ref, tail_ref, ent_ref, hub_ref, relt_ref,
            query_ref, headv_ref, relv_ref, sent_ref, place_ref):
    head = head_ref[...]

    def gather(table, ids):
        marks = hot(iota((table.shape[1], TRIP), 0) == ids)
        high, low = split(table)
        return dot(high, marks) + dot(low, marks)

    heads = gather(hub_ref[...], head) + gather(ent_ref[...], head - HUB)
    rels = gather(relt_ref[...], rel_ref[...])
    h_re, h_im, r_re, r_im = heads[:HALF], heads[HALF:], rels[:HALF], rels[HALF:]
    q_re = h_re * r_re - h_im * r_im
    q_im = h_re * r_im + h_im * r_re
    headv_ref[...] = widen(h_re, h_im).T
    relv_ref[...] = widen(r_re, r_im).T
    query_ref[...] = widen(q_re, q_im).T

    owner = owner_ref[...]
    owned = hot(iota((2 * CHIP_COUNT, TRIP), 0) == owner)
    before = hot(iota((TRIP, TRIP), 0) < iota((TRIP, TRIP), 1))
    rank = jnp.sum(dot(owned, before) * owned.astype(F32), axis=0, keepdims=True)
    place = owner * CAP + rank.astype(I32)
    place_ref[...] = jnp.broadcast_to(place.astype(F32), (128, TRIP)).T.astype(I32)

    marks = hot(iota((SLOTS, TRIP), 0) == place)
    high, low = split(widen(q_re, q_im, tail_ref[...].astype(F32) + 1.0).T)
    sent_ref[...] = dot(marks, high) + dot(marks, low)


def turn_tables(own_ref, ent_ref, hub_ref, relt_ref, hubacc_ref, relacc_ref,
                high_ref, low_ref, mine_ref, held_ref):
    for block in range(ENT // 512):
        part = ent_ref[:, block * 512 : (block + 1) * 512]
        high, low = split(widen(part[:HALF], part[HALF:]).T)
        high_ref[block * 512 : (block + 1) * 512, :] = high
        low_ref[block * 512 : (block + 1) * 512, :] = low
    own = own_ref[0]
    lane = iota((1, 128), 1)

    def rows_of(ref, first, at):
        block = ref[:, pl.ds(pl.multiple_of((first // 128) * 128, 128), 128)]
        return pltpu.roll(block, (at - first % 128 + 128) % 128, 1)

    hub = rows_of(hub_ref, own * HUB_OWN, 0)
    rel = rows_of(relt_ref, own * REL_OWN, HUB_OWN)
    hub_acc = rows_of(hubacc_ref, own * HUB_OWN, 0)
    rel_acc = rows_of(relacc_ref, own * REL_OWN, HUB_OWN)
    is_hub, is_rel = lane < HUB_OWN, (lane >= HUB_OWN) & (lane < HUB_OWN + REL_OWN)
    both = jnp.where(is_hub, hub, jnp.where(is_rel, rel, 0.0))
    acc = jnp.where(is_hub, hub_acc, jnp.where(is_rel, rel_acc, 1.0))
    held_ref[...] = widen(both[:HALF], both[HALF:], acc)
    held_ref[SIDE + HALF : SIDE + HALF + 8, :] = jnp.broadcast_to(acc, (8, 128))
    rows = held_ref[...].T
    rel = rows[HUB_OWN : HUB_OWN + 8]
    rel = jnp.where(iota(rel.shape, 0) < REL_OWN, rel, pltpu.roll(rel, REL_OWN, 0))
    for k, tile in enumerate(pack(rows[:HUB_OWN], rel)):
        mine_ref[k * 8 : (k + 1) * 8, :] = tile


def pack(hub, rel):
    lane, low = iota((hub.shape[0], 128), 1), iota((hub.shape[0], 128), 0) % 8 < REL_OWN
    hubs = [hub[:, k * 128 : (k + 1) * 128] for k in range(4)]
    rels = [rel[:, k * 128 : (k + 1) * 128] for k in range(4)]
    turned = pltpu.roll(hubs[3], 72, 1)
    tail = pltpu.roll(jnp.where(low, rels[1], rels[3]), 16, 1)
    last = jnp.where(lane < 16, turned, jnp.where(lane < 89, tail, pltpu.roll(hubs[1], 17, 1)))
    return (
        hubs[0],
        hubs[2],
        jnp.where(low, rels[0], rels[2]),
        jnp.where(lane < 72, hubs[1], turned),
        jnp.where(lane < 90, last, 0.0),
    )


def answer_queries(asked_ref, high_ref, low_ref, out_ref):
    asked = asked_ref[...]
    row = aux_column(asked).astype(I32) - 1
    marks = hot(iota((asked.shape[0], ENT), 1) == row)
    tails = dot(marks, high_ref[...]) + dot(marks, low_ref[...])
    positive = jnp.sum(asked * tails, axis=1, keepdims=True)
    slope = -jax.nn.sigmoid(-positive)
    out_ref[...] = jnp.where(iota(tails.shape, 1) == AUX, positive, slope * tails)


def log_one_plus(x):
    series = x * (1.0 - x * (0.5 - x * (1.0 / 3.0)))
    return jnp.where(x < 1e-3, series, jnp.log(1.0 + x))


def score(at_ref, query_ref, other_ref, neg_ref, back_ref, grad_ref, gradother_ref,
          qh_ref, ql_ref, sum_ref, loss_ref):
    step, last = pl.program_id(0), pl.num_programs(0) - 1

    @pl.when(step == 0)
    def _():
        for first, ref in ((0, query_ref), (TRIP, other_ref)):
            high, low = split(ref[...])
            qh_ref[first : first + TRIP, :] = high
            ql_ref[first : first + TRIP, :] = low
        sum_ref[...] = jnp.zeros_like(sum_ref)
        loss_ref[...] = jnp.zeros_like(loss_ref)

    qh, ql = qh_ref[...], ql_ref[...]
    grad, total = sum_ref[...], loss_ref[...]
    negs = neg_ref[...].reshape(-1, WIDE)
    chunk = 256
    backs = []
    q_cols, q_rows = jnp.concatenate([qh, qh, ql], axis=1), jnp.concatenate([qh, ql, qh], axis=0)
    for first in range(0, negs.shape[0], chunk):
        nh, nl = split(negs[first : first + chunk, :])
        s = dot(q_cols, jnp.concatenate([nh, nl, nh], axis=1), ((1,), (1,)))
        small = jnp.exp(-jnp.abs(s))
        loss = jnp.maximum(s, 0.0) + log_one_plus(small)
        for part in range(chunk // 128):
            total = total + loss[:, part * 128 : (part + 1) * 128]
        whole = 1.0 + small
        turn = pl.reciprocal(whole, approx=True)
        turn = turn * (2.0 - whole * turn)
        weight = jnp.where(s >= 0.0, turn, small * turn)
        gh, gl = split(weight)
        grad = grad + dot(
            jnp.concatenate([gh, gh, gl], axis=1), jnp.concatenate([nh, nl, nh], axis=0)
        )
        back = dot(jnp.concatenate([gh, gh, gl], axis=0), q_rows, ((0,), (0,)))
        backs.append(back * (1.0 / ENT_NEGS))
    sum_ref[...] = grad
    loss_ref[...] = total
    back = jnp.concatenate(backs, axis=0).reshape(-1, 4, NEG, WIDE)
    for k in range(4):
        back_ref[(at_ref[0] + 4 - k) & 3] = back[:, k]

    @pl.when(step == last)
    def _():
        for first, ref in ((0, grad_ref), (TRIP, gradother_ref)):
            loss = jnp.sum(loss_ref[first : first + TRIP, :], axis=1, keepdims=True)
            grad = sum_ref[first : first + TRIP, :]
            ref[...] = jnp.where(iota(grad.shape, 1) == AUX, loss, grad) * (1.0 / ENT_NEGS)


ENT_NEGS = 2 * CHIP_COUNT * NEG


def close_triples(core_ref, back_ref, place_ref, headv_ref, relv_ref, gradq_ref, gradmore_ref,
                  head_ref, rel_ref, gradh_ref, mine_ref, other_ref, out_ref):
    place = place_ref[...]
    lane = iota((TRIP, 128), 1)
    marks = jnp.concatenate(
        [hot(place == lane + part * 128) for part in range(SLOTS // 128)], axis=1
    )
    high, low = split(back_ref[...])
    tail = dot(marks, high) + dot(marks, low)
    positive = aux_column(tail)
    from_negs = gradq_ref[...] + gradmore_ref[...]
    neg_loss = aux_column(from_negs)
    drop = -positive
    loss = jnp.maximum(drop, 0.0) + jnp.log1p(jnp.exp(-jnp.abs(drop))) + neg_loss
    out_ref[...] = jnp.broadcast_to(loss, (TRIP, 128)).T[:1]
    grad = without_aux(tail + from_negs)
    g_re, g_im = grad[:, :SIDE], grad[:, SIDE:]
    heads, rels = headv_ref[...], relv_ref[...]
    h_re, h_im, r_re, r_im = heads[:, :SIDE], heads[:, SIDE:], rels[:, :SIDE], rels[:, SIDE:]
    gh = jnp.concatenate([g_re * r_re + g_im * r_im, g_im * r_re - g_re * r_im], axis=1)
    gr = jnp.concatenate([g_re * h_re + g_im * h_im, g_im * h_re - g_re * h_im], axis=1)
    gradh_ref[...] = gh

    core = core_ref[0]
    at = iota((2 * CHIP_COUNT * 8, TRIP), 0)
    head, rel = head_ref[...], rel_ref[...]
    hub_id = (at + core * (HUB // 2)) % HUB
    rel_id = (at // 8 * REL_OWN + at % REL_OWN + core * (REL // 2)) % REL
    sums = []
    for marks, value in ((hot(hub_id == head), gh), (hot(rel_id == rel), gr)):
        high, low = split(value)
        sums.append(dot(marks, high) + dot(marks, low))
    for k, tile in enumerate(pack(*sums)):
        tile = tile.reshape(2, CHIP_COUNT, 8, 128)
        mine_ref[:, k * 8 : (k + 1) * 8, :] = tile[0]
        other_ref[:, k * 8 : (k + 1) * 8, :] = tile[1]


def scatter_entities(head_ref, gradh_ref, asked_ref, answer_ref, out_ref,
                     th_ref, tl_ref, hh_ref, hl_ref, row_ref):
    @pl.when(pl.program_id(0) == 0)
    def _():
        asked = asked_ref[...]
        row_ref[...] = jnp.broadcast_to(aux_column(asked).astype(I32) - 1, (SLOTS, 128))
        slope = -jax.nn.sigmoid(-aux_column(answer_ref[...]))
        high, low = split((without_aux(asked) * slope).T)
        th_ref[...] = high
        tl_ref[...] = low
        high, low = split(gradh_ref[...].T)
        hh_ref[...] = high
        hl_ref[...] = low

    count = out_ref.shape[1]
    first = pl.program_id(0) * count
    rows = row_ref[...]
    lane = iota((SLOTS, 128), 1) + first
    marks = jnp.concatenate([hot(rows == lane + k * 128) for k in range(count // 128)], axis=1)
    grad = dot(th_ref[...], marks) + dot(tl_ref[...], marks)
    marks = hot(iota((count, TRIP), 0) + first == head_ref[...] - HUB)
    nt = ((1,), (1,))
    grad = grad + (dot(hh_ref[...], marks, nt) + dot(hl_ref[...], marks, nt))
    out_ref[:HALF, :] = grad[:HALF]
    out_ref[HALF:, :] = grad[SIDE : SIDE + HALF]


def update_own(sums_ref, mine_ref, out_ref):
    lane = iota((8, 128), 1)
    grads = [jnp.sum(sums_ref[:, k * 8 : (k + 1) * 8, :], axis=0) for k in range(5)]
    mine = [mine_ref[k * 8 : (k + 1) * 8, :] for k in range(5)]

    def across(x):
        return jnp.sum(x, axis=1, keepdims=True)

    in_hub, in_rel = lane < 16, (lane >= 16) & (lane < 88)
    squares = [g * g for g in grads]
    hub = across(squares[0] + squares[1] + squares[3] + jnp.where(in_hub, squares[4], 0.0))
    rel = jnp.broadcast_to(across(squares[2] + jnp.where(in_rel, squares[4], 0.0)), (8, 128))
    rel = rel + pltpu.roll(rel, REL_OWN, 0)
    hub_acc = across(jnp.where(lane == 89, mine[4], 0.0)) + hub / WIDTH
    rel_acc = across(jnp.where(lane == 88, mine[4], 0.0)) + rel / WIDTH
    hub_root, rel_root = jnp.sqrt(hub_acc), jnp.sqrt(rel_acc)
    mixed = jnp.where(in_hub, hub_root, rel_root)
    roots = (hub_root, hub_root, rel_root, hub_root, mixed)
    new = [m - LEARN_RATE * g / root for m, g, root in zip(mine, grads, roots)]
    new[4] = jnp.where(lane == 88, rel_acc, jnp.where(lane == 89, hub_acc, new[4]))
    for k in range(5):
        out_ref[:, k * 8 : (k + 1) * 8, :] = jnp.broadcast_to(new[k][None], (CHIP_COUNT, 8, 128))


def place_new(side_ref, part_ref, *refs):
    hub_ref, hubacc_ref, rel_ref, relacc_ref, held_ref = refs[-5:]

    def turned(k):
        return part_ref[:, k * 8 : (k + 1) * 8, :].reshape(CHIP_COUNT * 8, 128).T

    hub_ref[0:128, :] = turned(0)
    hub_ref[HALF : HALF + 128, :] = turned(1)
    mixed = turned(3)
    hub_ref[128:HALF, :] = mixed[:72]
    hub_ref[HALF + 128 : HALF + 184, :] = mixed[72:]
    last = turned(4)
    hub_ref[HALF + 184 : WIDTH, :] = last[:16]
    hubacc_ref[...] = last[89:90]
    for chip in range(CHIP_COUNT):
        here = slice(chip * REL_OWN, (chip + 1) * REL_OWN)
        held_ref[0, here, :] = part_ref[chip, 16:20, :]
        held_ref[1, here, :] = part_ref[chip, 32:36, :]
        held_ref[2, here, :] = part_ref[chip, 20:24, :]
        held_ref[3, here, :] = part_ref[chip, 36:40, :]
    for half in range(2):
        rel_ref[half * HALF : half * HALF + 128, :] = held_ref[2 * half].T
        last = held_ref[2 * half + 1].T
        rel_ref[half * HALF + 128 : (half + 1) * HALF, :] = last[16:88]
        if half == 0:
            relacc_ref[...] = last[88:89]


def update_entities(rows_ref, neg_ref, ent_ref, acc_ref, grad_ref, new_ref, newacc_ref,
                    high_ref, low_ref):
    @pl.when(pl.program_id(0) == 0)
    def _():
        high, low = split(jnp.sum(neg_ref[...], axis=0))
        high_ref[...] = high
        low_ref[...] = low

    count = ent_ref.shape[1]
    first = pl.program_id(0) * count
    rows = rows_ref[...][:, :1]
    marks = hot(iota((NEG, count), 1) + first == rows)
    tn = ((0,), (0,))
    more = dot(high_ref[...], marks, tn) + dot(low_ref[...], marks, tn)
    g_re = grad_ref[:HALF, :] + more[:HALF]
    g_im = grad_ref[HALF:, :] + more[SIDE : SIDE + HALF]
    square = jnp.sum(g_re * g_re, axis=0, keepdims=True) + jnp.sum(
        g_im * g_im, axis=0, keepdims=True
    )
    accum = acc_ref[...] + square / WIDTH
    newacc_ref[...] = accum
    root = jnp.sqrt(accum)
    new_ref[:HALF, :] = ent_ref[:HALF, :] - LEARN_RATE * g_re / root
    new_ref[HALF:, :] = ent_ref[HALF:, :] - LEARN_RATE * g_im / root


def around(block, axis):
    count = SIZES[SHARD.index(axis)]
    turns = [[(i, (i + k) % count) for i in range(count)] for k in range(1, count)]
    return [block] + [lax.ppermute(block, axis, turn) for turn in turns]


def shape(*dims, dtype=F32):
    return jax.ShapeDtypeStruct(dims, dtype)


def body(
    entity_table,
    entity_accum,
    hub_table,
    hub_accum,
    relation_table,
    relation_accum,
    head_ids,
    relation_ids,
    tail_owner,
    tail_rows,
    negative_rows,
):
    core = lax.axis_index("core").astype(I32)
    chip = lax.axis_index(CHIPS).astype(I32)
    core_arg = core.reshape(1)
    own_arg = (core * CHIP_COUNT + chip).reshape(1)
    ent_t, hub_t, rel_t = entity_table.T, hub_table.T, relation_table.T
    head_row, rel_row = head_ids.reshape(1, TRIP), relation_ids.reshape(1, TRIP)
    owner_row, tail_row = tail_owner.reshape(1, TRIP), tail_rows.reshape(1, TRIP)

    picked = pl.pallas_call(
        pick_negatives,
        out_shape=shape(NEG, WIDE),
        in_specs=[SMEM, VMEM],
        out_specs=VMEM,
        scratch_shapes=[pltpu.VMEM((WIDE, 128), F32)],
        compiler_params=params(),
        name="pick_negatives",
    )(negative_rows, ent_t)
    picked, head_row = lax.optimization_barrier((picked, head_row))
    near = jnp.concatenate(around(picked, "z"), axis=0)

    query, heads, rels, sent, place = pl.pallas_call(
        prepare,
        out_shape=[
            shape(TRIP, WIDE), shape(TRIP, WIDE), shape(TRIP, WIDE), shape(SLOTS, WIDE),
            shape(TRIP, 128, dtype=I32),
        ],
        in_specs=[VMEM] * 7,
        out_specs=[VMEM] * 5,
        compiler_params=params(),
        name="prepare",
    )(head_row, rel_row, owner_row, tail_row, ent_t, hub_t, rel_t)

    def exchange(rows):
        parts = rows.reshape(2 * CHIP_COUNT, CAP, WIDE)
        got = lax.all_to_all(parts, SHARD, split_axis=0, concat_axis=0, tiled=True)
        return got.reshape(SLOTS, WIDE)

    sent, near, own_arg = lax.optimization_barrier((sent, near, own_arg))
    near = lax.all_gather(near, ("x", "y"), axis=0, tiled=True)
    query_other = lax.ppermute(query, "core", SWAP)
    asked = exchange(sent)
    ent_high, ent_low, mine_rows = pl.pallas_call(
        turn_tables,
        out_shape=[
            shape(ENT, WIDE, dtype=BF16), shape(ENT, WIDE, dtype=BF16), shape(OWN, 128)
        ],
        in_specs=[SMEM] + [VMEM] * 5,
        out_specs=[VMEM] * 3,
        scratch_shapes=[pltpu.VMEM((WIDE, 128), F32)],
        compiler_params=params(),
        cost_estimate=cost(1e6, 1e5),
        name="turn_tables",
    )(own_arg, ent_t, hub_t, rel_t, hub_accum.reshape(1, HUB), relation_accum.reshape(1, REL))

    rows = 256
    answer = pl.pallas_call(
        answer_queries,
        out_shape=shape(SLOTS, WIDE),
        grid=(SLOTS // rows,),
        in_specs=[pl.BlockSpec((rows, WIDE), lambda i: (i, 0)), VMEM, VMEM],
        out_specs=pl.BlockSpec((rows, WIDE), lambda i: (i, 0)),
        compiler_params=params(),
        name="answer_queries",
    )(asked, ent_high, ent_low)
    near, _ = lax.optimization_barrier((near, answer))
    back = exchange(answer)

    group, places = 8, 16
    whole = pl.BlockSpec((TRIP, WIDE), lambda i, at: (0, 0))
    part, grad_q, grad_other = pl.pallas_call(
        score,
        out_shape=[shape(4, places, NEG, WIDE), shape(TRIP, WIDE), shape(TRIP, WIDE)],
        grid_spec=pltpu.PrefetchScalarGridSpec(
            num_scalar_prefetch=1,
            grid=(places // group,),
            in_specs=[
                whole, whole, pl.BlockSpec((group, 4 * NEG, WIDE), lambda i, at: (i, 0, 0))
            ],
            out_specs=[
                pl.BlockSpec((4, group, NEG, WIDE), lambda i, at: (0, i, 0, 0)), whole, whole
            ],
            scratch_shapes=[
                pltpu.VMEM((2 * TRIP, WIDE), BF16), pltpu.VMEM((2 * TRIP, WIDE), BF16),
                pltpu.VMEM((2 * TRIP, WIDE), F32), pltpu.VMEM((2 * TRIP, 128), F32),
            ],
        ),
        compiler_params=params(),
        cost_estimate=cost(20e9, 12e6),
        name="score",
    )(
        lax.axis_index("z").astype(I32).reshape(1),
        query,
        query_other,
        near.reshape(places, 4 * NEG, WIDE),
    )
    grad_other, back = lax.optimization_barrier((grad_other, back))
    grad_more = lax.ppermute(grad_other, "core", SWAP)
    part, back = lax.optimization_barrier((part.reshape(CHIP_COUNT, NEG, WIDE), back))
    neg_sums = lax.all_to_all(part, CHIPS, split_axis=0, concat_axis=0, tiled=True)

    grad_head, both_mine, both_other, loss = pl.pallas_call(
        close_triples,
        out_shape=[
            shape(TRIP, WIDE), shape(CHIP_COUNT, OWN, 128), shape(CHIP_COUNT, OWN, 128),
            shape(1, TRIP),
        ],
        in_specs=[SMEM] + [VMEM] * 8,
        out_specs=[VMEM] * 4,
        compiler_params=params(),
        name="close_triples",
    )(core_arg, back, place, heads, rels, grad_q, grad_more, head_row, rel_row)
    both_swapped = lax.ppermute(both_other, "core", SWAP)

    paired = both_mine + both_swapped
    paired, neg_sums, asked, answer = lax.optimization_barrier((paired, neg_sums, asked, answer))
    sums = lax.all_to_all(paired, CHIPS, split_axis=0, concat_axis=0, tiled=True)

    columns = 256
    whole = pl.BlockSpec((SLOTS, WIDE), lambda i: (0, 0))
    entity_grad = pl.pallas_call(
        scatter_entities,
        out_shape=shape(WIDTH, ENT),
        grid=(ENT // columns,),
        in_specs=[
            pl.BlockSpec((1, TRIP), lambda i: (0, 0)),
            pl.BlockSpec((TRIP, WIDE), lambda i: (0, 0)),
            whole,
            whole,
        ],
        out_specs=pl.BlockSpec((WIDTH, columns), lambda i: (0, i)),
        scratch_shapes=[
            pltpu.VMEM((WIDE, SLOTS), BF16), pltpu.VMEM((WIDE, SLOTS), BF16),
            pltpu.VMEM((WIDE, TRIP), BF16), pltpu.VMEM((WIDE, TRIP), BF16),
            pltpu.VMEM((SLOTS, 128), I32),
        ],
        compiler_params=params(),
        cost_estimate=cost(1e6, 1e5),
        name="scatter_entities",
    )(head_row, grad_head, asked, answer)

    sums, entity_grad = lax.optimization_barrier((sums, entity_grad))
    own_new = pl.pallas_call(
        update_own,
        out_shape=shape(CHIP_COUNT, OWN, 128),
        in_specs=[VMEM] * 2,
        out_specs=VMEM,
        compiler_params=params(),
        name="update_own",
    )(sums, mine_rows)
    new_mine = lax.all_to_all(own_new, CHIPS, split_axis=0, concat_axis=0, tiled=True)
    columns = 512
    entity_new, entity_accum_new = pl.pallas_call(
        update_entities,
        out_shape=[shape(WIDTH, ENT), shape(1, ENT)],
        grid=(ENT // columns,),
        in_specs=[
            pl.BlockSpec((NEG, 128), lambda i: (0, 0)),
            pl.BlockSpec((CHIP_COUNT, NEG, WIDE), lambda i: (0, 0, 0)),
            pl.BlockSpec((WIDTH, columns), lambda i: (0, i)),
            pl.BlockSpec((1, columns), lambda i: (0, i)),
            pl.BlockSpec((WIDTH, columns), lambda i: (0, i)),
        ],
        out_specs=[
            pl.BlockSpec((WIDTH, columns), lambda i: (0, i)),
            pl.BlockSpec((1, columns), lambda i: (0, i)),
        ],
        scratch_shapes=[pltpu.VMEM((NEG, WIDE), BF16), pltpu.VMEM((NEG, WIDE), BF16)],
        compiler_params=params(),
        cost_estimate=cost(1e6, 1e5),
        name="update_entities",
    )(
        jnp.broadcast_to(negative_rows[:, None], (NEG, 128)),
        neg_sums,
        ent_t,
        entity_accum.reshape(1, ENT),
        entity_grad,
    )

    new_mine, entity_new = lax.optimization_barrier((new_mine, entity_new))
    new_other = lax.ppermute(new_mine, "core", SWAP)

    def placed(side, part, *before):
        sizes = ((WIDTH, HUB), (1, HUB), (WIDTH, REL), (1, REL))
        return pl.pallas_call(
            place_new,
            out_shape=[shape(*size) for size in sizes],
            grid_spec=pltpu.PrefetchScalarGridSpec(
                num_scalar_prefetch=1,
                grid=(1,),
                in_specs=[pl.BlockSpec((CHIP_COUNT, OWN, 128), lambda i, side: (0, 0, 0))]
                + [pl.BlockSpec(memory_space=pl.ANY)] * len(before),
                out_specs=[
                    pl.BlockSpec((rows, count // 2), lambda i, side: (0, side[0]))
                    for rows, count in sizes
                ],
                scratch_shapes=[pltpu.VMEM((4, REL // 2, 128), F32)],
            ),
            input_output_aliases={k + 2: k for k in range(len(before))},
            compiler_params=params(),
            name="place_new",
        )(side, part, *before)

    halves = placed(core_arg, new_mine)
    hub_new, hub_accum_new, rel_new, rel_accum_new = placed(1 - core_arg, new_other, *halves)
    return (
        entity_new.T,
        entity_accum_new.reshape(ENT),
        hub_new.T,
        hub_accum_new.reshape(HUB),
        rel_new.T,
        rel_accum_new.reshape(REL),
        loss.reshape(TRIP),
    )


def solution(mesh):
    fine = Mesh(mesh.devices.reshape(SIZES), SHARD)
    rows, vector = P(SHARD, None), P(SHARD)
    placed = (rows, vector, P(), P(), P(), P(), vector, vector, rows, vector, vector)
    return jax.shard_map(
        body,
        mesh=fine,
        in_specs=placed,
        out_specs=(rows, vector, P(), P(), P(), P(), vector),
        check_vma=False,
    )
```

```python
import jax
import jax.numpy as jnp
from jax import lax
from jax.experimental import pallas as pl
from jax.experimental.pallas import tpu as pltpu
from jax.sharding import Mesh, PartitionSpec as P

LEARN_RATE = 0.1
CHIPS = ("z", "x", "y")
SHARD = ("z", "x", "y", "core")
SIZES = (4, 4, 4, 2)
SWAP = [(0, 1), (1, 0)]
F32, BF16, I32 = jnp.float32, jnp.bfloat16, jnp.int32

WIDTH, HALF, SIDE, WIDE, AUX = 400, 200, 256, 512, 200
ENT, HUB, REL, TRIP, CHIP_COUNT, CAP, NEG = 2048, 1024, 512, 512, 64, 8, 16
SLOTS = 2 * CHIP_COUNT * CAP
NEG_PACKED = 56
HUB_OWN, REL_OWN, OWN = 8, 4, 40
VMEM = pl.BlockSpec(memory_space=pltpu.VMEM)
SMEM = pl.BlockSpec(memory_space=pltpu.SMEM)


def params(mib=56):
    return pltpu.CompilerParams(vmem_limit_bytes=mib << 20)


def cost(flops, nbytes):
    return pl.CostEstimate(flops=int(flops), bytes_accessed=int(nbytes), transcendentals=0)


def split(x):
    high = x.astype(BF16)
    return high, (x - high.astype(F32)).astype(BF16)


def dot(a, b, contract=((1,), (0,))):
    return lax.dot_general(a, b, (contract, ((), ())), preferred_element_type=F32)


def hot(condition):
    return jnp.where(condition, 1.0, 0.0).astype(BF16)


def iota(shape, axis):
    return lax.broadcasted_iota(I32, shape, axis)


def aux_column(rows):
    part = rows[:, 128:SIDE]
    return jnp.sum(jnp.where(iota(part.shape, 1) == AUX - 128, part, 0.0), axis=1, keepdims=True)


def without_aux(rows):
    return jnp.where(iota(rows.shape, 1) == AUX, 0.0, rows)


def widen(re, im, aux=None):
    n = re.shape[1]
    gap = jnp.zeros((SIDE - HALF, n), F32)
    if aux is not None:
        first = jnp.where(iota((8, n), 0) == 0, aux, 0.0)
        middle = jnp.concatenate([first, jnp.zeros((SIDE - HALF - 8, n), F32)], axis=0)
    else:
        middle = gap
    return jnp.concatenate([re, middle, im, gap], axis=0)


def pick_negatives(rows_ref, ent_ref, out_ref, held_ref):
    held_ref[...] = jnp.zeros_like(held_ref)
    lane = iota((WIDTH, 128), 1)
    for j in range(NEG):
        row = rows_ref[j]
        block = ent_ref[:, pl.ds(pl.multiple_of((row // 128) * 128, 128), 128)]
        block = pltpu.roll(block, (j - row % 128 + 128) % 128, 1)
        here = lane == j
        held_ref[0:HALF, :] = jnp.where(here[:HALF], block[:HALF], held_ref[0:HALF, :])
        held_ref[SIDE : SIDE + HALF, :] = jnp.where(
            here[:HALF], block[HALF:], held_ref[SIDE : SIDE + HALF, :]
        )
    out_ref[...] = held_ref[...].T[:NEG]


def embed(head_ref, rel_ref, ent_ref, hub_ref, relt_ref):
    head = head_ref[...]

    def gather(table, ids):
        marks = hot(iota((table.shape[1], TRIP), 0) == ids)
        high, low = split(table)
        return dot(high, marks) + dot(low, marks)

    heads = gather(hub_ref[...], head) + gather(ent_ref[...], head - HUB)
    rels = gather(relt_ref[...], rel_ref[...])
    h_re, h_im, r_re, r_im = heads[:HALF], heads[HALF:], rels[:HALF], rels[HALF:]
    q_re = h_re * r_re - h_im * r_im
    q_im = h_re * r_im + h_im * r_re
    return (h_re, h_im), (r_re, r_im), (q_re, q_im)


def embed_rows(head_ref, rel_ref, ent_ref, hub_ref, relt_ref, query_ref, headv_ref, relv_ref):
    heads, rels, queries = embed(head_ref, rel_ref, ent_ref, hub_ref, relt_ref)
    headv_ref[...] = widen(*heads).T
    relv_ref[...] = widen(*rels).T
    query_ref[...] = widen(*queries).T


def prepare(head_ref, rel_ref, owner_ref, tail_ref, ent_ref, hub_ref, relt_ref,
            sent_ref, place_ref):
    _, _, queries = embed(head_ref, rel_ref, ent_ref, hub_ref, relt_ref)
    owner = owner_ref[...]
    owned = hot(iota((2 * CHIP_COUNT, TRIP), 0) == owner)
    before = hot(iota((TRIP, TRIP), 0) < iota((TRIP, TRIP), 1))
    rank = jnp.sum(dot(owned, before) * owned.astype(F32), axis=0, keepdims=True)
    place = owner * CAP + rank.astype(I32)
    place_ref[...] = jnp.broadcast_to(place.astype(F32), (128, TRIP)).T.astype(I32)

    marks = hot(iota((SLOTS, TRIP), 0) == place)
    high, low = split(widen(*queries, tail_ref[...].astype(F32) + 1.0).T)
    sent_ref[...] = dot(marks, high) + dot(marks, low)


def turn_tables(own_ref, ent_ref, hub_ref, relt_ref, hubacc_ref, relacc_ref,
                high_ref, low_ref, mine_ref, held_ref):
    for block in range(ENT // 512):
        part = ent_ref[:, block * 512 : (block + 1) * 512]
        high, low = split(widen(part[:HALF], part[HALF:]).T)
        high_ref[block * 512 : (block + 1) * 512, :] = high
        low_ref[block * 512 : (block + 1) * 512, :] = low
    own = own_ref[0]
    lane = iota((1, 128), 1)

    def rows_of(ref, first, at):
        block = ref[:, pl.ds(pl.multiple_of((first // 128) * 128, 128), 128)]
        return pltpu.roll(block, (at - first % 128 + 128) % 128, 1)

    hub = rows_of(hub_ref, own * HUB_OWN, 0)
    rel = rows_of(relt_ref, own * REL_OWN, HUB_OWN)
    hub_acc = rows_of(hubacc_ref, own * HUB_OWN, 0)
    rel_acc = rows_of(relacc_ref, own * REL_OWN, HUB_OWN)
    is_hub, is_rel = lane < HUB_OWN, (lane >= HUB_OWN) & (lane < HUB_OWN + REL_OWN)
    both = jnp.where(is_hub, hub, jnp.where(is_rel, rel, 0.0))
    acc = jnp.where(is_hub, hub_acc, jnp.where(is_rel, rel_acc, 1.0))
    held_ref[...] = widen(both[:HALF], both[HALF:], acc)
    held_ref[SIDE + HALF : SIDE + HALF + 8, :] = jnp.broadcast_to(acc, (8, 128))
    rows = held_ref[...].T
    rel = rows[HUB_OWN : HUB_OWN + 8]
    rel = jnp.where(iota(rel.shape, 0) < REL_OWN, rel, pltpu.roll(rel, REL_OWN, 0))
    for k, tile in enumerate(pack(rows[:HUB_OWN], rel)):
        mine_ref[k * 8 : (k + 1) * 8, :] = tile


def pack(hub, rel):
    lane, low = iota((hub.shape[0], 128), 1), iota((hub.shape[0], 128), 0) % 8 < REL_OWN
    hubs = [hub[:, k * 128 : (k + 1) * 128] for k in range(4)]
    rels = [rel[:, k * 128 : (k + 1) * 128] for k in range(4)]
    turned = pltpu.roll(hubs[3], 72, 1)
    tail = pltpu.roll(jnp.where(low, rels[1], rels[3]), 16, 1)
    last = jnp.where(lane < 16, turned, jnp.where(lane < 89, tail, pltpu.roll(hubs[1], 17, 1)))
    return (
        hubs[0],
        hubs[2],
        jnp.where(low, rels[0], rels[2]),
        jnp.where(lane < 72, hubs[1], turned),
        jnp.where(lane < 90, last, 0.0),
    )


def answer_queries(asked_ref, high_ref, low_ref, out_ref):
    asked = asked_ref[...]
    row = aux_column(asked).astype(I32) - 1
    marks = hot(iota((asked.shape[0], ENT), 1) == row)
    tails = dot(marks, high_ref[...]) + dot(marks, low_ref[...])
    positive = jnp.sum(asked * tails, axis=1, keepdims=True)
    slope = -jax.nn.sigmoid(-positive)
    out_ref[...] = jnp.where(iota(tails.shape, 1) == AUX, positive, slope * tails)


def log_one_plus(x):
    series = x * (1.0 - x * (0.5 - x * (1.0 / 3.0)))
    return jnp.where(x < 1e-3, series, jnp.log(1.0 + x))


def score(at_ref, query_ref, other_ref, neg_ref, back_ref, grad_ref, gradother_ref,
          qh_ref, ql_ref, sum_ref, loss_ref):
    step, last = pl.program_id(0), pl.num_programs(0) - 1

    @pl.when(step == 0)
    def _():
        for first, ref in ((0, query_ref), (TRIP, other_ref)):
            high, low = split(ref[...])
            qh_ref[first : first + TRIP, :] = high
            ql_ref[first : first + TRIP, :] = low
        sum_ref[...] = jnp.zeros_like(sum_ref)
        loss_ref[...] = jnp.zeros_like(loss_ref)

    qh, ql = qh_ref[...], ql_ref[...]
    grad, total = sum_ref[...], loss_ref[...]
    negs = neg_ref[...].reshape(-1, WIDE)
    chunk = 256
    backs = []
    q_cols, q_rows = jnp.concatenate([qh, qh, ql], axis=1), jnp.concatenate([qh, ql, qh], axis=0)
    for first in range(0, negs.shape[0], chunk):
        nh, nl = split(negs[first : first + chunk, :])
        s = dot(q_cols, jnp.concatenate([nh, nl, nh], axis=1), ((1,), (1,)))
        small = jnp.exp(-jnp.abs(s))
        loss = jnp.maximum(s, 0.0) + log_one_plus(small)
        for part in range(chunk // 128):
            total = total + loss[:, part * 128 : (part + 1) * 128]
        whole = 1.0 + small
        turn = pl.reciprocal(whole, approx=True)
        turn = turn * (2.0 - whole * turn)
        weight = jnp.where(s >= 0.0, turn, small * turn)
        gh, gl = split(weight)
        grad = grad + dot(
            jnp.concatenate([gh, gh, gl], axis=1), jnp.concatenate([nh, nl, nh], axis=0)
        )
        back = dot(jnp.concatenate([gh, gh, gl], axis=0), q_rows, ((0,), (0,)))
        backs.append(back * (1.0 / ENT_NEGS))
    sum_ref[...] = grad
    loss_ref[...] = total
    back = jnp.concatenate(backs, axis=0)
    tiles = [back[:, k * 128 : (k + 1) * 128] for k in range(4)]
    lane = iota(tiles[0].shape, 1)
    turned = pltpu.roll(tiles[3], 72, 1)
    tiles = tiles[0], tiles[2], jnp.where(lane < 72, tiles[1], turned), turned
    tiles = [tile.reshape(-1, 4, NEG, 128) for tile in tiles]
    rest = jnp.where(lane < 32, pltpu.roll(turned, 16, 1), 0.0).reshape(-1, 4, NEG, 128)
    low = iota((1, 8, 128), 2) < 16
    for k in range(4):
        at = (at_ref[0] + 4 - k) & 3
        for j in range(3):
            back_ref[at, :, j * NEG : (j + 1) * NEG, :] = tiles[j][:, k]
        back_ref[at, :, 3 * NEG :, :] = jnp.where(low, tiles[3][:, k, :8], rest[:, k, 8:])

    @pl.when(step == last)
    def _():
        for first, ref in ((0, grad_ref), (TRIP, gradother_ref)):
            loss = jnp.sum(loss_ref[first : first + TRIP, :], axis=1, keepdims=True)
            grad = sum_ref[first : first + TRIP, :]
            ref[...] = jnp.where(iota(grad.shape, 1) == AUX, loss, grad) * (1.0 / ENT_NEGS)


ENT_NEGS = 2 * CHIP_COUNT * NEG


def close_triples(core_ref, back_ref, place_ref, headv_ref, relv_ref, gradq_ref, gradmore_ref,
                  head_ref, rel_ref, gradh_ref, mine_ref, other_ref, out_ref):
    place = place_ref[...]
    lane = iota((TRIP, 128), 1)
    marks = jnp.concatenate(
        [hot(place == lane + part * 128) for part in range(SLOTS // 128)], axis=1
    )
    high, low = split(back_ref[...])
    tail = dot(marks, high) + dot(marks, low)
    positive = aux_column(tail)
    from_negs = gradq_ref[...] + gradmore_ref[...]
    neg_loss = aux_column(from_negs)
    drop = -positive
    loss = jnp.maximum(drop, 0.0) + jnp.log1p(jnp.exp(-jnp.abs(drop))) + neg_loss
    out_ref[...] = jnp.broadcast_to(loss, (TRIP, 128)).T[:1]
    grad = without_aux(tail + from_negs)
    g_re, g_im = grad[:, :SIDE], grad[:, SIDE:]
    heads, rels = headv_ref[...], relv_ref[...]
    h_re, h_im, r_re, r_im = heads[:, :SIDE], heads[:, SIDE:], rels[:, :SIDE], rels[:, SIDE:]
    gh = jnp.concatenate([g_re * r_re + g_im * r_im, g_im * r_re - g_re * r_im], axis=1)
    gr = jnp.concatenate([g_re * h_re + g_im * h_im, g_im * h_re - g_re * h_im], axis=1)
    gradh_ref[...] = gh

    core = core_ref[0]
    at = iota((2 * CHIP_COUNT * 8, TRIP), 0)
    head, rel = head_ref[...], rel_ref[...]
    hub_id = (at + core * (HUB // 2)) % HUB
    rel_id = (at // 8 * REL_OWN + at % REL_OWN + core * (REL // 2)) % REL
    sums = []
    for marks, value in ((hot(hub_id == head), gh), (hot(rel_id == rel), gr)):
        high, low = split(value)
        sums.append(dot(marks, high) + dot(marks, low))
    for k, tile in enumerate(pack(*sums)):
        tile = tile.reshape(2, CHIP_COUNT, 8, 128)
        mine_ref[:, k * 8 : (k + 1) * 8, :] = tile[0]
        other_ref[:, k * 8 : (k + 1) * 8, :] = tile[1]


def scatter_entities(head_ref, gradh_ref, asked_ref, answer_ref, out_ref,
                     th_ref, tl_ref, hh_ref, hl_ref, row_ref):
    @pl.when(pl.program_id(0) == 0)
    def _():
        asked = asked_ref[...]
        row_ref[...] = jnp.broadcast_to(aux_column(asked).astype(I32) - 1, (SLOTS, 128))
        slope = -jax.nn.sigmoid(-aux_column(answer_ref[...]))
        high, low = split((without_aux(asked) * slope).T)
        th_ref[...] = high
        tl_ref[...] = low
        high, low = split(gradh_ref[...].T)
        hh_ref[...] = high
        hl_ref[...] = low

    count = out_ref.shape[1]
    first = pl.program_id(0) * count
    rows = row_ref[...]
    lane = iota((SLOTS, 128), 1) + first
    marks = jnp.concatenate([hot(rows == lane + k * 128) for k in range(count // 128)], axis=1)
    grad = dot(th_ref[...], marks) + dot(tl_ref[...], marks)
    marks = hot(iota((count, TRIP), 0) + first == head_ref[...] - HUB)
    nt = ((1,), (1,))
    grad = grad + (dot(hh_ref[...], marks, nt) + dot(hl_ref[...], marks, nt))
    out_ref[:HALF, :] = grad[:HALF]
    out_ref[HALF:, :] = grad[SIDE : SIDE + HALF]


def update_own(sums_ref, mine_ref, out_ref):
    lane = iota((8, 128), 1)
    grads = [jnp.sum(sums_ref[:, k * 8 : (k + 1) * 8, :], axis=0) for k in range(5)]
    mine = [mine_ref[k * 8 : (k + 1) * 8, :] for k in range(5)]

    def across(x):
        return jnp.sum(x, axis=1, keepdims=True)

    in_hub, in_rel = lane < 16, (lane >= 16) & (lane < 88)
    squares = [g * g for g in grads]
    hub = across(squares[0] + squares[1] + squares[3] + jnp.where(in_hub, squares[4], 0.0))
    rel = jnp.broadcast_to(across(squares[2] + jnp.where(in_rel, squares[4], 0.0)), (8, 128))
    rel = rel + pltpu.roll(rel, REL_OWN, 0)
    hub_acc = across(jnp.where(lane == 89, mine[4], 0.0)) + hub / WIDTH
    rel_acc = across(jnp.where(lane == 88, mine[4], 0.0)) + rel / WIDTH
    hub_root, rel_root = jnp.sqrt(hub_acc), jnp.sqrt(rel_acc)
    mixed = jnp.where(in_hub, hub_root, rel_root)
    roots = (hub_root, hub_root, rel_root, hub_root, mixed)
    new = [m - LEARN_RATE * g / root for m, g, root in zip(mine, grads, roots)]
    new[4] = jnp.where(lane == 88, rel_acc, jnp.where(lane == 89, hub_acc, new[4]))
    for k in range(5):
        out_ref[:, k * 8 : (k + 1) * 8, :] = jnp.broadcast_to(new[k][None], (CHIP_COUNT, 8, 128))


def place_new(side_ref, part_ref, *refs):
    hub_ref, hubacc_ref, rel_ref, relacc_ref, held_ref = refs[-5:]

    def turned(k):
        return part_ref[:, k * 8 : (k + 1) * 8, :].reshape(CHIP_COUNT * 8, 128).T

    hub_ref[0:128, :] = turned(0)
    hub_ref[HALF : HALF + 128, :] = turned(1)
    mixed = turned(3)
    hub_ref[128:HALF, :] = mixed[:72]
    hub_ref[HALF + 128 : HALF + 184, :] = mixed[72:]
    last = turned(4)
    hub_ref[HALF + 184 : WIDTH, :] = last[:16]
    hubacc_ref[...] = last[89:90]
    for chip in range(CHIP_COUNT):
        here = slice(chip * REL_OWN, (chip + 1) * REL_OWN)
        held_ref[0, here, :] = part_ref[chip, 16:20, :]
        held_ref[1, here, :] = part_ref[chip, 32:36, :]
        held_ref[2, here, :] = part_ref[chip, 20:24, :]
        held_ref[3, here, :] = part_ref[chip, 36:40, :]
    for half in range(2):
        rel_ref[half * HALF : half * HALF + 128, :] = held_ref[2 * half].T
        last = held_ref[2 * half + 1].T
        rel_ref[half * HALF + 128 : (half + 1) * HALF, :] = last[16:88]
        if half == 0:
            relacc_ref[...] = last[88:89]


def update_entities(rows_ref, neg_ref, ent_ref, acc_ref, grad_ref, new_ref, newacc_ref,
                    high_ref, low_ref):
    @pl.when(pl.program_id(0) == 0)
    def _():
        total = jnp.sum(neg_ref[...], axis=0)
        first, second, mixed = [total[j * NEG : (j + 1) * NEG] for j in range(3)]
        rest = total[3 * NEG :]
        rest = jnp.concatenate([rest, pltpu.roll(rest, 112, 1)], axis=0)
        lane = iota(mixed.shape, 1)
        fourth = jnp.where(lane < 56, pltpu.roll(mixed, 56, 1), pltpu.roll(rest, 56, 1))
        parts = [first, jnp.where(lane < 72, mixed, 0.0), second, jnp.where(lane < 72, fourth, 0.0)]
        high, low = split(jnp.concatenate(parts, axis=1))
        high_ref[...] = high
        low_ref[...] = low

    count = ent_ref.shape[1]
    first = pl.program_id(0) * count
    rows = rows_ref[...][:, :1]
    marks = hot(iota((NEG, count), 1) + first == rows)
    tn = ((0,), (0,))
    more = dot(high_ref[...], marks, tn) + dot(low_ref[...], marks, tn)
    g_re = grad_ref[:HALF, :] + more[:HALF]
    g_im = grad_ref[HALF:, :] + more[SIDE : SIDE + HALF]
    square = jnp.sum(g_re * g_re, axis=0, keepdims=True) + jnp.sum(
        g_im * g_im, axis=0, keepdims=True
    )
    accum = acc_ref[...] + square / WIDTH
    newacc_ref[...] = accum
    root = jnp.sqrt(accum)
    new_ref[:HALF, :] = ent_ref[:HALF, :] - LEARN_RATE * g_re / root
    new_ref[HALF:, :] = ent_ref[HALF:, :] - LEARN_RATE * g_im / root


def around(block, axis):
    count = SIZES[SHARD.index(axis)]
    turns = [[(i, (i + k) % count) for i in range(count)] for k in range(1, count)]
    return [block] + [lax.ppermute(block, axis, turn) for turn in turns]


def shape(*dims, dtype=F32):
    return jax.ShapeDtypeStruct(dims, dtype)


def body(
    entity_table,
    entity_accum,
    hub_table,
    hub_accum,
    relation_table,
    relation_accum,
    head_ids,
    relation_ids,
    tail_owner,
    tail_rows,
    negative_rows,
):
    core = lax.axis_index("core").astype(I32)
    chip = lax.axis_index(CHIPS).astype(I32)
    core_arg = core.reshape(1)
    own_arg = (core * CHIP_COUNT + chip).reshape(1)
    ent_t, hub_t, rel_t = entity_table.T, hub_table.T, relation_table.T
    head_row, rel_row = head_ids.reshape(1, TRIP), relation_ids.reshape(1, TRIP)
    owner_row, tail_row = tail_owner.reshape(1, TRIP), tail_rows.reshape(1, TRIP)

    picked = pl.pallas_call(
        pick_negatives,
        out_shape=shape(NEG, WIDE),
        in_specs=[SMEM, VMEM],
        out_specs=VMEM,
        scratch_shapes=[pltpu.VMEM((WIDE, 128), F32)],
        compiler_params=params(),
        name="pick_negatives",
    )(negative_rows, ent_t)
    picked, head_row = lax.optimization_barrier((picked, head_row))
    near = jnp.concatenate(around(picked, "z"), axis=0)

    sent, place = pl.pallas_call(
        prepare,
        out_shape=[shape(SLOTS, WIDE), shape(TRIP, 128, dtype=I32)],
        in_specs=[VMEM] * 7,
        out_specs=[VMEM] * 2,
        compiler_params=params(),
        name="prepare",
    )(head_row, rel_row, owner_row, tail_row, ent_t, hub_t, rel_t)

    def exchange(rows):
        parts = rows.reshape(2 * CHIP_COUNT, CAP, WIDE)
        got = lax.all_to_all(parts, SHARD, split_axis=0, concat_axis=0, tiled=True)
        return got.reshape(SLOTS, WIDE)

    sent, near, own_arg, rel_row = lax.optimization_barrier((sent, near, own_arg, rel_row))
    query, heads, rels = pl.pallas_call(
        embed_rows,
        out_shape=[shape(TRIP, WIDE)] * 3,
        in_specs=[VMEM] * 5,
        out_specs=[VMEM] * 3,
        compiler_params=params(),
        cost_estimate=cost(1e6, 1e5),
        name="embed_rows",
    )(head_row, rel_row, ent_t, hub_t, rel_t)
    near = lax.all_gather(near, ("x", "y"), axis=0, tiled=True)
    query_other = lax.ppermute(query, "core", SWAP)
    asked = exchange(sent)
    ent_high, ent_low, mine_rows = pl.pallas_call(
        turn_tables,
        out_shape=[
            shape(ENT, WIDE, dtype=BF16), shape(ENT, WIDE, dtype=BF16), shape(OWN, 128)
        ],
        in_specs=[SMEM] + [VMEM] * 5,
        out_specs=[VMEM] * 3,
        scratch_shapes=[pltpu.VMEM((WIDE, 128), F32)],
        compiler_params=params(),
        cost_estimate=cost(1e6, 1e5),
        name="turn_tables",
    )(own_arg, ent_t, hub_t, rel_t, hub_accum.reshape(1, HUB), relation_accum.reshape(1, REL))

    rows = 256
    answer = pl.pallas_call(
        answer_queries,
        out_shape=shape(SLOTS, WIDE),
        grid=(SLOTS // rows,),
        in_specs=[pl.BlockSpec((rows, WIDE), lambda i: (i, 0)), VMEM, VMEM],
        out_specs=pl.BlockSpec((rows, WIDE), lambda i: (i, 0)),
        compiler_params=params(),
        name="answer_queries",
    )(asked, ent_high, ent_low)
    near, _ = lax.optimization_barrier((near, answer))
    back = exchange(answer)

    group, places = 8, 16
    whole = pl.BlockSpec((TRIP, WIDE), lambda i, at: (0, 0))
    part, grad_q, grad_other = pl.pallas_call(
        score,
        out_shape=[
            shape(4, places, NEG_PACKED, 128), shape(TRIP, WIDE), shape(TRIP, WIDE)
        ],
        grid_spec=pltpu.PrefetchScalarGridSpec(
            num_scalar_prefetch=1,
            grid=(places // group,),
            in_specs=[
                whole, whole, pl.BlockSpec((group, 4 * NEG, WIDE), lambda i, at: (i, 0, 0))
            ],
            out_specs=[
                pl.BlockSpec((4, group, NEG_PACKED, 128), lambda i, at: (0, i, 0, 0)),
                whole, whole
            ],
            scratch_shapes=[
                pltpu.VMEM((2 * TRIP, WIDE), BF16), pltpu.VMEM((2 * TRIP, WIDE), BF16),
                pltpu.VMEM((2 * TRIP, WIDE), F32), pltpu.VMEM((2 * TRIP, 128), F32),
            ],
        ),
        compiler_params=params(),
        cost_estimate=cost(20e9, 12e6),
        name="score",
    )(
        lax.axis_index("z").astype(I32).reshape(1),
        query,
        query_other,
        near.reshape(places, 4 * NEG, WIDE),
    )
    grad_other, back = lax.optimization_barrier((grad_other, back))
    grad_more = lax.ppermute(grad_other, "core", SWAP)
    part, back = lax.optimization_barrier((part.reshape(CHIP_COUNT, NEG_PACKED, 128), back))
    neg_sums = lax.all_to_all(part, CHIPS, split_axis=0, concat_axis=0, tiled=True)

    grad_head, both_mine, both_other, loss = pl.pallas_call(
        close_triples,
        out_shape=[
            shape(TRIP, WIDE), shape(CHIP_COUNT, OWN, 128), shape(CHIP_COUNT, OWN, 128),
            shape(1, TRIP),
        ],
        in_specs=[SMEM] + [VMEM] * 8,
        out_specs=[VMEM] * 4,
        compiler_params=params(),
        name="close_triples",
    )(core_arg, back, place, heads, rels, grad_q, grad_more, head_row, rel_row)
    both_swapped = lax.ppermute(both_other, "core", SWAP)

    paired = both_mine + both_swapped
    paired, neg_sums, asked, answer = lax.optimization_barrier((paired, neg_sums, asked, answer))
    sums = lax.all_to_all(paired, CHIPS, split_axis=0, concat_axis=0, tiled=True)

    columns = 256
    whole = pl.BlockSpec((SLOTS, WIDE), lambda i: (0, 0))
    entity_grad = pl.pallas_call(
        scatter_entities,
        out_shape=shape(WIDTH, ENT),
        grid=(ENT // columns,),
        in_specs=[
            pl.BlockSpec((1, TRIP), lambda i: (0, 0)),
            pl.BlockSpec((TRIP, WIDE), lambda i: (0, 0)),
            whole,
            whole,
        ],
        out_specs=pl.BlockSpec((WIDTH, columns), lambda i: (0, i)),
        scratch_shapes=[
            pltpu.VMEM((WIDE, SLOTS), BF16), pltpu.VMEM((WIDE, SLOTS), BF16),
            pltpu.VMEM((WIDE, TRIP), BF16), pltpu.VMEM((WIDE, TRIP), BF16),
            pltpu.VMEM((SLOTS, 128), I32),
        ],
        compiler_params=params(),
        cost_estimate=cost(1e6, 1e5),
        name="scatter_entities",
    )(head_row, grad_head, asked, answer)

    sums, entity_grad = lax.optimization_barrier((sums, entity_grad))
    own_new = pl.pallas_call(
        update_own,
        out_shape=shape(CHIP_COUNT, OWN, 128),
        in_specs=[VMEM] * 2,
        out_specs=VMEM,
        compiler_params=params(12),
        name="update_own",
    )(sums, mine_rows)
    new_mine = lax.all_to_all(own_new, CHIPS, split_axis=0, concat_axis=0, tiled=True)
    columns = 512
    entity_new, entity_accum_new = pl.pallas_call(
        update_entities,
        out_shape=[shape(WIDTH, ENT), shape(1, ENT)],
        grid=(ENT // columns,),
        in_specs=[
            pl.BlockSpec((NEG, 128), lambda i: (0, 0)),
            pl.BlockSpec((CHIP_COUNT, NEG_PACKED, 128), lambda i: (0, 0, 0)),
            pl.BlockSpec((WIDTH, columns), lambda i: (0, i)),
            pl.BlockSpec((1, columns), lambda i: (0, i)),
            pl.BlockSpec((WIDTH, columns), lambda i: (0, i)),
        ],
        out_specs=[
            pl.BlockSpec((WIDTH, columns), lambda i: (0, i)),
            pl.BlockSpec((1, columns), lambda i: (0, i)),
        ],
        scratch_shapes=[pltpu.VMEM((NEG, WIDE), BF16), pltpu.VMEM((NEG, WIDE), BF16)],
        compiler_params=params(),
        cost_estimate=cost(1e6, 1e5),
        name="update_entities",
    )(
        jnp.broadcast_to(negative_rows[:, None], (NEG, 128)),
        neg_sums,
        ent_t,
        entity_accum.reshape(1, ENT),
        entity_grad,
    )

    new_mine, entity_new = lax.optimization_barrier((new_mine, entity_new))
    new_other = lax.ppermute(new_mine, "core", SWAP)

    def placed(side, part, *before):
        sizes = ((WIDTH, HUB), (1, HUB), (WIDTH, REL), (1, REL))
        return pl.pallas_call(
            place_new,
            out_shape=[shape(*size) for size in sizes],
            grid_spec=pltpu.PrefetchScalarGridSpec(
                num_scalar_prefetch=1,
                grid=(1,),
                in_specs=[pl.BlockSpec((CHIP_COUNT, OWN, 128), lambda i, side: (0, 0, 0))]
                + [pl.BlockSpec(memory_space=pl.ANY)] * len(before),
                out_specs=[
                    pl.BlockSpec((rows, count // 2), lambda i, side: (0, side[0]))
                    for rows, count in sizes
                ],
                scratch_shapes=[pltpu.VMEM((4, REL // 2, 128), F32)],
            ),
            input_output_aliases={k + 2: k for k in range(len(before))},
            compiler_params=params(16),
            name="place_new",
        )(side, part, *before)

    halves = placed(core_arg, new_mine)
    hub_new, hub_accum_new, rel_new, rel_accum_new = placed(1 - core_arg, new_other, *halves)
    return (
        entity_new.T,
        entity_accum_new.reshape(ENT),
        hub_new.T,
        hub_accum_new.reshape(HUB),
        rel_new.T,
        rel_accum_new.reshape(REL),
        loss.reshape(TRIP),
    )


def solution(mesh):
    fine = Mesh(mesh.devices.reshape(SIZES), SHARD)
    rows, vector = P(SHARD, None), P(SHARD)
    placed = (rows, vector, P(), P(), P(), P(), vector, vector, rows, vector, vector)
    return jax.shard_map(
        body,
        mesh=fine,
        in_specs=placed,
        out_specs=(rows, vector, P(), P(), P(), P(), vector),
        check_vma=False,
    )
```
